32 devices in a mesh: dp: 8 (over z, y), mp: 4 (over x, core).
Axes of the slice: x: 2, y: 2, z: 4, core: 2. Of those that a mesh axis runs over, the one named last changes fastest.
Arguments:
- block_input: float32 [25088, 768], P(('dp', 'mp')), may hold values from -6 to 6
- cotangent: float32 [25088, 768], P(('dp', 'mp')), may hold values from -6 to 6
- image_size: int32 [128, 2], P('dp'), may hold values from 7 to 14, as said below
- attention_weights: float32 [4, 768, 768], P(None, 'dp', 'mp')
- attention_first: float32 [4, 768, 768], P(None, 'dp', 'mp'), may hold values from -112 to 112
- attention_second: float32 [4, 768, 768], P(None, 'dp', 'mp'), may hold values from 12.544 to 200.704
- mlp_weights: float32 [2, 768, 3072], P(None, 'dp', 'mp')
- mlp_first: float32 [2, 768, 3072], P(None, 'dp', 'mp'), may hold values from -112 to 112
- mlp_second: float32 [2, 768, 3072], P(None, 'dp', 'mp'), may hold values from 12.544 to 200.704
- head_params: float32 [12, 857], P('mp')
- head_first: float32 [12, 857], P('mp'), may hold values from -112 to 112
- head_second: float32 [12, 857], P('mp'), may hold values from 12.544 to 200.704
- norm_params: float32 [12, 768], replicated, as said below
- norm_first: float32 [12, 768], replicated, may hold values from -112 to 112
- norm_second: float32 [12, 768], replicated, may hold values from 12.544 to 200.704
Outputs:
- block_output: float32 [25088, 768], P(('dp', 'mp'))
- input_grad: float32 [25088, 768], P(('dp', 'mp'))
- attention_grad: float32 [4, 768, 768], P(None, 'dp', 'mp')
- attention_second_new: float32 [4, 768, 768], P(None, 'dp', 'mp')
- attention_new: float32 [4, 768, 768], P(None, 'dp', 'mp')
- mlp_grad: float32 [2, 768, 3072], P(None, 'dp', 'mp')
- mlp_second_new: float32 [2, 768, 3072], P(None, 'dp', 'mp')
- mlp_new: float32 [2, 768, 3072], P(None, 'dp', 'mp')
- head_grad: float32 [12, 857], P('mp')
- head_second_new: float32 [12, 857], P('mp')
- head_new: float32 [12, 857], P('mp')
- norm_grad: float32 [12, 768], replicated
- norm_second_new: float32 [12, 768], replicated
- norm_new: float32 [12, 768], replicated
The draws below stay inside these ranges and needn't reach their ends.
Inputs may be any that keep to these rules, and one draw needn't show every extreme that they name: `image_size`: column 0 holds heights, column 1 widths, in patches of a 14 x 14 grid; the first image fills the grid and the second is the smallest. `norm_params`: rows 0, 2, 5 and 7 are positive.
All inputs are finite; a program needn't handle non-finite values.
Results may differ from the reference program's by a relative error of at most 0.017.
Values may be sent and summed in bfloat16 or wider, within the bound.
No kernel may reach another device: no remote copies, remote signals or barrier semaphores. Data moves between devices by JAX's collectives and lax.ppermute only.
A program may use at most 256 MiB of HBM per device.

```python
import math
import jax
import jax.numpy as jnp
from jax import lax

D = 768
H = 12
HD = 64
FF = 3072
GRID = 14
STEP = 10
IMG_DEV = 16
PATCHES = 196
NREL = 729
IMAGES = 128
TOKENS = 25088
N_DP = 8


def draw_image_size(key, part):
    key = jax.random.fold_in(key, 11)
    extents = jax.random.randint(key, (IMAGES, 2), GRID // 2, GRID + 1, dtype=jnp.int32)
    extents = extents.at[0].set(GRID)
    return extents.at[1].set(GRID // 2)


def draw_attention_weights(key, part):
    key = jax.random.fold_in(key, 23)
    values = jax.random.normal(key, (4, D, D), dtype=jnp.float32)
    factor = jnp.array([1.0, 1.0, 1.0, 6.0], jnp.float32) * D ** (-0.5)
    return values * factor[:, None, None]


def draw_mlp_weights(key, part):
    key = jax.random.fold_in(key, 31)
    values = jax.random.normal(key, (2, D, FF), dtype=jnp.float32)
    factor = jnp.array([D ** (-0.5), 1.5 * FF ** (-0.5)], jnp.float32)
    return values * factor[:, None, None]


def draw_head_params(key, part):
    key = jax.random.fold_in(key, 29)
    values = jax.random.normal(key, (H, 2 * HD + NREL), dtype=jnp.float32)
    column = jnp.arange(2 * HD + NREL)[None, :]
    return jnp.where(column < 2 * HD, 0.1 * values, 0.6 * values)


def draw_norm_params(key, part):
    key = jax.random.fold_in(key, 37)
    values = jax.random.normal(key, (12, D), dtype=jnp.float32)
    row_index = jnp.arange(12)[:, None]
    positive = (row_index == 0) | (row_index == 2) | (row_index == 5) | (row_index == 7)
    return jnp.where(positive, jnp.exp(0.3 * values), 0.1 * values)


def block_levels(own_key, dims, split, smallest, high):
    loudness = 1.0
    for dim, shards_of in split:
        draws = jax.random.uniform(jax.random.fold_in(jax.random.fold_in(own_key, 6), dim), (shards_of,), jnp.float32, smallest / len(split), high / len(split))
        loudness = loudness * jnp.repeat(jnp.exp(draws), dims[dim] // shards_of).reshape((-1,) + (1,) * (len(dims) - 1 - dim))
    return loudness


def gaussian(own_key, dims, spread, reach, shards=(), held_as=jnp.bfloat16):
    factor_of = block_levels(own_key, dims, shards, -0.22, 0.18) if shards else 1.0
    values = jax.random.normal(own_key, dims, jnp.float32) * spread * factor_of
    return jnp.minimum(jnp.maximum(values, -reach), reach).astype(held_as)


def setup_inputs(seed: int = 0) -> dict:
    splits = jax.random.split(jax.random.key(seed), 16)
    return {
        "block_input": gaussian(splits[0], (TOKENS, D), 1.0, 6.0, ((0, 32),), jnp.float32),
        "cotangent": gaussian(splits[1], (TOKENS, D), 1.0, 6.0, ((0, 32),), jnp.float32),
        "image_size": draw_image_size(jax.random.fold_in(splits[15], 71), 0),
        "attention_weights": draw_attention_weights(jax.random.fold_in(splits[15], 71), 0),
        "attention_first": gaussian(splits[4], (4, D, D), (0.11 * TOKENS ** 0.5), 112.0, ((1, 8), (2, 4)), jnp.float32),
        "attention_second": jnp.clip(jnp.exp(math.log(200.704) - 2.7725887 * jax.random.uniform(splits[5], (4, D, D), jnp.float32) ** block_levels(splits[5], (4, D, D), ((1, 8), (2, 4)), -0.2, 0.2)), 12.544, 200.704),
        "mlp_weights": draw_mlp_weights(jax.random.fold_in(splits[15], 71), 0),
        "mlp_first": gaussian(splits[7], (2, D, FF), (0.11 * TOKENS ** 0.5), 112.0, ((1, 8), (2, 4)), jnp.float32),
        "mlp_second": jnp.clip(jnp.exp(math.log(200.704) - 2.7725887 * jax.random.uniform(splits[8], (2, D, FF), jnp.float32) ** block_levels(splits[8], (2, D, FF), ((1, 8), (2, 4)), -0.2, 0.2)), 12.544, 200.704),
        "head_params": draw_head_params(jax.random.fold_in(splits[15], 71), 0),
        "head_first": gaussian(splits[10], (H, 2 * HD + NREL), (0.11 * TOKENS ** 0.5), 112.0, ((0, 4),), jnp.float32),
        "head_second": jnp.clip(jnp.exp(math.log(200.704) - 2.7725887 * jax.random.uniform(splits[11], (H, 2 * HD + NREL), jnp.float32) ** block_levels(splits[11], (H, 2 * HD + NREL), ((0, 4),), -0.2, 0.2)), 12.544, 200.704),
        "norm_params": draw_norm_params(jax.random.fold_in(splits[15], 71), 0),
        "norm_first": gaussian(splits[13], (12, D), (0.11 * TOKENS ** 0.5), 112.0, (), jnp.float32),
        "norm_second": jnp.clip(jnp.exp(jax.random.uniform(splits[14], (12, D), jnp.float32, math.log(12.544), math.log(200.704))), 12.544, 200.704),
    }


EPSILON = 1e-06
NEGATIVE = -1e+30
BETA_ONE = 0.9
BETA_TWO = 0.999
ADAM_EPSILON = 1e-08
RATE_MATRIX = 0.05
RATE_VECTOR = 0.4
DECAY_MATRIX = 0.05
HIGHEST = lax.Precision.HIGHEST

@jax.custom_vjp
def low(v):
    return lax.optimization_barrier(v.astype(jnp.bfloat16)).astype(jnp.float32)

@jax.custom_vjp
def low_back(v):
    return v

def low_keep(v):
    return (low(v), None)

def low_pass(kept, grad):
    return (grad,)

def back_keep(v):
    return (v, None)

def back_low(kept, grad):
    return (low(grad),)
low.defvjp(low_keep, low_pass)
low_back.defvjp(back_keep, back_low)

def layer_norm(values, norm_gain, norm_shift):
    row_mean = lax.optimization_barrier(jnp.mean(values, axis=-1, keepdims=True))
    centre = values - row_mean
    variance = lax.optimization_barrier(jnp.mean(centre * centre, axis=-1, keepdims=True))
    return centre * lax.rsqrt(variance + EPSILON) * norm_gain + norm_shift

def product(former, latter):
    return jnp.dot(former, latter, precision=HIGHEST)

def block(block_rows, valid_keys, attention, mlp, head_table, vectors, pair_bias):
    images = valid_keys.shape[0]
    shape_four = (images, PATCHES, H, HD)
    normed = low(layer_norm(block_rows, vectors[0], vectors[1]))
    query_bias = head_table[:, :HD].reshape(D)
    value_bias = head_table[:, HD:2 * HD].reshape(D)
    queries = low(low_back(product(normed, attention[0]) + query_bias) * HD ** (-0.5))
    key_rows = low(low_back(product(normed, attention[1])))
    values = low(low_back(product(normed, attention[2]) + value_bias))
    scores = jnp.einsum('iqhd,ikhd->ihqk', queries.reshape(shape_four), key_rows.reshape(shape_four), precision=HIGHEST)
    scores = low_back(scores + pair_bias[None])
    scores = jnp.where(valid_keys[:, None, None, :], scores, NEGATIVE)
    row_max = lax.optimization_barrier(jnp.max(scores, axis=-1, keepdims=True))
    exponent = jnp.exp(scores - row_max)
    softmax = low(exponent / lax.optimization_barrier(jnp.sum(exponent, axis=-1, keepdims=True)))
    context = jnp.einsum('ihqk,ikhd->iqhd', softmax, values.reshape(shape_four), precision=HIGHEST)
    context = low(low_back(context.reshape(images * PATCHES, D)))
    attended = low_back(product(context, attention[3].T)) + vectors[4]
    middle = block_rows + vectors[5] * attended
    normed_two = low(layer_norm(middle, vectors[2], vectors[3]))
    hidden = low_back(product(normed_two, mlp[0]) + vectors[8:].reshape(FF))
    active = low(jax.nn.gelu(hidden, approximate=False))
    down_out = low_back(product(active, mlp[1].T)) + vectors[6]
    return middle + vectors[7] * down_out

def adam(weight, moment_one, moment_two, incoming, step_rate, decay_rate):
    first_new = BETA_ONE * moment_one + (1.0 - BETA_ONE) * incoming
    second_new = BETA_TWO * moment_two + (1.0 - BETA_TWO) * incoming * incoming
    update = first_new / (1.0 - BETA_ONE ** STEP) / (jnp.sqrt(second_new / (1.0 - BETA_TWO ** STEP)) + ADAM_EPSILON)
    return (second_new, weight * (1.0 - step_rate * decay_rate) - step_rate * update)

def reference(block_input, cotangent, image_size, attention_weights, attention_first, attention_second, mlp_weights, mlp_first, mlp_second, head_params, head_first, head_second, norm_params, norm_first, norm_second):
    position = jnp.arange(PATCHES, dtype=jnp.int32)
    patch_row = position // GRID
    patch_col = position % GRID
    valid_keys = (patch_row[None, :] < image_size[:, 0:1]) & (patch_col[None, :] < image_size[:, 1:2])
    valid_keys = valid_keys.reshape(N_DP, IMG_DEV, PATCHES)
    offset = (patch_row[:, None] - patch_row[None, :] + GRID - 1) * (2 * GRID - 1) + (patch_col[:, None] - patch_col[None, :] + GRID - 1)
    grouped = block_input.reshape(N_DP, IMG_DEV * PATCHES, D)

    def forward(group_rows, attention, mlp, head_table, vectors):
        attention_low = low(attention)
        mlp_low = low(mlp)
        pair_bias = head_table[:, 2 * HD:][:, offset]
        group_step = jax.checkpoint(lambda group_item: block(group_item[0], group_item[1], attention_low, mlp_low, head_table, vectors, pair_bias))
        return lax.map(group_step, (group_rows, valid_keys))
    output, pullback = jax.vjp(forward, grouped, attention_weights, mlp_weights, head_params, norm_params)
    grad_rows, grad_attention, grad_mlp, grad_heads, grad_norms = pullback(cotangent.reshape(output.shape))
    attention_second_new, attention_new = adam(attention_weights, attention_first, attention_second, grad_attention, RATE_MATRIX, DECAY_MATRIX)
    mlp_second_new, mlp_new = adam(mlp_weights, mlp_first, mlp_second, grad_mlp, RATE_MATRIX, DECAY_MATRIX)
    head_second_new, head_new = adam(head_params, head_first, head_second, grad_heads, RATE_VECTOR, 0.0)
    norm_second_new, norm_new = adam(norm_params, norm_first, norm_second, grad_norms, RATE_VECTOR, 0.0)
    return (output.reshape(TOKENS, D), grad_rows.reshape(TOKENS, D), grad_attention, attention_second_new, attention_new, grad_mlp, mlp_second_new, mlp_new, grad_heads, head_second_new, head_new, grad_norms, norm_second_new, norm_new)
```

```python
import functools

import jax
import jax.numpy as jnp
from jax import lax
from jax.experimental import pallas as pl
from jax.experimental.pallas import tpu as pltpu
from jax.sharding import PartitionSpec as P

HD = 64
GRID = 14
SPAN = 2 * GRID - 1
STEP = 10
PATCHES = 196
PADDED = 208
PACK = 640
OUT_PACK = 256
CHUNKS = 8
LANES = 4
HEADS_LANE = 3

EPSILON = 1e-06
NEGATIVE = -1e30
BETA_ONE = 0.9
BETA_TWO = 0.999
ADAM_EPSILON = 1e-08
RATE_MATRIX = 0.05
RATE_VECTOR = 0.4
DECAY_MATRIX = 0.05

LOW = jnp.bfloat16
FULL = jnp.float32
INV_SQRT2 = 0.7071067811865476
INV_SQRT2PI = 0.3989422804014327
VMEM_LIMIT = 60 << 20


def dot(former, latter, former_dim=1, latter_dim=0):
    return lax.dot_general(
        former,
        latter,
        (((former_dim,), (latter_dim,)), ((), ())),
        preferred_element_type=FULL,
    )


def normalise(values):
    row_mean = jnp.mean(values, axis=-1, keepdims=True)
    centre = values - row_mean
    variance = jnp.mean(centre * centre, axis=-1, keepdims=True)
    inverse = lax.rsqrt(variance + EPSILON)
    return centre * inverse, inverse


def norm_back(incoming, norm_gain, scaled, inverse):
    weighted = incoming * norm_gain
    centred = weighted - jnp.mean(weighted, axis=-1, keepdims=True)
    return inverse * (centred - scaled * jnp.mean(weighted * scaled, axis=-1, keepdims=True))


def fold(values):
    rows, cols = values.shape
    return jnp.sum(values.reshape(rows // 8, 8, cols), axis=0)


def reversed_bits(index):
    return (index & 1) * 4 + (index & 2) + (index & 4) // 4


def whole(shape):
    zeros = (0,) * len(shape)
    return pl.BlockSpec(tuple(shape), lambda *_: zeros)


def params():
    return pltpu.CompilerParams(vmem_limit_bytes=VMEM_LIMIT)


def cost(flops, moved):
    return pl.CostEstimate(flops=int(flops), bytes_accessed=int(moved), transcendentals=0)


def place_rows(target, source, mine, at=None):
    rows = source.shape[1]
    for chunk in range(CHUNKS):
        value = source[reversed_bits(chunk) ^ mine]
        if at is None:
            target[chunk * rows : (chunk + 1) * rows, :] = value
        else:
            target[at, chunk * rows : (chunk + 1) * rows, :] = value


def load_image(pad, source, step):
    for image in range(source.shape[0] // PATCHES):

        @pl.when(step == image)
        def _(image=image):
            pad[0:PATCHES, :] = source[image * PATCHES : (image + 1) * PATCHES, :]

    return pad[...]


def store_image(target, pad, value, step):
    pad[...] = value
    for image in range(target.shape[0] // PATCHES):

        @pl.when(step == image)
        def _(image=image):
            target[image * PATCHES : (image + 1) * PATCHES, :] = pad[0:PATCHES, :]


def prepare_body(images, x_ref, vec_ref, spread_ref, normed_ref, bias_ref, pad_s):
    pad_s[...] = jnp.zeros_like(pad_s)
    for image in range(images):
        scaled, _ = normalise(x_ref[image * PATCHES : (image + 1) * PATCHES, :])
        pad_s[0:PATCHES, :] = scaled * vec_ref[0:1, :] + vec_ref[1:2, :]
        normed_ref[image * PADDED : (image + 1) * PADDED, :] = pad_s[...].astype(LOW)

    def head(index, carry):
        bias_ref[index] = jnp.zeros(bias_ref.shape[1:], FULL)
        for row in range(GRID):
            start = GRID * (GRID - 1 - row)
            bias_ref[index, row * GRID : (row + 1) * GRID, 0:PATCHES] = spread_ref[
                index, :, start : start + PATCHES
            ]
        return carry

    lax.fori_loop(0, bias_ref.shape[0], head, 0)


def prepare(x, vectors, spread, images):
    rows, width = x.shape
    heads = spread.shape[0]
    return pl.pallas_call(
        functools.partial(prepare_body, images),
        out_shape=[
            jax.ShapeDtypeStruct((images * PADDED, width), LOW),
            jax.ShapeDtypeStruct((heads, PADDED, PADDED), FULL),
        ],
        scratch_shapes=[pltpu.VMEM((PADDED, width), FULL)],
        compiler_params=params(),
        cost_estimate=cost(1e6, 8e6),
    )(x, vectors, spread)


Q_TILE = (0, 0, 1)
K_TILE = (3, 3, 4)
V_TILE = (2, 2, 1)
QK_ODD = (False, True, False)
V_ODD = (False, True, True)


def halves():
    lane = lax.broadcasted_iota(jnp.int32, (PADDED, 128), 1)
    return lane


def half_of(value, lane, odd):
    keep = lane >= HD if odd else lane < HD
    return jnp.where(keep, value, jnp.zeros_like(value))


def attend_body(
    me_ref, n_ref, bias_ref, add_ref, scale_ref, mask_ref, w0, w1, w2, w3, qkv_ref, prob_ref, ctx_ref, full_ref
):
    mine = me_ref[0]

    @pl.when(pl.program_id(0) == 0)
    def _():
        for group, piece in enumerate((w0, w1, w2, w3)):
            place_rows(full_ref, piece, mine, group)

    lane = halves()
    mask = mask_ref[0]
    zero = jnp.zeros_like(mask)
    one = jnp.ones_like(mask)
    for group in range(LANES):
        acc = dot(n_ref[...], full_ref[group])
        qkv = ((acc + add_ref[group]) * scale_ref[...]).astype(LOW)
        qkv_ref[group] = qkv
        tiles = [qkv[:, 128 * t : 128 * (t + 1)] for t in range(5)]
        outs = []
        for head in range(HEADS_LANE):
            odd = QK_ODD[head]
            mark = 0 if odd else HD
            keep = lane >= HD if odd else lane < HD
            key = jnp.where(keep, tiles[K_TILE[head]], jnp.where(lane == mark, mask, zero))
            query = jnp.where(lane == mark, one, tiles[Q_TILE[head]])
            scores = dot(key, query, 1, 1) + bias_ref[group * HEADS_LANE + head]
            top = jnp.max(scores, axis=0, keepdims=True)
            exponent = jnp.exp(scores - top)
            total = jnp.sum(exponent, axis=0, keepdims=True)
            prob = (exponent * (1.0 / total)).astype(LOW)
            prob_ref[0, group * HEADS_LANE + head] = prob
            value = half_of(tiles[V_TILE[head]], lane, V_ODD[head])
            outs.append(dot(prob, value, 0, 0))
        ctx_ref[:, group * OUT_PACK : group * OUT_PACK + 128] = (outs[0] + outs[1]).astype(LOW)
        ctx_ref[:, group * OUT_PACK + 128 : (group + 1) * OUT_PACK] = outs[2].astype(LOW)


def attend(mine, normed, bias, add, scale, mask, pieces, images):
    rows, width = normed.shape
    heads = bias.shape[0]
    return pl.pallas_call(
        attend_body,
        grid=(images,),
        in_specs=[
            pl.BlockSpec(memory_space=pltpu.SMEM),
            pl.BlockSpec((PADDED, width), lambda i: (i, 0)),
            whole(bias.shape),
            whole(add.shape),
            whole(scale.shape),
            pl.BlockSpec((1, PADDED, 128), lambda i: (i, 0, 0)),
        ]
        + [whole(piece.shape) for piece in pieces],
        out_specs=[
            pl.BlockSpec((LANES, PADDED, PACK), lambda i: (0, i, 0)),
            pl.BlockSpec((1, heads, PADDED, PADDED), lambda i: (i, 0, 0, 0)),
            pl.BlockSpec((PADDED, LANES * OUT_PACK), lambda i: (i, 0)),
            whole((LANES, width, PACK)),
        ],
        out_shape=[
            jax.ShapeDtypeStruct((LANES, rows, PACK), LOW),
            jax.ShapeDtypeStruct((images, heads, PADDED, PADDED), LOW),
            jax.ShapeDtypeStruct((rows, LANES * OUT_PACK), LOW),
            jax.ShapeDtypeStruct((LANES, width, PACK), LOW),
        ],
        compiler_params=params(),
        cost_estimate=cost(8e9, 2e7),
    )(mine, normed, bias, add, scale, mask, *pieces)


def middle_body(
    me_ref, ctx_ref, x_ref, cot_ref, vec_ref, w0, w1, w2, w3, att_ref, mid_ref, n_ref, gd_ref, cs_ref, full_ref, pad_s
):
    mine = me_ref[0]
    step = pl.program_id(0)

    @pl.when(step == 0)
    def _():
        for group, piece in enumerate((w0, w1, w2, w3)):
            place_rows(full_ref, piece, mine, group)
        pad_s[...] = jnp.zeros_like(pad_s)
        cs_ref[...] = jnp.zeros_like(cs_ref)

    total = vec_ref[4:5, :]
    for group in range(LANES):
        total = total + dot(
            ctx_ref[:, group * OUT_PACK : (group + 1) * OUT_PACK], full_ref[group], 1, 1
        )
    att_ref[...] = total
    mid = load_image(pad_s, x_ref, step) + vec_ref[5:6, :] * total
    mid_ref[...] = mid
    scaled, _ = normalise(mid)
    n_ref[...] = (scaled * vec_ref[2:3, :] + vec_ref[3:4, :]).astype(LOW)
    cot = load_image(pad_s, cot_ref, step)
    gd_ref[...] = (cot * vec_ref[7:8, :]).astype(LOW)
    cs_ref[...] += fold(cot)


def middle(mine, ctx, x, cot, vectors, pieces, images):
    rows = images * PADDED
    width = x.shape[1]
    block = lambda: pl.BlockSpec((PADDED, width), lambda i: (i, 0))
    return pl.pallas_call(
        middle_body,
        grid=(images,),
        in_specs=[
            pl.BlockSpec(memory_space=pltpu.SMEM),
            pl.BlockSpec((PADDED, LANES * OUT_PACK), lambda i: (i, 0)),
            whole(x.shape),
            whole(cot.shape),
            whole(vectors.shape),
        ]
        + [whole(piece.shape) for piece in pieces],
        out_specs=[block(), block(), block(), block(), whole((8, width)), whole((LANES, width, OUT_PACK))],
        out_shape=[
            jax.ShapeDtypeStruct((rows, width), FULL),
            jax.ShapeDtypeStruct((rows, width), FULL),
            jax.ShapeDtypeStruct((rows, width), LOW),
            jax.ShapeDtypeStruct((rows, width), LOW),
            jax.ShapeDtypeStruct((8, width), FULL),
            jax.ShapeDtypeStruct((LANES, width, OUT_PACK), LOW),
        ],
        scratch_shapes=[pltpu.VMEM((PADDED, width), FULL)],
        compiler_params=params(),
        cost_estimate=cost(1.3e9, 1.5e7),
    )(mine, ctx, x, cot, vectors, *pieces)


def gelu_pair(values):
    density = jnp.exp(values * values * -0.5) * INV_SQRT2PI
    below = 0.5 * lax.erf(values * INV_SQRT2) + 0.5
    return values * below, below + values * density


def feed_body(steps, blocks, me_ref, n_ref, gd_ref, ub_ref, *refs):
    up = refs[:LANES]
    down = refs[LANES : 2 * LANES]
    out_ref, gn_ref, keep1, send1, keep2, send2, gub_ref, nt_s, gdt_s, up_s, down_s, act_s, gh_s = refs[
        2 * LANES :
    ]
    step = pl.program_id(0)
    mine = me_ref[0]
    rows = n_ref.shape[0]
    per = rows // blocks
    chunk_rows = up[0].shape[1]

    @pl.when(step == 0)
    def _():
        nt_s[...] = n_ref[...].T
        gdt_s[...] = gd_ref[...].T
        out_ref[...] = jnp.zeros_like(out_ref)
        gn_ref[...] = jnp.zeros_like(gn_ref)

    for piece in range(LANES):

        @pl.when(step // steps == piece)
        def _(piece=piece):
            place_rows(up_s, up[piece], mine)
            place_rows(down_s, down[piece], mine)

    up_weight = up_s[...]
    down_weight = down_s[...]
    unit_sums = jnp.zeros((8, up_weight.shape[1]), FULL)
    for block in range(blocks):
        part = slice(block * per, (block + 1) * per)
        hidden = dot(n_ref[part, :], up_weight) + ub_ref[0]
        active, slope = gelu_pair(hidden)
        active = active.astype(LOW)
        act_s[part, :] = active
        grad = (dot(gd_ref[part, :], down_weight) * slope).astype(LOW)
        gh_s[part, :] = grad
        unit_sums = unit_sums + fold(grad.astype(FULL))
        out_ref[part, :] += dot(active, down_weight, 1, 1)
        gn_ref[part, :] += dot(grad, up_weight, 1, 1)
    gub_ref[0] = unit_sums
    grad_up = dot(nt_s[...], gh_s[...]).astype(LOW)
    grad_down = dot(gdt_s[...], act_s[...]).astype(LOW)
    for piece in range(LANES):

        @pl.when(step // steps == piece)
        def _(piece=piece):
            one, two = (keep1, keep2) if piece % 2 == 0 else (send1, send2)
            for chunk in range(CHUNKS):
                slot = reversed_bits(chunk) ^ mine
                one[0, slot] = grad_up[chunk * chunk_rows : (chunk + 1) * chunk_rows]
                two[0, slot] = grad_down[chunk * chunk_rows : (chunk + 1) * chunk_rows]


def feed(mine, normed, grad_down, unit_bias, up, down, images):
    rows, width = normed.shape
    _, chunk_rows, units = up[0].shape
    sub = units if images <= 4 else units // 2
    blocks = 2 if images <= 4 else 4
    steps = units // sub

    def piece_map(piece):
        return lambda j: (0, 0, jnp.clip(j - piece * steps, 0, steps - 1))

    def keep_map(j):
        slot = jnp.where(j >= 2 * steps, 1, 0)
        return (slot, 0, 0, jnp.clip(j - 2 * steps * slot, 0, steps - 1))

    def send_map(j):
        slot = jnp.where(j >= 3 * steps, 1, 0)
        return (slot, 0, 0, jnp.clip(j - steps - 2 * steps * slot, 0, steps - 1))

    grad_block = (1, CHUNKS, chunk_rows, sub)
    grads = jax.ShapeDtypeStruct((2, CHUNKS, chunk_rows, units), LOW)
    total = LANES * steps
    return pl.pallas_call(
        functools.partial(feed_body, steps, blocks),
        grid=(total,),
        in_specs=[
            pl.BlockSpec(memory_space=pltpu.SMEM),
            whole((rows, width)),
            whole((rows, width)),
            pl.BlockSpec((1, 1, sub), lambda j: (j, 0, 0)),
        ]
        + [pl.BlockSpec((CHUNKS, chunk_rows, sub), piece_map(p)) for p in range(LANES)] * 2,
        out_specs=[
            whole((rows, width)),
            whole((rows, width)),
            pl.BlockSpec(grad_block, keep_map),
            pl.BlockSpec(grad_block, send_map),
            pl.BlockSpec(grad_block, keep_map),
            pl.BlockSpec(grad_block, send_map),
            pl.BlockSpec((1, 8, sub), lambda j: (j, 0, 0)),
        ],
        out_shape=[jax.ShapeDtypeStruct((rows, width), FULL)] * 2
        + [grads] * 4
        + [jax.ShapeDtypeStruct((total, 8, sub), FULL)],
        scratch_shapes=[
            pltpu.VMEM((width, rows), LOW),
            pltpu.VMEM((width, rows), LOW),
            pltpu.VMEM((width, sub), LOW),
            pltpu.VMEM((width, sub), LOW),
            pltpu.VMEM((rows, sub), LOW),
            pltpu.VMEM((rows, sub), LOW),
        ],
        compiler_params=params(),
        cost_estimate=cost(12 * rows * width * units * LANES, 4e7),
    )(mine, normed, grad_down, unit_bias.reshape(total, 1, sub), *up, *down)


def back_body(
    me_ref,
    down_ref,
    gn_ref,
    mid_ref,
    att_ref,
    ctx_ref,
    cot_ref,
    vec_ref,
    wo_ref,
    qkv_ref,
    prob_ref,
    out_ref,
    gm_ref,
    dqkv_ref,
    keep_ref,
    send_ref,
    spread_ref,
    sums_ref,
    cols_ref,
    pad_s,
    out_s,
    ga_s,
    pair_s,
):
    mine = me_ref[0]
    step = pl.program_id(0)
    heads = pair_s.shape[0]

    @pl.when(step == 0)
    def _():
        pad_s[...] = jnp.zeros_like(pad_s)
        pair_s[...] = jnp.zeros_like(pair_s)
        sums_ref[...] = jnp.zeros_like(sums_ref)
        cols_ref[...] = jnp.zeros_like(cols_ref)

    cot = load_image(pad_s, cot_ref, step)
    down = down_ref[...] + vec_ref[6:7, :]
    mid = mid_ref[...]
    store_image(out_ref, out_s, mid + vec_ref[7:8, :] * down, step)
    scaled, inverse = normalise(mid)
    grad_normed = gn_ref[...]
    grad_mid = cot + norm_back(grad_normed, vec_ref[2:3, :], scaled, inverse)
    gm_ref[...] = grad_mid
    sums_ref[0] += fold(grad_normed * scaled)
    sums_ref[1] += fold(grad_normed)
    sums_ref[2] += fold(grad_mid)
    sums_ref[3] += fold(grad_mid * att_ref[...])
    sums_ref[4] += fold(cot * down)
    grad_att = (grad_mid * vec_ref[5:6, :]).astype(LOW)
    ga_s[pl.ds(pl.multiple_of(step * PADDED, PADDED), PADDED), :] = grad_att

    lane = halves()
    for group in range(LANES):
        grad_ctx = dot(grad_att, wo_ref[group]).astype(LOW)
        qkv = qkv_ref[group]
        tiles = [qkv[:, 128 * t : 128 * (t + 1)] for t in range(5)]
        grads = []
        for head in range(HEADS_LANE):
            odd, value_odd = QK_ODD[head], V_ODD[head]
            query = half_of(tiles[Q_TILE[head]], lane, odd)
            key = half_of(tiles[K_TILE[head]], lane, odd)
            value = tiles[V_TILE[head]]
            half = 128 if head == 2 else 0
            upstream = half_of(grad_ctx[:, half : half + 128], lane, value_odd)
            prob = prob_ref[0, group * HEADS_LANE + head]
            grad_prob = dot(value, upstream, 1, 1)
            soft = prob.astype(FULL)
            weighted = soft * grad_prob
            inner = jnp.sum(weighted, axis=0, keepdims=True)
            grad_score = weighted - soft * inner
            pair_s[group * HEADS_LANE + head] += grad_score
            low_score = grad_score.astype(LOW)
            grads.append(
                (
                    dot(low_score, key, 0, 0) * HD**-0.5,
                    dot(low_score, query),
                    dot(prob, upstream),
                )
            )
        packed = (
            grads[0][0] + grads[1][0],
            grads[2][0] + grads[2][2],
            grads[0][2] + grads[1][2],
            grads[0][1] + grads[1][1],
            grads[2][1],
        )
        for tile, value in enumerate(packed):
            low_value = value.astype(LOW)
            dqkv_ref[group, :, 128 * tile : 128 * (tile + 1)] = low_value
            cols_ref[group, :, 128 * tile : 128 * (tile + 1)] += fold(low_value.astype(FULL))

    @pl.when(step == pl.num_programs(0) - 1)
    def _():
        grad_out = dot(ga_s[...], ctx_ref[...], 0, 0).astype(LOW)
        rows = keep_ref.shape[2]
        for group in range(LANES):
            target = (keep_ref, send_ref)[group % 2]
            for chunk in range(CHUNKS):
                target[group // 2, reversed_bits(chunk) ^ mine] = grad_out[
                    chunk * rows : (chunk + 1) * rows, group * OUT_PACK : (group + 1) * OUT_PACK
                ]
        spread_ref[...] = jnp.zeros_like(spread_ref)

        def head_sum(index, carry):
            for row in range(GRID):
                at = GRID * (GRID - 1 - row)
                spread_ref[index, :, at : at + PATCHES] += pair_s[
                    index, row * GRID : (row + 1) * GRID, 0:PATCHES
                ]
            return carry

        lax.fori_loop(0, heads, head_sum, 0)


def back(mine, down, grad_normed, mid, att, ctx, cot, vectors, wo, qkv, prob, images, chunk_rows):
    rows, width = mid.shape
    heads = prob.shape[1]
    block = lambda: pl.BlockSpec((PADDED, width), lambda i: (i, 0))
    grads = (2, CHUNKS, chunk_rows, OUT_PACK)
    return pl.pallas_call(
        back_body,
        grid=(images,),
        in_specs=[
            pl.BlockSpec(memory_space=pltpu.SMEM),
            block(),
            block(),
            block(),
            block(),
            whole(ctx.shape),
            whole(cot.shape),
            whole(vectors.shape),
            whole(wo.shape),
            pl.BlockSpec((LANES, PADDED, PACK), lambda i: (0, i, 0)),
            pl.BlockSpec((1, heads, PADDED, PADDED), lambda i: (i, 0, 0, 0)),
        ],
        out_specs=[
            whole(cot.shape),
            block(),
            pl.BlockSpec((LANES, PADDED, PACK), lambda i: (0, i, 0)),
            whole(grads),
            whole(grads),
            whole((heads, GRID, 384)),
            whole((5, 8, width)),
            whole((LANES, 8, PACK)),
        ],
        out_shape=[
            jax.ShapeDtypeStruct(cot.shape, FULL),
            jax.ShapeDtypeStruct((rows, width), FULL),
            jax.ShapeDtypeStruct((LANES, rows, PACK), LOW),
            jax.ShapeDtypeStruct(grads, LOW),
            jax.ShapeDtypeStruct(grads, LOW),
            jax.ShapeDtypeStruct((heads, GRID, 384), FULL),
            jax.ShapeDtypeStruct((5, 8, width), FULL),
            jax.ShapeDtypeStruct((LANES, 8, PACK), FULL),
        ],
        scratch_shapes=[
            pltpu.VMEM((PADDED, width), FULL),
            pltpu.VMEM((PADDED, width), FULL),
            pltpu.VMEM((rows, width), LOW),
            pltpu.VMEM((heads, PADDED, PADDED), FULL),
        ],
        compiler_params=params(),
        cost_estimate=cost(1.2e10, 4e7),
    )(mine, down, grad_normed, mid, att, ctx, cot, vectors, wo, qkv, prob)


def project_body(me_ref, n_ref, dqkv_ref, keep_ref, send_ref, nt_s):
    mine = me_ref[0]
    nt_s[...] = n_ref[...].T
    rows = keep_ref.shape[2]
    for group in range(LANES):
        grad = dot(nt_s[...], dqkv_ref[group]).astype(LOW)
        target = (keep_ref, send_ref)[group % 2]
        for chunk in range(CHUNKS):
            target[group // 2, reversed_bits(chunk) ^ mine] = grad[chunk * rows : (chunk + 1) * rows]


def project(mine, normed, dqkv, chunk_rows):
    rows, width = normed.shape
    grads = jax.ShapeDtypeStruct((2, CHUNKS, chunk_rows, PACK), LOW)
    return pl.pallas_call(
        project_body,
        in_specs=[pl.BlockSpec(memory_space=pltpu.SMEM)] + [pl.BlockSpec(memory_space=pltpu.VMEM)] * 2,
        out_shape=[grads, grads],
        scratch_shapes=[pltpu.VMEM((width, rows), LOW)],
        compiler_params=params(),
        cost_estimate=cost(2 * rows * width * PACK * LANES, 1e7),
    )(mine, normed, dqkv)


def input_body(dqkv_ref, full_ref, gm_ref, x_ref, vec_ref, out_ref, sums_ref, pad_s, out_s):
    step = pl.program_id(0)

    @pl.when(step == 0)
    def _():
        pad_s[...] = jnp.zeros_like(pad_s)
        sums_ref[...] = jnp.zeros_like(sums_ref)

    scaled, inverse = normalise(load_image(pad_s, x_ref, step))
    grad = dot(dqkv_ref[0], full_ref[0], 1, 1)
    for group in range(1, LANES):
        grad = grad + dot(dqkv_ref[group], full_ref[group], 1, 1)
    sums_ref[0] += fold(grad * scaled)
    sums_ref[1] += fold(grad)
    result = gm_ref[...] + norm_back(grad, vec_ref[0:1, :], scaled, inverse)
    store_image(out_ref, out_s, result, step)


def input_back(dqkv, full, grad_mid, x, vectors, images):
    width = x.shape[1]
    return pl.pallas_call(
        input_body,
        grid=(images,),
        in_specs=[
            pl.BlockSpec((LANES, PADDED, PACK), lambda i: (0, i, 0)),
            whole(full.shape),
            pl.BlockSpec((PADDED, width), lambda i: (i, 0)),
            whole(x.shape),
            whole(vectors.shape),
        ],
        out_specs=[whole(x.shape), whole((2, 8, width))],
        out_shape=[jax.ShapeDtypeStruct(x.shape, FULL), jax.ShapeDtypeStruct((2, 8, width), FULL)],
        scratch_shapes=[pltpu.VMEM((PADDED, width), FULL)] * 2,
        compiler_params=params(),
        cost_estimate=cost(4e9, 1.5e7),
    )(dqkv, full, grad_mid, x, vectors)


def swap(values, axis, bit):
    count = lax.axis_size(axis)
    return lax.ppermute(values, axis, [(index, index ^ bit) for index in range(count)])


def gather_near(piece):
    held = piece[None]
    for bit in (4, 2, 1):
        held = jnp.concatenate([held, swap(held, "dp", bit)], axis=0)
    far = swap(held, "mp", 2)
    return (held, swap(held, "mp", 1), far, swap(far, "mp", 1))


def scatter_near(keep, send):
    got = swap(send, "mp", 1)
    near = keep[0].astype(FULL) + got[0].astype(FULL)
    away = (keep[1].astype(FULL) + got[1].astype(FULL)).astype(LOW)
    near = near + swap(away, "mp", 2).astype(FULL)
    for bit, half in ((1, 4), (2, 2), (4, 1)):
        near = near[:half] + swap(near[half:].astype(LOW), "dp", bit).astype(FULL)
    return near[0]


def adam(weight, moment_one, moment_two, incoming, step_rate, decay_rate):
    first_new = BETA_ONE * moment_one + (1.0 - BETA_ONE) * incoming
    second_new = BETA_TWO * moment_two + (1.0 - BETA_TWO) * incoming * incoming
    update = (
        first_new
        / (1.0 - BETA_ONE**STEP)
        / (jnp.sqrt(second_new / (1.0 - BETA_TWO**STEP)) + ADAM_EPSILON)
    )
    return (second_new, weight * (1.0 - step_rate * decay_rate) - step_rate * update)


def pack_attention(weights):
    query, key, value, out = (weights[index] for index in range(4))
    rows = query.shape[0]
    blank = jnp.zeros((rows, HD), weights.dtype)
    first = jnp.concatenate([query, value[:, 128:], value[:, :128], key, blank], axis=1)
    last = jnp.concatenate([out[:, :128], blank, out[:, 128:]], axis=1)
    return first, last


def unpack_attention(first, last):
    query = first[:, :192]
    value = jnp.concatenate([first[:, 256:384], first[:, 192:256]], axis=1)
    key = first[:, 384:576]
    out = jnp.concatenate([last[:, :128], last[:, 192:]], axis=1)
    return jnp.stack([query, key, value, out])


def spread_table(table):
    heads = table.shape[0]
    cube = table.reshape(heads, SPAN, SPAN)
    parts = [cube[:, :, GRID - 1 - col : SPAN - col] for col in range(GRID)]
    flat = jnp.stack(parts, axis=1).reshape(heads, GRID, SPAN * GRID)
    return jnp.pad(flat, ((0, 0), (0, 0), (0, 384 - SPAN * GRID)))


def gather_table(spread):
    heads = spread.shape[0]
    cube = spread[:, :, : SPAN * GRID].reshape(heads, GRID, SPAN, GRID)
    total = 0.0
    for col in range(GRID):
        total = total + jnp.pad(cube[:, col], ((0, 0), (0, 0), (GRID - 1 - col, col)))
    return total.reshape(heads, SPAN * SPAN)


def shards(
    block_input,
    cotangent,
    image_size,
    attention_weights,
    attention_first,
    attention_second,
    mlp_weights,
    mlp_first,
    mlp_second,
    head_params,
    head_first,
    head_second,
    norm_params,
    norm_first,
    norm_second,
):
    near = lax.axis_size("dp") == CHUNKS
    lane_index = lax.axis_index("mp")
    local_rows, width = block_input.shape
    images = local_rows // PATCHES
    local_heads = head_params.shape[0]
    chunk_rows = width // CHUNKS

    first, last = pack_attention(attention_weights.astype(LOW))
    mlp_low = mlp_weights.astype(LOW)
    if near:
        mine = reversed_bits(lax.axis_index("dp")).astype(jnp.int32)[None]
        other = swap(head_params, "mp", 2)
        both = jnp.stack([head_params, other])
        cross = swap(both, "mp", 1)
        tables = jnp.stack([both[0], cross[0], both[1], cross[1]])
        unit_bias = norm_params[8:]
        qkv_pieces = gather_near(first)
        out_pieces = gather_near(last)
        up_pieces = gather_near(mlp_low[0])
        down_pieces = gather_near(mlp_low[1])
        lanes = [lane_index ^ index for index in range(LANES)]
        unit_bias = jnp.stack([lax.dynamic_index_in_dim(unit_bias, lane, 0, False) for lane in lanes])
    else:
        mine = jnp.zeros((1,), jnp.int32)

        def gather_far(piece):
            full = lax.all_gather(piece, "dp", axis=0, tiled=True)
            full = lax.all_gather(full, "mp", axis=0, tiled=False)
            full = full.reshape(LANES, CHUNKS, chunk_rows, piece.shape[1])
            order = [reversed_bits(index) for index in range(CHUNKS)]
            full = jnp.stack([full[:, index] for index in order], axis=1)
            return tuple(full[index] for index in range(LANES))

        tables = lax.all_gather(head_params, "mp", axis=0, tiled=False)
        qkv_pieces = gather_far(first)
        out_pieces = gather_far(last)
        up_pieces = gather_far(mlp_low[0])
        down_pieces = gather_far(mlp_low[1])
        unit_bias = norm_params[8:]

    per_lane = image_size.shape[0] // LANES
    image_dims = lax.dynamic_slice_in_dim(image_size, lane_index * per_lane, per_lane, 0)
    position = jnp.arange(PADDED, dtype=jnp.int32)
    valid = (
        ((position // GRID)[None, :] < image_dims[:, 0:1])
        & ((position % GRID)[None, :] < image_dims[:, 1:2])
        & (position < PATCHES)[None, :]
    )
    mask = jnp.where(valid, 0.0, NEGATIVE).astype(LOW)
    mask = jnp.broadcast_to(mask[:, :, None], (images, PADDED, 128))

    query_bias = tables[:, :, :HD].reshape(LANES, -1)
    value_bias = tables[:, :, HD : 2 * HD].reshape(LANES, -1)
    blank = jnp.zeros((LANES, PACK - 384), FULL)
    add = jnp.concatenate(
        [query_bias, value_bias[:, 128:], value_bias[:, :128], blank], axis=1
    ).reshape(LANES, 1, PACK)
    scale = jnp.where(jnp.arange(PACK) < 192, HD**-0.5, 1.0).astype(FULL)[None]
    spread = spread_table(tables[:, :, 2 * HD :].reshape(LANES * local_heads, -1))

    normed_one, bias = prepare(block_input, norm_params, spread, images)
    qkv, prob, ctx, full = attend(mine, normed_one, bias, add, scale, mask, qkv_pieces, images)
    att, mid, normed_two, grad_down, cot_sum, wo = middle(
        mine, ctx, block_input, cotangent, norm_params, out_pieces, images
    )
    down, grad_normed, keep1, send1, keep2, send2, unit_sums = feed(
        mine, normed_two, grad_down, unit_bias, up_pieces, down_pieces, images
    )
    output, grad_mid, dqkv, keep_out, send_out, grad_spread, sums, cols = back(
        mine, down, grad_normed, mid, att, ctx, cotangent, norm_params, wo, qkv, prob, images, chunk_rows
    )
    keep_qkv, send_qkv = project(mine, normed_one, dqkv, chunk_rows)
    grad_input, first_sums = input_back(dqkv, full, grad_mid, block_input, norm_params, images)

    sums = jnp.sum(sums, axis=1)
    first_sums = jnp.sum(first_sums, axis=1)
    cot_sum = jnp.sum(cot_sum, axis=0)
    vector_rows = jnp.stack(
        [
            first_sums[0],
            first_sums[1],
            sums[0],
            sums[1],
            sums[2] * norm_params[5],
            sums[3],
            cot_sum * norm_params[7],
            sums[4],
        ]
    )
    unit_sums = jnp.sum(unit_sums, axis=1).reshape(LANES, width)
    cols = jnp.sum(cols, axis=1)
    grad_heads = jnp.concatenate(
        [
            cols[:, :192].reshape(LANES, local_heads, HD),
            jnp.concatenate([cols[:, 256:384], cols[:, 192:256]], axis=1).reshape(
                LANES, local_heads, HD
            ),
            gather_table(grad_spread).reshape(LANES, local_heads, -1),
        ],
        axis=2,
    )
    if near:
        placed = jnp.stack(
            [lax.dynamic_index_in_dim(unit_sums, lane, 0, False) for lane in lanes]
        )
        heads_width = grad_heads.shape[2]
        wide = lambda rows: jnp.pad(rows, ((0, 0), (0, heads_width - width)))
        norms = wide(jnp.concatenate([vector_rows, placed], axis=0))
        keep = jnp.concatenate([norms, grad_heads[0], grad_heads[2]], axis=0)
        send = jnp.concatenate([norms, grad_heads[1], grad_heads[3]], axis=0)
        small = keep + swap(send, "mp", 1)
        rest = 12 + local_heads
        keep = small[:rest]
        send = jnp.concatenate([small[:12], small[rest:]], axis=0)
        small = keep + swap(send, "mp", 2)
        for bit in (1, 2, 4):
            small = small + swap(small, "dp", bit)
        reduced_norms = small[:12, :width]
        reduced_heads = small[12:]
        grad_up = scatter_near(keep1, send1)
        grad_dn = scatter_near(keep2, send2)
        grad_out = scatter_near(keep_out, send_out)
        grad_qkv = scatter_near(keep_qkv, send_qkv)
    else:
        norms = jnp.concatenate([vector_rows, unit_sums], axis=0)
        reduced_norms = lax.psum(norms, ("dp", "mp"))
        reduced_heads = lax.psum_scatter(
            lax.psum(grad_heads, "dp"), "mp", scatter_dimension=0, tiled=False
        )

        def scatter_far(keep, send):
            terms = jnp.stack([keep[0], send[0], keep[1], send[1]])
            order = [reversed_bits(index) for index in range(CHUNKS)]
            terms = jnp.stack([terms[:, index] for index in order], axis=1)
            terms = terms.reshape(LANES, width, terms.shape[-1])
            mine_only = lax.psum_scatter(terms, "mp", scatter_dimension=0, tiled=False)
            return lax.psum_scatter(
                mine_only.astype(FULL), "dp", scatter_dimension=0, tiled=True
            )

        grad_up = scatter_far(keep1, send1)
        grad_dn = scatter_far(keep2, send2)
        grad_out = scatter_far(keep_out, send_out)
        grad_qkv = scatter_far(keep_qkv, send_qkv)

    reduced_attention = unpack_attention(grad_qkv, grad_out)
    reduced_mlp = jnp.stack([grad_up, grad_dn])
    attention_second_new, attention_new = adam(
        attention_weights,
        attention_first,
        attention_second,
        reduced_attention,
        RATE_MATRIX,
        DECAY_MATRIX,
    )
    mlp_second_new, mlp_new = adam(
        mlp_weights, mlp_first, mlp_second, reduced_mlp, RATE_MATRIX, DECAY_MATRIX
    )
    head_second_new, head_new = adam(
        head_params, head_first, head_second, reduced_heads, RATE_VECTOR, 0.0
    )
    norm_second_new, norm_new = adam(
        norm_params, norm_first, norm_second, reduced_norms, RATE_VECTOR, 0.0
    )
    return (
        output,
        grad_input,
        reduced_attention,
        attention_second_new,
        attention_new,
        reduced_mlp,
        mlp_second_new,
        mlp_new,
        reduced_heads,
        head_second_new,
        head_new,
        reduced_norms,
        norm_second_new,
        norm_new,
    )


def solution(mesh):
    rows = P(("dp", "mp"), None)
    matrix = P(None, "dp", "mp")
    head = P("mp", None)
    placed = (rows, rows, P("dp", None)) + (matrix,) * 6 + (head,) * 3 + (P(),) * 3
    given = (rows, rows) + (matrix,) * 6 + (head,) * 3 + (P(),) * 3
    return jax.shard_map(shards, mesh=mesh, in_specs=placed, out_specs=given, check_vma=False)
```

```python
import functools

import jax
import jax.numpy as jnp
from jax import lax
from jax.experimental import pallas as pl
from jax.experimental.pallas import tpu as pltpu
from jax.sharding import PartitionSpec as P

HD = 64
GRID = 14
SPAN = 2 * GRID - 1
STEP = 10
PATCHES = 196
PADDED = 208
PACK = 640
OUT_PACK = 256
CHUNKS = 8
LANES = 4
HEADS_LANE = 3

EPSILON = 1e-06
NEGATIVE = -1e30
BETA_ONE = 0.9
BETA_TWO = 0.999
ADAM_EPSILON = 1e-08
RATE_MATRIX = 0.05
RATE_VECTOR = 0.4
DECAY_MATRIX = 0.05

LOW = jnp.bfloat16
FULL = jnp.float32
INV_SQRT2 = 0.7071067811865476
INV_SQRT2PI = 0.3989422804014327
VMEM_LIMIT = 60 << 20


def dot(former, latter, former_dim=1, latter_dim=0):
    return lax.dot_general(
        former,
        latter,
        (((former_dim,), (latter_dim,)), ((), ())),
        preferred_element_type=FULL,
    )


def normalise(values):
    row_mean = jnp.mean(values, axis=-1, keepdims=True)
    centre = values - row_mean
    variance = jnp.mean(centre * centre, axis=-1, keepdims=True)
    inverse = lax.rsqrt(variance + EPSILON)
    return centre * inverse, inverse


def norm_back(incoming, norm_gain, scaled, inverse):
    weighted = incoming * norm_gain
    centred = weighted - jnp.mean(weighted, axis=-1, keepdims=True)
    return inverse * (centred - scaled * jnp.mean(weighted * scaled, axis=-1, keepdims=True))


def fold(values):
    rows, cols = values.shape
    return jnp.sum(values.reshape(rows // 8, 8, cols), axis=0)


def reversed_bits(index):
    return (index & 1) * 4 + (index & 2) + (index & 4) // 4


def whole(shape):
    zeros = (0,) * len(shape)
    return pl.BlockSpec(tuple(shape), lambda *_: zeros)


def params():
    return pltpu.CompilerParams(vmem_limit_bytes=VMEM_LIMIT)


def cost(flops, moved):
    return pl.CostEstimate(flops=int(flops), bytes_accessed=int(moved), transcendentals=0)


def fetch(group, table, refs, columns, target, sem, place):
    for rows, part in table[group]:
        for slot, (source, lead) in enumerate(part):
            height = refs[source].shape[1]
            chunk = target.shape[0] // CHUNKS
            start = (reversed_bits(slot) ^ place) * chunk + rows
            pltpu.make_async_copy(
                refs[source].at[lead, :, columns[0] : columns[1]],
                target.at[pl.ds(pl.multiple_of(start, 16), height), :],
                sem,
            ).start()


def fetched(target, sem):
    pltpu.make_async_copy(target, target, sem).wait()


def anywhere():
    return pl.BlockSpec(memory_space=pl.ANY)


def load_image(pad, source, step):
    for image in range(source.shape[0] // PATCHES):

        @pl.when(step == image)
        def _(image=image):
            pad[0:PATCHES, :] = source[image * PATCHES : (image + 1) * PATCHES, :]

    return pad[...]


def store_image(target, pad, value, step):
    pad[...] = value
    for image in range(target.shape[0] // PATCHES):

        @pl.when(step == image)
        def _(image=image):
            target[image * PATCHES : (image + 1) * PATCHES, :] = pad[0:PATCHES, :]


def prepare_body(images, x_ref, vec_ref, spread_ref, normed_ref, bias_ref, pad_s):
    pad_s[...] = jnp.zeros_like(pad_s)
    for image in range(images):
        scaled, _ = normalise(x_ref[image * PATCHES : (image + 1) * PATCHES, :])
        pad_s[0:PATCHES, :] = scaled * vec_ref[0:1, :] + vec_ref[1:2, :]
        normed_ref[image * PADDED : (image + 1) * PADDED, :] = pad_s[...].astype(LOW)

    def head(index, carry):
        bias_ref[index] = jnp.zeros(bias_ref.shape[1:], FULL)
        for row in range(GRID):
            start = GRID * (GRID - 1 - row)
            bias_ref[index, row * GRID : (row + 1) * GRID, 0:PATCHES] = spread_ref[
                index, :, start : start + PATCHES
            ]
        return carry

    lax.fori_loop(0, bias_ref.shape[0], head, 0)


def prepare(x, vectors, spread, images):
    rows, width = x.shape
    heads = spread.shape[0]
    return pl.pallas_call(
        functools.partial(prepare_body, images),
        out_shape=[
            jax.ShapeDtypeStruct((images * PADDED, width), LOW),
            jax.ShapeDtypeStruct((heads, PADDED, PADDED), FULL),
        ],
        scratch_shapes=[pltpu.VMEM((PADDED, width), FULL)],
        compiler_params=params(),
        cost_estimate=cost(1e6, 8e6),
    )(x, vectors, spread)


Q_TILE = (0, 0, 1)
K_TILE = (3, 3, 4)
V_TILE = (2, 2, 1)
QK_ODD = (False, True, False)
V_ODD = (False, True, True)


def halves():
    lane = lax.broadcasted_iota(jnp.int32, (PADDED, 128), 1)
    return lane


def half_of(value, lane, odd):
    keep = lane >= HD if odd else lane < HD
    return jnp.where(keep, value, jnp.zeros_like(value))


def attend_body(table, me_ref, n_ref, bias_ref, add_ref, scale_ref, mask_ref, *refs):
    pieces = refs[:-5]
    qkv_ref, prob_ref, ctx_ref, full_ref, sems = refs[-5:]

    @pl.when(pl.program_id(0) == 0)
    def _():
        for group in range(LANES):
            fetch(group, table, pieces, (0, PACK), full_ref.at[group], sems.at[group], me_ref[0])
        for group in range(LANES):
            fetched(full_ref.at[group], sems.at[group])

    lane = halves()
    mask = mask_ref[0]
    zero = jnp.zeros_like(mask)
    one = jnp.ones_like(mask)
    for group in range(LANES):
        acc = dot(n_ref[...], full_ref[group])
        qkv = ((acc + add_ref[group]) * scale_ref[...]).astype(LOW)
        qkv_ref[group] = qkv
        tiles = [qkv[:, 128 * t : 128 * (t + 1)] for t in range(5)]
        outs = []
        for head in range(HEADS_LANE):
            odd = QK_ODD[head]
            mark = 0 if odd else HD
            keep = lane >= HD if odd else lane < HD
            key = jnp.where(keep, tiles[K_TILE[head]], jnp.where(lane == mark, mask, zero))
            query = jnp.where(lane == mark, one, tiles[Q_TILE[head]])
            scores = dot(key, query, 1, 1) + bias_ref[group * HEADS_LANE + head]
            top = jnp.max(scores, axis=0, keepdims=True)
            exponent = jnp.exp(scores - top)
            total = jnp.sum(exponent, axis=0, keepdims=True)
            prob = (exponent * (1.0 / total)).astype(LOW)
            prob_ref[0, group * HEADS_LANE + head] = prob
            value = half_of(tiles[V_TILE[head]], lane, V_ODD[head])
            outs.append(dot(prob, value, 0, 0))
        ctx_ref[:, group * OUT_PACK : group * OUT_PACK + 128] = (outs[0] + outs[1]).astype(LOW)
        ctx_ref[:, group * OUT_PACK + 128 : (group + 1) * OUT_PACK] = outs[2].astype(LOW)


def attend(mine, normed, bias, add, scale, mask, gathered, images):
    rows, width = normed.shape
    heads = bias.shape[0]
    pieces, table = gathered
    return pl.pallas_call(
        functools.partial(attend_body, table),
        grid=(images,),
        in_specs=[
            pl.BlockSpec(memory_space=pltpu.SMEM),
            pl.BlockSpec((PADDED, width), lambda i: (i, 0)),
            whole(bias.shape),
            whole(add.shape),
            whole(scale.shape),
            pl.BlockSpec((1, PADDED, 128), lambda i: (i, 0, 0)),
        ]
        + [anywhere()] * len(pieces),
        out_specs=[
            pl.BlockSpec((LANES, PADDED, PACK), lambda i: (0, i, 0)),
            pl.BlockSpec((1, heads, PADDED, PADDED), lambda i: (i, 0, 0, 0)),
            pl.BlockSpec((PADDED, LANES * OUT_PACK), lambda i: (i, 0)),
            whole((LANES, width, PACK)),
        ],
        out_shape=[
            jax.ShapeDtypeStruct((LANES, rows, PACK), LOW),
            jax.ShapeDtypeStruct((images, heads, PADDED, PADDED), LOW),
            jax.ShapeDtypeStruct((rows, LANES * OUT_PACK), LOW),
            jax.ShapeDtypeStruct((LANES, width, PACK), LOW),
        ],
        scratch_shapes=[pltpu.SemaphoreType.DMA((LANES,))],
        compiler_params=params(),
        cost_estimate=cost(1.5e10, 2e7),
    )(mine, normed, bias, add, scale, mask, *pieces)


def middle_body(table, columns, me_ref, ctx_ref, x_ref, cot_ref, vec_ref, *refs):
    pieces = refs[:-8]
    att_ref, mid_ref, n_ref, gd_ref, cs_ref, full_ref, pad_s, sems = refs[-8:]
    step = pl.program_id(0)

    @pl.when(step == 0)
    def _():
        for group in range(LANES):
            fetch(group, table, pieces, columns, full_ref.at[group], sems.at[group], me_ref[0])
        for group in range(LANES):
            fetched(full_ref.at[group], sems.at[group])
        pad_s[...] = jnp.zeros_like(pad_s)
        cs_ref[...] = jnp.zeros_like(cs_ref)

    total = vec_ref[4:5, :]
    for group in range(LANES):
        total = total + dot(
            ctx_ref[:, group * OUT_PACK : (group + 1) * OUT_PACK], full_ref[group], 1, 1
        )
    att_ref[...] = total
    mid = load_image(pad_s, x_ref, step) + vec_ref[5:6, :] * total
    mid_ref[...] = mid
    scaled, _ = normalise(mid)
    n_ref[...] = (scaled * vec_ref[2:3, :] + vec_ref[3:4, :]).astype(LOW)
    cot = load_image(pad_s, cot_ref, step)
    gd_ref[...] = (cot * vec_ref[7:8, :]).astype(LOW)
    cs_ref[...] += fold(cot)


def middle(mine, ctx, x, cot, vectors, gathered, columns, images):
    rows = images * PADDED
    width = x.shape[1]
    pieces, table = gathered
    block = lambda: pl.BlockSpec((PADDED, width), lambda i: (i, 0))
    return pl.pallas_call(
        functools.partial(middle_body, table, columns),
        grid=(images,),
        in_specs=[
            pl.BlockSpec(memory_space=pltpu.SMEM),
            pl.BlockSpec((PADDED, LANES * OUT_PACK), lambda i: (i, 0)),
            whole(x.shape),
            whole(cot.shape),
            whole(vectors.shape),
        ]
        + [anywhere()] * len(pieces),
        out_specs=[block(), block(), block(), block(), whole((8, width)), whole((LANES, width, OUT_PACK))],
        out_shape=[
            jax.ShapeDtypeStruct((rows, width), FULL),
            jax.ShapeDtypeStruct((rows, width), FULL),
            jax.ShapeDtypeStruct((rows, width), LOW),
            jax.ShapeDtypeStruct((rows, width), LOW),
            jax.ShapeDtypeStruct((8, width), FULL),
            jax.ShapeDtypeStruct((LANES, width, OUT_PACK), LOW),
        ],
        scratch_shapes=[pltpu.VMEM((PADDED, width), FULL), pltpu.SemaphoreType.DMA((LANES,))],
        compiler_params=params(),
        cost_estimate=cost(8e9, 1.5e7),
    )(mine, ctx, x, cot, vectors, *pieces)


def gelu_pair(values):
    density = jnp.exp(values * values * -0.5) * INV_SQRT2PI
    below = 0.5 * lax.erf(values * INV_SQRT2) + 0.5
    return values * below, below + values * density


def feed_body(blocks, layout, me_ref, n_ref, gd_ref, ub_ref, *refs):
    count = sum(part[3] for part in layout)
    pieces = refs[:count]
    out_ref, gn_ref, keep_ref, send_ref, gub_ref, nt_s, gdt_s, up_s, down_s, act_s, gh_s, sems = refs[count:]
    step = pl.program_id(0)
    place = me_ref[0]
    rows = n_ref.shape[0]
    units = up_s.shape[3]
    per = rows // blocks

    def begin(group):
        slot = group % 2
        for index, (_, table, first, number, up_at, down_at) in enumerate(layout):
            held = pieces[first : first + number]
            for target, at, kind in ((up_s, up_at, 0), (down_s, down_at, 1)):
                fetch(
                    group,
                    table,
                    held,
                    (at, at + units),
                    target.at[slot, index],
                    sems.at[slot, kind, index],
                    place,
                )

    @pl.when(step == 0)
    def _():
        begin(0)
        nt_s[...] = n_ref[...].T
        gdt_s[...] = gd_ref[...].T
        out_ref[...] = jnp.zeros_like(out_ref)
        gn_ref[...] = jnp.zeros_like(gn_ref)

    for group in range(LANES):

        @pl.when(step == group)
        def _(group=group):
            if group + 1 < LANES:
                begin(group + 1)

    now = step % 2
    parts = len(layout)
    for index in range(parts):
        for kind, target in enumerate((up_s, down_s)):
            fetched(target.at[now, index], sems.at[now, kind, index])
    up_weight = [up_s[now, index] for index in range(parts)]
    down_weight = [down_s[now, index] for index in range(parts)]
    if parts > 1:
        up_weight = [jnp.concatenate(up_weight, axis=1)]
        down_weight = [jnp.concatenate(down_weight, axis=1)]
    up_weight, down_weight = up_weight[0], down_weight[0]
    unit_sums = jnp.zeros((8, up_weight.shape[1]), FULL)
    for block in range(blocks):
        part = slice(block * per, (block + 1) * per)
        hidden = dot(n_ref[part, :], up_weight) + ub_ref[0]
        active, slope = gelu_pair(hidden)
        active = active.astype(LOW)
        act_s[part, :] = active
        grad = (dot(gd_ref[part, :], down_weight) * slope).astype(LOW)
        gh_s[part, :] = grad
        unit_sums = unit_sums + fold(grad.astype(FULL))
        out_ref[part, :] += dot(active, down_weight, 1, 1)
        gn_ref[part, :] += dot(grad, up_weight, 1, 1)
    gub_ref[0] = unit_sums
    grad_up = dot(nt_s[...], gh_s[...]).astype(LOW)
    grad_down = dot(gdt_s[...], act_s[...]).astype(LOW)
    chunk_rows = keep_ref.shape[2]
    wide = grad_up.shape[1]
    for odd, target in enumerate((keep_ref, send_ref)):

        @pl.when(step % 2 == odd)
        def _(target=target):
            for chunk in range(CHUNKS):
                slot = reversed_bits(chunk) ^ reversed_bits(place)
                at = slice(chunk * chunk_rows, (chunk + 1) * chunk_rows)
                target[0, slot, :, :wide] = grad_up[at]
                target[0, slot, :, wide:] = grad_down[at]


def feed(mine, normed, grad_down, unit_bias, groups, units, images):
    rows, width = normed.shape
    blocks = 2 if images <= 4 else 4
    parts = len(groups)
    sub = units // parts
    pieces, layout = [], []
    for (arrays, table), up_at, down_at in groups:
        layout.append((None, table, len(pieces), len(arrays), up_at, down_at))
        pieces.extend(arrays)
    chunk_rows = width // CHUNKS
    grad_block = (1, CHUNKS, chunk_rows, 2 * units)
    grads = jax.ShapeDtypeStruct((2,) + grad_block[1:], LOW)
    return pl.pallas_call(
        functools.partial(feed_body, blocks, layout),
        grid=(LANES,),
        in_specs=[
            pl.BlockSpec(memory_space=pltpu.SMEM),
            whole((rows, width)),
            whole((rows, width)),
            pl.BlockSpec((1, 1, units), lambda j: (j, 0, 0)),
        ]
        + [anywhere()] * len(pieces),
        out_specs=[
            whole((rows, width)),
            whole((rows, width)),
            pl.BlockSpec(grad_block, lambda j: (j // 2, 0, 0, 0)),
            pl.BlockSpec(grad_block, lambda j: (jnp.maximum(j - 1, 0) // 2, 0, 0, 0)),
            pl.BlockSpec((1, 8, units), lambda j: (j, 0, 0)),
        ],
        out_shape=[jax.ShapeDtypeStruct((rows, width), FULL)] * 2
        + [grads] * 2
        + [jax.ShapeDtypeStruct((LANES, 8, units), FULL)],
        scratch_shapes=[
            pltpu.VMEM((width, rows), LOW),
            pltpu.VMEM((width, rows), LOW),
            pltpu.VMEM((2, parts, width, sub), LOW),
            pltpu.VMEM((2, parts, width, sub), LOW),
            pltpu.VMEM((rows, units), LOW),
            pltpu.VMEM((rows, units), LOW),
            pltpu.SemaphoreType.DMA((2, 2, parts)),
        ],
        compiler_params=params(),
        cost_estimate=cost(3.5e10, 4e7),
    )(mine, normed, grad_down, unit_bias.reshape(LANES, 1, units), *pieces)


def back_body(
    down_ref,
    gn_ref,
    mid_ref,
    att_ref,
    cot_ref,
    vec_ref,
    wo_ref,
    qkv_ref,
    prob_ref,
    out_ref,
    gm_ref,
    dqkv_ref,
    ga_ref,
    spread_ref,
    sums_ref,
    cols_ref,
    pad_s,
    out_s,
    pair_s,
):
    step = pl.program_id(0)
    heads = pair_s.shape[0]

    @pl.when(step == 0)
    def _():
        pad_s[...] = jnp.zeros_like(pad_s)
        pair_s[...] = jnp.zeros_like(pair_s)
        sums_ref[...] = jnp.zeros_like(sums_ref)
        cols_ref[...] = jnp.zeros_like(cols_ref)

    cot = load_image(pad_s, cot_ref, step)
    down = down_ref[...] + vec_ref[6:7, :]
    mid = mid_ref[...]
    store_image(out_ref, out_s, mid + vec_ref[7:8, :] * down, step)
    scaled, inverse = normalise(mid)
    grad_normed = gn_ref[...]
    grad_mid = cot + norm_back(grad_normed, vec_ref[2:3, :], scaled, inverse)
    gm_ref[...] = grad_mid
    sums_ref[0] += fold(grad_normed * scaled)
    sums_ref[1] += fold(grad_normed)
    sums_ref[2] += fold(grad_mid)
    sums_ref[3] += fold(grad_mid * att_ref[...])
    sums_ref[4] += fold(cot * down)
    grad_att = (grad_mid * vec_ref[5:6, :]).astype(LOW)
    ga_ref[...] = grad_att

    lane = halves()
    for group in range(LANES):
        grad_ctx = dot(grad_att, wo_ref[group]).astype(LOW)
        qkv = qkv_ref[group]
        tiles = [qkv[:, 128 * t : 128 * (t + 1)] for t in range(5)]
        grads = []
        for head in range(HEADS_LANE):
            odd, value_odd = QK_ODD[head], V_ODD[head]
            query = half_of(tiles[Q_TILE[head]], lane, odd)
            key = half_of(tiles[K_TILE[head]], lane, odd)
            value = tiles[V_TILE[head]]
            half = 128 if head == 2 else 0
            upstream = half_of(grad_ctx[:, half : half + 128], lane, value_odd)
            prob = prob_ref[0, group * HEADS_LANE + head]
            grad_prob = dot(value, upstream, 1, 1)
            soft = prob.astype(FULL)
            weighted = soft * grad_prob
            inner = jnp.sum(weighted, axis=0, keepdims=True)
            grad_score = weighted - soft * inner
            pair_s[group * HEADS_LANE + head] += grad_score
            low_score = grad_score.astype(LOW)
            grads.append(
                (
                    dot(low_score, key, 0, 0) * HD**-0.5,
                    dot(low_score, query),
                    dot(prob, upstream),
                )
            )
        packed = (
            grads[0][0] + grads[1][0],
            grads[2][0] + grads[2][2],
            grads[0][2] + grads[1][2],
            grads[0][1] + grads[1][1],
            grads[2][1],
        )
        for tile, value in enumerate(packed):
            low_value = value.astype(LOW)
            dqkv_ref[group, :, 128 * tile : 128 * (tile + 1)] = low_value
            cols_ref[group, :, 128 * tile : 128 * (tile + 1)] += fold(low_value.astype(FULL))

    @pl.when(step == pl.num_programs(0) - 1)
    def _():
        spread_ref[...] = jnp.zeros_like(spread_ref)

        def head_sum(index, carry):
            for row in range(GRID):
                at = GRID * (GRID - 1 - row)
                spread_ref[index, :, at : at + PATCHES] += pair_s[
                    index, row * GRID : (row + 1) * GRID, 0:PATCHES
                ]
            return carry

        lax.fori_loop(0, heads, head_sum, 0)


def back(down, grad_normed, mid, att, cot, vectors, wo, qkv, prob, images):
    rows, width = mid.shape
    heads = prob.shape[1]
    block = lambda: pl.BlockSpec((PADDED, width), lambda i: (i, 0))
    return pl.pallas_call(
        back_body,
        grid=(images,),
        in_specs=[
            block(),
            block(),
            block(),
            block(),
            whole(cot.shape),
            whole(vectors.shape),
            whole(wo.shape),
            pl.BlockSpec((LANES, PADDED, PACK), lambda i: (0, i, 0)),
            pl.BlockSpec((1, heads, PADDED, PADDED), lambda i: (i, 0, 0, 0)),
        ],
        out_specs=[
            whole(cot.shape),
            block(),
            pl.BlockSpec((LANES, PADDED, PACK), lambda i: (0, i, 0)),
            block(),
            whole((heads, GRID, 384)),
            whole((5, 8, width)),
            whole((LANES, 8, PACK)),
        ],
        out_shape=[
            jax.ShapeDtypeStruct(cot.shape, FULL),
            jax.ShapeDtypeStruct((rows, width), FULL),
            jax.ShapeDtypeStruct((LANES, rows, PACK), LOW),
            jax.ShapeDtypeStruct((rows, width), LOW),
            jax.ShapeDtypeStruct((heads, GRID, 384), FULL),
            jax.ShapeDtypeStruct((5, 8, width), FULL),
            jax.ShapeDtypeStruct((LANES, 8, PACK), FULL),
        ],
        scratch_shapes=[
            pltpu.VMEM((PADDED, width), FULL),
            pltpu.VMEM((PADDED, width), FULL),
            pltpu.VMEM((heads, PADDED, PADDED), FULL),
        ],
        compiler_params=params(),
        cost_estimate=cost(3e10, 4e7),
    )(down, grad_normed, mid, att, cot, vectors, wo, qkv, prob)


def project_body(me_ref, n_ref, dqkv_ref, ga_ref, ctx_ref, keep_ref, send_ref, t_s):
    rows = keep_ref.shape[2]
    mine = reversed_bits(me_ref[0])

    def give(group, grad, first):
        target = (keep_ref, send_ref)[group % 2]
        for chunk in range(CHUNKS):
            target[group // 2, reversed_bits(chunk) ^ mine, :, first : first + grad.shape[1]] = grad[
                chunk * rows : (chunk + 1) * rows
            ]

    t_s[...] = ga_ref[...].T
    for group in range(LANES):
        at = slice(group * OUT_PACK, (group + 1) * OUT_PACK)
        give(group, dot(t_s[...], ctx_ref[:, at]).astype(LOW), PACK)
    t_s[...] = n_ref[...].T
    for group in range(LANES):
        give(group, dot(t_s[...], dqkv_ref[group]).astype(LOW), 0)


def project(mine, normed, dqkv, grad_att, ctx):
    rows, width = normed.shape
    grads = jax.ShapeDtypeStruct((2, CHUNKS, width // CHUNKS, PACK + OUT_PACK), LOW)
    return pl.pallas_call(
        project_body,
        in_specs=[pl.BlockSpec(memory_space=pltpu.SMEM)] + [pl.BlockSpec(memory_space=pltpu.VMEM)] * 4,
        out_shape=[grads, grads],
        scratch_shapes=[pltpu.VMEM((width, rows), LOW)],
        compiler_params=params(),
        cost_estimate=cost(8e9, 1e7),
    )(mine, normed, dqkv, grad_att, ctx)


def input_body(dqkv_ref, full_ref, gm_ref, x_ref, vec_ref, out_ref, sums_ref, pad_s, out_s):
    step = pl.program_id(0)

    @pl.when(step == 0)
    def _():
        pad_s[...] = jnp.zeros_like(pad_s)
        sums_ref[...] = jnp.zeros_like(sums_ref)

    scaled, inverse = normalise(load_image(pad_s, x_ref, step))
    grad = dot(dqkv_ref[0], full_ref[0], 1, 1)
    for group in range(1, LANES):
        grad = grad + dot(dqkv_ref[group], full_ref[group], 1, 1)
    sums_ref[0] += fold(grad * scaled)
    sums_ref[1] += fold(grad)
    result = gm_ref[...] + norm_back(grad, vec_ref[0:1, :], scaled, inverse)
    store_image(out_ref, out_s, result, step)


def input_back(dqkv, full, grad_mid, x, vectors, images):
    width = x.shape[1]
    return pl.pallas_call(
        input_body,
        grid=(images,),
        in_specs=[
            pl.BlockSpec((LANES, PADDED, PACK), lambda i: (0, i, 0)),
            whole(full.shape),
            pl.BlockSpec((PADDED, width), lambda i: (i, 0)),
            whole(x.shape),
            whole(vectors.shape),
        ],
        out_specs=[whole(x.shape), whole((2, 8, width))],
        out_shape=[jax.ShapeDtypeStruct(x.shape, FULL), jax.ShapeDtypeStruct((2, 8, width), FULL)],
        scratch_shapes=[pltpu.VMEM((PADDED, width), FULL)] * 2,
        compiler_params=params(),
        cost_estimate=cost(4e9, 1.5e7),
    )(dqkv, full, grad_mid, x, vectors)


def swap(values, axis, bit):
    count = lax.axis_size(axis)
    return lax.ppermute(values, axis, [(index, index ^ bit) for index in range(count)])


def after(values, *others):
    return lax.optimization_barrier((values,) + others)[0]


def z_gather(piece, *others):
    held = after(piece, *others)[None]
    for bit in (4, 2):
        held = jnp.concatenate([held, swap(held, "dp", bit)], axis=0)
    return held


def plane_one(held):
    half = held.shape[1] // 2
    upper, lower = held[:, :half], held[:, half:]
    return upper, swap(upper, "dp", 1), lower, swap(lower, "mp", 2)


def plane_two(upper, upper_y, lower, lower_x):
    upper = jnp.concatenate([upper, upper_y], axis=0)
    lower = jnp.concatenate([lower, lower_x], axis=0)
    return upper, swap(upper, "mp", 2), lower, swap(lower, "dp", 1)


def plane_core(upper, upper_x, lower, lower_y):
    arrays = [upper, upper_x, lower, lower_y]
    arrays = arrays + [swap(array, "mp", 1) for array in arrays]
    half = upper.shape[1]

    def part(first, far):
        top = [(first + far, slot) for slot in range(8)]
        low = [(first + 2 + slot // 4, 4 * far + slot % 4) for slot in range(8)]
        return ((0, top), (half, low))

    return arrays, (part(0, 0), part(4, 0), part(0, 1), part(4, 1))


def late(state, *others):
    return (state[0], after(state[1], *others), state[2], after(state[3], *others))


def sum_core(keep, send):
    got = swap(send, "mp", 1)
    half = keep.shape[2] // 2

    def term(*at):
        return keep[at].astype(FULL) + got[at].astype(FULL)

    upper, lower = slice(0, half), slice(half, 2 * half)
    one, two = slice(0, 4), slice(4, 8)
    every = slice(None)
    upper_pair = (term(0, every, upper), term(1, every, upper).astype(LOW))
    lower_pair = (term(every, one, lower), term(every, two, lower).astype(LOW))
    return upper_pair, lower_pair


def sum_plane_one(pairs):
    (upper, upper_away), (lower, lower_away) = pairs
    upper_got = swap(upper_away, "mp", 2)
    lower_got = swap(lower_away, "dp", 1)
    return upper, upper_got, lower, lower_got


def sum_plane_two(upper, upper_got, lower, lower_got):
    upper_got, lower_got = upper_got.astype(FULL), lower_got.astype(FULL)
    upper_next = swap((upper[4:] + upper_got[4:]).astype(LOW), "dp", 1)
    lower_next = swap((lower[1] + lower_got[1]).astype(LOW), "mp", 2)
    return upper[:4] + upper_got[:4], upper_next, lower[0] + lower_got[0], lower_next


def sum_line_one(upper, upper_got, lower, lower_got):
    here = jnp.concatenate(
        [upper + upper_got.astype(FULL), lower + lower_got.astype(FULL)], axis=1
    )
    return here[:2], swap(here[2:].astype(LOW), "dp", 2)


def sum_line_two(here, got):
    here = here + got.astype(FULL)
    return here[0], swap(here[1].astype(LOW)[None], "dp", 4)[0]


def sum_end(here, got):
    return here + got.astype(FULL)


def adam(weight, moment_one, moment_two, incoming, step_rate, decay_rate):
    first_new = BETA_ONE * moment_one + (1.0 - BETA_ONE) * incoming
    second_new = BETA_TWO * moment_two + (1.0 - BETA_TWO) * incoming * incoming
    update = (
        first_new
        / (1.0 - BETA_ONE**STEP)
        / (jnp.sqrt(second_new / (1.0 - BETA_TWO**STEP)) + ADAM_EPSILON)
    )
    return (second_new, weight * (1.0 - step_rate * decay_rate) - step_rate * update)


def pack_attention(weights):
    query, key, value, out = (weights[index] for index in range(4))
    rows = query.shape[0]
    blank = jnp.zeros((rows, HD), weights.dtype)
    first = jnp.concatenate([query, value[:, 128:], value[:, :128], key, blank], axis=1)
    last = jnp.concatenate([out[:, :128], blank, out[:, 128:]], axis=1)
    return first, last


def unpack_attention(first, last):
    query = first[:, :192]
    value = jnp.concatenate([first[:, 256:384], first[:, 192:256]], axis=1)
    key = first[:, 384:576]
    out = jnp.concatenate([last[:, :128], last[:, 192:]], axis=1)
    return jnp.stack([query, key, value, out])


def spread_table(table):
    heads = table.shape[0]
    cube = table.reshape(heads, SPAN, SPAN)
    parts = [cube[:, :, GRID - 1 - col : SPAN - col] for col in range(GRID)]
    flat = jnp.stack(parts, axis=1).reshape(heads, GRID, SPAN * GRID)
    return jnp.pad(flat, ((0, 0), (0, 0), (0, 384 - SPAN * GRID)))


def gather_table(spread):
    heads = spread.shape[0]
    cube = spread[:, :, : SPAN * GRID].reshape(heads, GRID, SPAN, GRID)
    total = 0.0
    for col in range(GRID):
        total = total + jnp.pad(cube[:, col], ((0, 0), (0, 0), (GRID - 1 - col, col)))
    return total.reshape(heads, SPAN * SPAN)


def shards(
    block_input,
    cotangent,
    image_size,
    attention_weights,
    attention_first,
    attention_second,
    mlp_weights,
    mlp_first,
    mlp_second,
    head_params,
    head_first,
    head_second,
    norm_params,
    norm_first,
    norm_second,
):
    near = lax.axis_size("dp") == CHUNKS
    lane_index = lax.axis_index("mp")
    local_rows, width = block_input.shape
    images = local_rows // PATCHES
    local_heads = head_params.shape[0]
    chunk_rows = width // CHUNKS

    first, last = pack_attention(attention_weights.astype(LOW))
    mlp_low = mlp_weights.astype(LOW)
    units = mlp_low.shape[2]
    part = units // 2
    second = jnp.concatenate([last, mlp_low[0, :, :part], mlp_low[1, :, :part]], axis=1)
    third = jnp.concatenate([mlp_low[0, :, part:], mlp_low[1, :, part:]], axis=1)
    if near:
        mine = lax.axis_index("dp").astype(jnp.int32)[None]
        other = swap(head_params, "mp", 2)
        both = jnp.stack([head_params, other])
        cross = swap(both, "mp", 1)
        tables = jnp.stack([both[0], cross[0], both[1], cross[1]])
        unit_bias = norm_params[8:]
        lanes = [lane_index ^ index for index in range(LANES)]
        unit_bias = jnp.stack([lax.dynamic_index_in_dim(unit_bias, lane, 0, False) for lane in lanes])
        first_z = z_gather(first)
        second_z = z_gather(second, first_z)
        third_z = z_gather(third, second_z)
        first_state = plane_two(*plane_one(first_z))
        first_all = plane_core(*first_state)
    else:
        mine = jnp.zeros((1,), jnp.int32)

        def gather_far(piece):
            full = lax.all_gather(piece, "dp", axis=0, tiled=True)
            full = lax.all_gather(full, "mp", axis=0, tiled=False)
            full = full.reshape(LANES, CHUNKS, chunk_rows, piece.shape[1])
            order = [reversed_bits(index) for index in range(CHUNKS)]
            full = jnp.stack([full[:, index] for index in order], axis=1)
            slots = range(CHUNKS)
            table = tuple(((0, [(group, slot) for slot in slots]),) for group in range(LANES))
            return [full[index] for index in range(LANES)], table

        tables = lax.all_gather(head_params, "mp", axis=0, tiled=False)
        unit_bias = norm_params[8:]
        first_all = gather_far(first)
        second_all = gather_far(second)
        third_all = gather_far(third)

    per_lane = image_size.shape[0] // LANES
    image_dims = lax.dynamic_slice_in_dim(image_size, lane_index * per_lane, per_lane, 0)
    position = jnp.arange(PADDED, dtype=jnp.int32)
    valid = (
        ((position // GRID)[None, :] < image_dims[:, 0:1])
        & ((position % GRID)[None, :] < image_dims[:, 1:2])
        & (position < PATCHES)[None, :]
    )
    mask = jnp.where(valid, 0.0, NEGATIVE).astype(LOW)
    mask = jnp.broadcast_to(mask[:, :, None], (images, PADDED, 128))

    query_bias = tables[:, :, :HD].reshape(LANES, -1)
    value_bias = tables[:, :, HD : 2 * HD].reshape(LANES, -1)
    blank = jnp.zeros((LANES, PACK - 384), FULL)
    add = jnp.concatenate(
        [query_bias, value_bias[:, 128:], value_bias[:, :128], blank], axis=1
    ).reshape(LANES, 1, PACK)
    scale = jnp.where(jnp.arange(PACK) < 192, HD**-0.5, 1.0).astype(FULL)[None]
    spread = spread_table(tables[:, :, 2 * HD :].reshape(LANES * local_heads, -1))

    normed_one, bias = prepare(block_input, norm_params, spread, images)
    if near:
        second_state = plane_two(*plane_one(after(second_z, bias)))
    qkv, prob, ctx, full = attend(mine, normed_one, bias, add, scale, mask, first_all, images)
    if near:
        third_state = plane_one(third_z)
        second_all = plane_core(*late(second_state, ctx))
        third_all = plane_core(*plane_two(*late(third_state, ctx)))
    att, mid, normed_two, grad_down, cot_sum, wo = middle(
        mine, ctx, block_input, cotangent, norm_params, second_all, (0, OUT_PACK), images
    )
    groups = ((second_all, OUT_PACK, OUT_PACK + part), (third_all, 0, part))
    down, grad_normed, keep_mlp, send_mlp, unit_sums = feed(
        mine, normed_two, grad_down, unit_bias, groups, units, images
    )
    if near:
        mlp_pairs = sum_core(keep_mlp, send_mlp)
        mlp_terms = sum_plane_one(mlp_pairs)
        down = after(down, mlp_pairs[0][1], mlp_pairs[1][1])
    output, grad_mid, dqkv, grad_att, grad_spread, sums, cols = back(
        down, grad_normed, mid, att, cotangent, norm_params, wo, qkv, prob, images
    )
    if near:
        mlp_terms = sum_plane_two(*late(mlp_terms, dqkv))
        dqkv = after(dqkv, mlp_terms[0], mlp_terms[2])
    keep_att, send_att = project(mine, normed_one, dqkv, grad_att, ctx)
    if near:
        mlp_line = sum_line_one(*late(mlp_terms, send_att))
        att_pairs = sum_core(keep_att, after(send_att, mlp_line[0]))
        att_terms = sum_plane_one(att_pairs)
        dqkv = after(dqkv, att_pairs[0][1], att_pairs[1][1])
    grad_input, first_sums = input_back(dqkv, full, grad_mid, block_input, norm_params, images)

    sums = jnp.sum(sums, axis=1)
    first_sums = jnp.sum(first_sums, axis=1)
    cot_sum = jnp.sum(cot_sum, axis=0)
    vector_rows = jnp.stack(
        [
            first_sums[0],
            first_sums[1],
            sums[0],
            sums[1],
            sums[2] * norm_params[5],
            sums[3],
            cot_sum * norm_params[7],
            sums[4],
        ]
    )
    unit_sums = jnp.sum(unit_sums, axis=1).reshape(LANES, width)
    cols = jnp.sum(cols, axis=1)
    grad_heads = jnp.concatenate(
        [
            cols[:, :192].reshape(LANES, local_heads, HD),
            jnp.concatenate([cols[:, 256:384], cols[:, 192:256]], axis=1).reshape(
                LANES, local_heads, HD
            ),
            gather_table(grad_spread).reshape(LANES, local_heads, -1),
        ],
        axis=2,
    )
    if near:
        placed = jnp.stack(
            [lax.dynamic_index_in_dim(unit_sums, lane, 0, False) for lane in lanes]
        )
        heads_width = grad_heads.shape[2]
        wide = lambda rows: jnp.pad(rows, ((0, 0), (0, heads_width - width)))
        norms = wide(jnp.concatenate([vector_rows, placed], axis=0))
        keep = jnp.concatenate([norms, grad_heads[0], grad_heads[2]], axis=0)
        send = jnp.concatenate([norms, grad_heads[1], grad_heads[3]], axis=0)
        small = keep + swap(after(send, att_terms[1], att_terms[3]), "mp", 1)
        rest = 12 + local_heads
        keep = small[:rest]
        send = jnp.concatenate([small[:12], small[rest:]], axis=0)
        small = keep + swap(send, "mp", 2)
        for bit in (1, 2, 4):
            small = small + swap(small, "dp", bit)
        att_terms = sum_plane_two(*att_terms)
        mlp_line = sum_line_two(*mlp_line)
        att_line = sum_line_two(*sum_line_one(*att_terms))
        sum_mlp = sum_end(*mlp_line)
        sum_att = sum_end(*att_line)
        reduced_norms = small[:12, :width]
        reduced_heads = small[12:]
    else:
        norms = jnp.concatenate([vector_rows, unit_sums], axis=0)
        reduced_norms = lax.psum(norms, ("dp", "mp"))
        reduced_heads = lax.psum_scatter(
            lax.psum(grad_heads, "dp"), "mp", scatter_dimension=0, tiled=False
        )

        def scatter_far(keep, send):
            terms = jnp.stack([keep[0], send[0], keep[1], send[1]])
            order = [reversed_bits(index) for index in range(CHUNKS)]
            terms = jnp.stack([terms[:, index] for index in order], axis=1)
            terms = terms.reshape(LANES, width, terms.shape[-1])
            mine_only = lax.psum_scatter(terms, "mp", scatter_dimension=0, tiled=False)
            return lax.psum_scatter(
                mine_only.astype(FULL), "dp", scatter_dimension=0, tiled=True
            )

        sum_mlp = scatter_far(keep_mlp, send_mlp)
        sum_att = scatter_far(keep_att, send_att)

    reduced_attention = unpack_attention(sum_att[:, :PACK], sum_att[:, PACK:])
    reduced_mlp = jnp.stack([sum_mlp[:, :units], sum_mlp[:, units:]])
    attention_second_new, attention_new = adam(
        attention_weights,
        attention_first,
        attention_second,
        reduced_attention,
        RATE_MATRIX,
        DECAY_MATRIX,
    )
    mlp_second_new, mlp_new = adam(
        mlp_weights, mlp_first, mlp_second, reduced_mlp, RATE_MATRIX, DECAY_MATRIX
    )
    head_second_new, head_new = adam(
        head_params, head_first, head_second, reduced_heads, RATE_VECTOR, 0.0
    )
    norm_second_new, norm_new = adam(
        norm_params, norm_first, norm_second, reduced_norms, RATE_VECTOR, 0.0
    )
    return (
        output,
        grad_input,
        reduced_attention,
        attention_second_new,
        attention_new,
        reduced_mlp,
        mlp_second_new,
        mlp_new,
        reduced_heads,
        head_second_new,
        head_new,
        reduced_norms,
        norm_second_new,
        norm_new,
    )


def solution(mesh):
    rows = P(("dp", "mp"), None)
    matrix = P(None, "dp", "mp")
    head = P("mp", None)
    placed = (rows, rows, P("dp", None)) + (matrix,) * 6 + (head,) * 3 + (P(),) * 3
    given = (rows, rows) + (matrix,) * 6 + (head,) * 3 + (P(),) * 3
    return jax.shard_map(shards, mesh=mesh, in_specs=placed, out_specs=given, check_vma=False)
```

```python
import functools

import jax
import jax.numpy as jnp
import numpy as np
from jax import lax
from jax.experimental import pallas as pl
from jax.experimental.pallas import tpu as pltpu
from jax.sharding import PartitionSpec as P

HD = 64
GRID = 14
SPAN = 2 * GRID - 1
STEP = 10
PATCHES = 196
PADDED = 208
PACK = 640
OUT_PACK = 256
CHUNKS = 8
LANES = 4
HEADS_LANE = 3
TWO = 2
TABLE = 768
SPREAD = 384

EPSILON = 1e-06
NEGATIVE = -1e30
BETA_ONE = 0.9
BETA_TWO = 0.999
ADAM_EPSILON = 1e-08
RATE_MATRIX = 0.05
RATE_VECTOR = 0.4
DECAY_MATRIX = 0.05

LOW = jnp.bfloat16
FULL = jnp.float32
INV_SQRT2 = 0.7071067811865476
INV_SQRT2PI = 0.3989422804014327
VMEM_LIMIT = 60 << 20


def dot(former, latter, former_dim=1, latter_dim=0):
    return lax.dot_general(
        former,
        latter,
        (((former_dim,), (latter_dim,)), ((), ())),
        preferred_element_type=FULL,
    )


def normalise(values):
    row_mean = jnp.mean(values, axis=-1, keepdims=True)
    centre = values - row_mean
    variance = jnp.mean(centre * centre, axis=-1, keepdims=True)
    inverse = lax.rsqrt(variance + EPSILON)
    return centre * inverse, inverse


def norm_back(incoming, norm_gain, scaled, inverse):
    weighted = incoming * norm_gain
    centred = weighted - jnp.mean(weighted, axis=-1, keepdims=True)
    return inverse * (centred - scaled * jnp.mean(weighted * scaled, axis=-1, keepdims=True))


def fold(values):
    rows, cols = values.shape
    return jnp.sum(values.reshape(rows // 8, 8, cols), axis=0)


def reversed_bits(index):
    return (index & 1) * 4 + (index & 2) + (index & 4) // 4


def whole(shape):
    zeros = (0,) * len(shape)
    return pl.BlockSpec(tuple(shape), lambda *_: zeros)


def params():
    return pltpu.CompilerParams(vmem_limit_bytes=VMEM_LIMIT)


def cost(flops, moved):
    return pl.CostEstimate(flops=int(flops), bytes_accessed=int(moved), transcendentals=0)


def fetch(group, table, refs, columns, target, sem, place):
    for rows, part in table[group]:
        for slot, (source, lead) in enumerate(part):
            height = refs[source].shape[1]
            chunk = target.shape[0] // CHUNKS
            start = (reversed_bits(slot) ^ place) * chunk + rows
            pltpu.make_async_copy(
                refs[source].at[lead, :, columns[0] : columns[1]],
                target.at[pl.ds(pl.multiple_of(start, 16), height), :],
                sem,
            ).start()


def fetched(target, sem):
    pltpu.make_async_copy(target, target, sem).wait()


def anywhere():
    return pl.BlockSpec(memory_space=pl.ANY)


def load_images(pad, source, step):
    count = pad.shape[0] // PADDED
    for first in range(0, source.shape[0] // PATCHES, count):

        @pl.when(step == first // count)
        def _(first=first):
            for index in range(count):
                at = (first + index) * PATCHES
                pad[index * PADDED : index * PADDED + PATCHES, :] = source[at : at + PATCHES, :]

    return pad[...]


def store_images(target, pad, value, step):
    count = pad.shape[0] // PADDED
    pad[...] = value
    for first in range(0, target.shape[0] // PATCHES, count):

        @pl.when(step == first // count)
        def _(first=first):
            for index in range(count):
                at = (first + index) * PATCHES
                target[at : at + PATCHES, :] = pad[index * PADDED : index * PADDED + PATCHES, :]


def first_norm_body(images, x_ref, cot_ref, vec_ref, normed_ref, gd_ref, pad_s):
    pad_s[...] = jnp.zeros_like(pad_s)
    for image in range(images):
        rows = slice(image * PATCHES, (image + 1) * PATCHES)
        target = slice(image * PADDED, (image + 1) * PADDED)
        scaled, _ = normalise(x_ref[rows, :])
        pad_s[0:PATCHES, :] = scaled * vec_ref[0:1, :] + vec_ref[1:2, :]
        normed_ref[target, :] = pad_s[...].astype(LOW)
        pad_s[0:PATCHES, :] = cot_ref[rows, :] * vec_ref[7:8, :]
        gd_ref[target, :] = pad_s[...].astype(LOW)


def first_norm(x, cot, vectors, images):
    width = x.shape[1]
    return pl.pallas_call(
        functools.partial(first_norm_body, images),
        out_shape=[jax.ShapeDtypeStruct((images * PADDED, width), LOW)] * 2,
        scratch_shapes=[pltpu.VMEM((PADDED, width), FULL)],
        compiler_params=params(),
        cost_estimate=cost(3e9, 4e6),
    )(x, cot, vectors)


def thin_matrix():
    matrix = np.zeros((TABLE, SPREAD), np.float32)
    for row in range(SPAN):
        for col in range(GRID):
            matrix[row * SPAN + col, row * GRID + col] = 1.0
    return matrix


def exact_dot(values, onehot, latter_dim=0):
    high = values.astype(LOW)
    rest = values - high.astype(FULL)
    mid = rest.astype(LOW)
    low = (rest - mid.astype(FULL)).astype(LOW)
    return (
        dot(high, onehot, 1, latter_dim)
        + dot(mid, onehot, 1, latter_dim)
        + dot(low, onehot, 1, latter_dim)
    )


def turn(values, shift):
    return pltpu.roll(values, shift % values.shape[1], 1)


def bias_body(t0, t1, t2, t3, thin_ref, bias_ref, add_ref, table_s, turned_s, spread_s):
    table_s[...] = jnp.zeros_like(table_s)
    for group, table in enumerate((t0, t1, t2, t3)):
        heads = slice(group * HEADS_LANE, (group + 1) * HEADS_LANE)
        table_s[heads, 0 : SPAN * SPAN] = table[:, 2 * HD :]
        rows = [table[head : head + 1, :HD] for head in range(HEADS_LANE)]
        more = [table[head : head + 1, HD : 2 * HD] for head in range(HEADS_LANE)]
        add_ref[group] = jnp.concatenate(
            rows + [more[2], more[0], more[1], jnp.zeros((1, PACK - 384), FULL)], axis=1
        )
    table = table_s[...]
    for col in range(GRID):
        turned_s[16 * col : 16 * (col + 1), :] = turn(table, col - (GRID - 1))
    spread = exact_dot(turned_s[...], thin_ref[...])
    for col in range(GRID):
        spread_s[:, col, :] = spread[16 * col : 16 * (col + 1)]

    def head(index, carry):
        bias_ref[index] = jnp.zeros(bias_ref.shape[1:], FULL)
        for row in range(GRID):
            start = GRID * (GRID - 1 - row)
            bias_ref[index, row * GRID : (row + 1) * GRID, 0:PATCHES] = spread_s[
                index, :, start : start + PATCHES
            ]
        return carry

    lax.fori_loop(0, bias_ref.shape[0], head, 0)


def spread_bias(tables, thin):
    heads = LANES * HEADS_LANE
    return pl.pallas_call(
        bias_body,
        out_shape=[
            jax.ShapeDtypeStruct((heads, PADDED, PADDED), FULL),
            jax.ShapeDtypeStruct((LANES, 1, PACK), FULL),
        ],
        scratch_shapes=[
            pltpu.VMEM((16, TABLE), FULL),
            pltpu.VMEM((16 * GRID, TABLE), FULL),
            pltpu.VMEM((16, GRID, SPREAD), FULL),
        ],
        compiler_params=params(),
        cost_estimate=cost(3e9, 4e6),
    )(*tables, thin)


Q_TILE = (0, 0, 1)
K_TILE = (3, 3, 4)
V_TILE = (2, 2, 1)
QK_ODD = (False, True, False)
V_ODD = (False, True, True)


def grid_places():
    position = np.arange(PADDED)
    row = np.where(position < PATCHES, position // GRID, 4 * GRID)
    places = np.stack([row, position % GRID]).astype(np.int32)
    return np.broadcast_to(places[:, :, None], (2, PADDED, 128)).copy()


def halves():
    lane = lax.broadcasted_iota(jnp.int32, (PADDED, 128), 1)
    return lane


def half_of(value, lane, odd):
    keep = lane >= HD if odd else lane < HD
    return jnp.where(keep, value, jnp.zeros_like(value))


def attend_body(table, images, me_ref, size_ref, grid_ref, n_ref, bias_ref, add_ref, *refs):
    pieces = refs[:-5]
    qkv_ref, prob_ref, ctx_ref, weight_s, sems = refs[-5:]
    step = pl.program_id(0)

    @pl.when(step == 0)
    def _():
        for group in range(LANES):
            fetch(group, table, pieces, (0, PACK), weight_s.at[group], sems.at[group], me_ref[0])

    fetched(weight_s.at[step], sems.at[step])
    scale = jnp.where(
        lax.broadcasted_iota(jnp.int32, (1, PACK), 1) < HEADS_LANE * HD, HD**-0.5, 1.0
    )
    acc = dot(n_ref[...], weight_s[step])
    qkv_ref[0] = ((acc + add_ref[0]) * scale).astype(LOW)

    lane = halves()
    masks = []
    for image in range(images):
        index = me_ref[2] * images + image
        inside = (grid_ref[0] < size_ref[index, 0]) & (grid_ref[1] < size_ref[index, 1])
        masks.append(jnp.where(inside, 0.0, NEGATIVE).astype(LOW))
    zero = jnp.zeros_like(masks[0])
    one = jnp.ones_like(masks[0])

    def tile(image, index):
        return qkv_ref[0, image * PADDED : (image + 1) * PADDED, 128 * index : 128 * (index + 1)]

    def score(image, head):
        odd = QK_ODD[head]
        mark = 0 if odd else HD
        keep = lane >= HD if odd else lane < HD
        key = jnp.where(
            keep, tile(image, K_TILE[head]), jnp.where(lane == mark, masks[image], zero)
        )
        query = jnp.where(lane == mark, one, tile(image, Q_TILE[head]))
        return dot(key, query, 1, 1) + bias_ref[head]

    def soften(scores, image, head):
        top = jnp.max(scores, axis=0, keepdims=True)
        exponent = jnp.exp(scores - top)
        total = jnp.sum(exponent, axis=0, keepdims=True)
        prob = (exponent * (1.0 / total)).astype(LOW)
        prob_ref[image, head] = prob
        return prob

    def gather(prob, image, head):
        return dot(prob, half_of(tile(image, V_TILE[head]), lane, V_ODD[head]), 0, 0)

    work = [(image, head) for image in range(images) for head in range(HEADS_LANE)]
    scores, probs, outs = {}, {}, {}
    for turn_index in range(len(work) + 2):
        if turn_index < len(work):
            scores[turn_index] = score(*work[turn_index])
        if 0 <= turn_index - 1 < len(work):
            probs[turn_index - 1] = soften(scores.pop(turn_index - 1), *work[turn_index - 1])
        done = turn_index - 2
        if done >= 0:
            image, head = work[done]
            outs[head] = gather(probs.pop(done), image, head)
            if head == HEADS_LANE - 1:
                rows = slice(image * PADDED, (image + 1) * PADDED)
                ctx_ref[rows, :128] = (outs[0] + outs[1]).astype(LOW)
                ctx_ref[rows, 128:] = outs[2].astype(LOW)


def attend(mine, sizes, normed, bias, add, gathered, images):
    rows, width = normed.shape
    heads = bias.shape[0]
    pieces, table = gathered
    return pl.pallas_call(
        functools.partial(attend_body, table, images),
        grid=(LANES,),
        in_specs=[
            pl.BlockSpec(memory_space=pltpu.SMEM),
            pl.BlockSpec(memory_space=pltpu.SMEM),
            whole((2, PADDED, 128)),
            whole(normed.shape),
            pl.BlockSpec((HEADS_LANE, PADDED, PADDED), lambda g: (g, 0, 0)),
            pl.BlockSpec((1, 1, PACK), lambda g: (g, 0, 0)),
        ]
        + [anywhere()] * len(pieces),
        out_specs=[
            pl.BlockSpec((1, rows, PACK), lambda g: (g, 0, 0)),
            pl.BlockSpec((images, HEADS_LANE, PADDED, PADDED), lambda g: (0, g, 0, 0)),
            pl.BlockSpec((rows, OUT_PACK), lambda g: (0, g)),
        ],
        out_shape=[
            jax.ShapeDtypeStruct((LANES, rows, PACK), LOW),
            jax.ShapeDtypeStruct((images, heads, PADDED, PADDED), LOW),
            jax.ShapeDtypeStruct((rows, LANES * OUT_PACK), LOW),
        ],
        scratch_shapes=[
            pltpu.VMEM((LANES, width, PACK), LOW),
            pltpu.SemaphoreType.DMA((LANES,)),
        ],
        compiler_params=params(),
        cost_estimate=cost(1.5e10, 2e7),
    )(mine, sizes, jnp.asarray(grid_places()), normed, bias, add, *pieces)


def middle_body(table, columns, me_ref, ctx_ref, x_ref, vec_ref, *refs):
    pieces = refs[:-6]
    att_ref, mid_ref, n_ref, weight_s, pad_s, sems = refs[-6:]
    step = pl.program_id(0)

    @pl.when(step == 0)
    def _():
        for group in range(LANES):
            fetch(group, table, pieces, columns, weight_s.at[group], sems.at[group], me_ref[0])
        for group in range(LANES):
            fetched(weight_s.at[group], sems.at[group])
        pad_s[...] = jnp.zeros_like(pad_s)

    total = vec_ref[4:5, :]
    for group in range(LANES):
        total = total + dot(
            ctx_ref[:, group * OUT_PACK : (group + 1) * OUT_PACK], weight_s[group], 1, 1
        )
    att_ref[...] = total.astype(LOW)
    mid = load_images(pad_s, x_ref, step) + vec_ref[5:6, :] * total
    mid_ref[...] = mid
    scaled, _ = normalise(mid)
    n_ref[...] = (scaled * vec_ref[2:3, :] + vec_ref[3:4, :]).astype(LOW)


def middle(mine, ctx, x, vectors, gathered, columns, images):
    rows = images * PADDED
    width = x.shape[1]
    pieces, table = gathered
    block = lambda: pl.BlockSpec((TWO * PADDED, width), lambda i: (i, 0))
    return pl.pallas_call(
        functools.partial(middle_body, table, columns),
        grid=(images // TWO,),
        in_specs=[
            pl.BlockSpec(memory_space=pltpu.SMEM),
            pl.BlockSpec((TWO * PADDED, LANES * OUT_PACK), lambda i: (i, 0)),
            whole(x.shape),
            whole(vectors.shape),
        ]
        + [anywhere()] * len(pieces),
        out_specs=[block(), block(), block()],
        out_shape=[
            jax.ShapeDtypeStruct((rows, width), LOW),
            jax.ShapeDtypeStruct((rows, width), FULL),
            jax.ShapeDtypeStruct((rows, width), LOW),
        ],
        scratch_shapes=[
            pltpu.VMEM((LANES, width, OUT_PACK), LOW),
            pltpu.VMEM((TWO * PADDED, width), FULL),
            pltpu.SemaphoreType.DMA((LANES,)),
        ],
        compiler_params=params(),
        cost_estimate=cost(8e9, 1.5e7),
    )(mine, ctx, x, vectors, *pieces)


def gelu_pair(values):
    density = jnp.exp(values * values * -0.5) * INV_SQRT2PI
    below = 0.5 * lax.erf(values * INV_SQRT2) + 0.5
    return values * below, below + values * density


def feed_body(blocks, layout, me_ref, n_ref, gd_ref, ub_ref, *refs):
    count = sum(part[3] for part in layout)
    pieces = refs[:count]
    out_ref, gn_ref, keep_ref, send_ref, gub_ref, nt_s, gdt_s, up_s, down_s, act_s, gh_s, sems = refs[count:]
    step = pl.program_id(0)
    place = me_ref[0]
    rows = n_ref.shape[0]
    units = up_s.shape[3]
    per = rows // blocks

    def begin(group):
        slot = group % 2
        for index, (_, table, first, number, up_at, down_at) in enumerate(layout):
            held = pieces[first : first + number]
            for target, at, kind in ((up_s, up_at, 0), (down_s, down_at, 1)):
                fetch(
                    group,
                    table,
                    held,
                    (at, at + units),
                    target.at[slot, index],
                    sems.at[slot, kind, index],
                    place,
                )

    @pl.when(step == 0)
    def _():
        begin(0)
        nt_s[...] = n_ref[...].T
        gdt_s[...] = gd_ref[...].T
        out_ref[...] = jnp.zeros_like(out_ref)
        gn_ref[...] = jnp.zeros_like(gn_ref)

    for group in range(LANES):

        @pl.when(step == group)
        def _(group=group):
            if group + 1 < LANES:
                begin(group + 1)

    now = step % 2
    parts = len(layout)
    for index in range(parts):
        for kind, target in enumerate((up_s, down_s)):
            fetched(target.at[now, index], sems.at[now, kind, index])
    up_weight = [up_s[now, index] for index in range(parts)]
    down_weight = [down_s[now, index] for index in range(parts)]
    if parts > 1:
        up_weight = [jnp.concatenate(up_weight, axis=1)]
        down_weight = [jnp.concatenate(down_weight, axis=1)]
    up_weight, down_weight = up_weight[0], down_weight[0]
    true_lane = step ^ me_ref[1]
    unit_bias = ub_ref[true_lane]
    unit_sums = jnp.zeros((8, up_weight.shape[1]), FULL)
    for block in range(blocks):
        part = slice(block * per, (block + 1) * per)
        hidden = dot(n_ref[part, :], up_weight) + unit_bias
        active, slope = gelu_pair(hidden)
        active = active.astype(LOW)
        act_s[part, :] = active
        grad = (dot(gd_ref[part, :], down_weight) * slope).astype(LOW)
        gh_s[part, :] = grad
        unit_sums = unit_sums + fold(grad.astype(FULL))
        out_ref[part, :] += dot(active, down_weight, 1, 1)
        gn_ref[part, :] += dot(grad, up_weight, 1, 1)
    gub_ref[true_lane] = jnp.sum(unit_sums, axis=0, keepdims=True)
    grad_up = dot(nt_s[...], gh_s[...]).astype(LOW)
    grad_down = dot(gdt_s[...], act_s[...]).astype(LOW)
    chunk_rows = keep_ref.shape[2]
    wide = grad_up.shape[1]
    for odd, target in enumerate((keep_ref, send_ref)):

        @pl.when(step % 2 == odd)
        def _(target=target):
            for chunk in range(CHUNKS):
                slot = reversed_bits(chunk) ^ reversed_bits(place)
                at = slice(chunk * chunk_rows, (chunk + 1) * chunk_rows)
                target[0, slot, :, :wide] = grad_up[at]
                target[0, slot, :, wide:] = grad_down[at]


def feed(mine, normed, grad_down, unit_bias, groups, units, images):
    rows, width = normed.shape
    blocks = 2 if images <= 4 else 4
    parts = len(groups)
    sub = units // parts
    pieces, layout = [], []
    for (arrays, table), up_at, down_at in groups:
        layout.append((None, table, len(pieces), len(arrays), up_at, down_at))
        pieces.extend(arrays)
    chunk_rows = width // CHUNKS
    grad_block = (1, CHUNKS, chunk_rows, 2 * units)
    grads = jax.ShapeDtypeStruct((2,) + grad_block[1:], LOW)
    return pl.pallas_call(
        functools.partial(feed_body, blocks, layout),
        grid=(LANES,),
        in_specs=[
            pl.BlockSpec(memory_space=pltpu.SMEM),
            whole((rows, width)),
            whole((rows, width)),
            whole((LANES, 1, units)),
        ]
        + [anywhere()] * len(pieces),
        out_specs=[
            whole((rows, width)),
            whole((rows, width)),
            pl.BlockSpec(grad_block, lambda j: (j // 2, 0, 0, 0)),
            pl.BlockSpec(grad_block, lambda j: (jnp.maximum(j - 1, 0) // 2, 0, 0, 0)),
            whole((LANES, 1, units)),
        ],
        out_shape=[jax.ShapeDtypeStruct((rows, width), FULL)] * 2
        + [grads] * 2
        + [jax.ShapeDtypeStruct((LANES, 1, units), FULL)],
        scratch_shapes=[
            pltpu.VMEM((width, rows), LOW),
            pltpu.VMEM((width, rows), LOW),
            pltpu.VMEM((2, parts, width, sub), LOW),
            pltpu.VMEM((2, parts, width, sub), LOW),
            pltpu.VMEM((rows, units), LOW),
            pltpu.VMEM((rows, units), LOW),
            pltpu.SemaphoreType.DMA((2, 2, parts)),
        ],
        compiler_params=params(),
        cost_estimate=cost(3.5e10, 4e7),
    )(mine, normed, grad_down, unit_bias, *pieces)


def second_body(
    me_ref, down_ref, gn_ref, mid_ref, att_ref, ctx_ref, cot_ref, vec_ref, out_ref, gm_ref, ga_ref, keep_ref, send_ref, rows_ref, pad_s, out_s, sums_s, gat_s
):
    step = pl.program_id(0)

    @pl.when(step == 0)
    def _():
        pad_s[...] = jnp.zeros_like(pad_s)
        sums_s[...] = jnp.zeros_like(sums_s)

    cot = load_images(pad_s, cot_ref, step)
    down = down_ref[...] + vec_ref[6:7, :]
    mid = mid_ref[...]
    store_images(out_ref, out_s, mid + vec_ref[7:8, :] * down, step)
    scaled, inverse = normalise(mid)
    grad_normed = gn_ref[...]
    grad_mid = cot + norm_back(grad_normed, vec_ref[2:3, :], scaled, inverse)
    gm_ref[...] = grad_mid
    grad_att = (grad_mid * vec_ref[5:6, :]).astype(LOW)
    ga_ref[...] = grad_att
    gat_s[step] = grad_att.T
    sums_s[0] += fold(grad_normed * scaled)
    sums_s[1] += fold(grad_normed)
    sums_s[2] += fold(grad_mid)
    sums_s[3] += fold(grad_mid * att_ref[...].astype(FULL))
    sums_s[4] += fold(cot)
    sums_s[5] += fold(cot * down)

    @pl.when(step == pl.num_programs(0) - 1)
    def _():
        sums = [jnp.sum(sums_s[index], axis=0, keepdims=True) for index in range(6)]
        sums[2] = sums[2] * vec_ref[5:6, :]
        sums[4] = sums[4] * vec_ref[7:8, :]
        for index in range(6):
            rows_ref[index : index + 1, :] = sums[index]
        images = gat_s.shape[0]
        for group in range(LANES):
            at = slice(group * OUT_PACK, (group + 1) * OUT_PACK)
            grad = dot(gat_s[0], ctx_ref[0:PADDED, at])
            for image in range(1, images):
                grad = grad + dot(
                    gat_s[image], ctx_ref[image * PADDED : (image + 1) * PADDED, at]
                )
            give(me_ref[0], keep_ref, send_ref, group, grad.astype(LOW))


def give(place, keep_ref, send_ref, group, grad):
    rows = keep_ref.shape[2]
    mine = reversed_bits(place)
    target = (keep_ref, send_ref)[group % 2]
    for chunk in range(CHUNKS):
        target[group // 2, reversed_bits(chunk) ^ mine] = grad[chunk * rows : (chunk + 1) * rows]


def second_back(mine, down, grad_normed, mid, att, ctx, cot, vectors, images):
    rows, width = mid.shape
    block = lambda: pl.BlockSpec((PADDED, width), lambda i: (i, 0))
    grads = (2, CHUNKS, width // CHUNKS, OUT_PACK)
    return pl.pallas_call(
        second_body,
        grid=(images,),
        in_specs=[
            pl.BlockSpec(memory_space=pltpu.SMEM),
            block(),
            block(),
            block(),
            block(),
            whole(ctx.shape),
            whole(cot.shape),
            whole(vectors.shape),
        ],
        out_specs=[whole(cot.shape), block(), block(), whole(grads), whole(grads), whole((6, width))],
        out_shape=[
            jax.ShapeDtypeStruct(cot.shape, FULL),
            jax.ShapeDtypeStruct((rows, width), FULL),
            jax.ShapeDtypeStruct((rows, width), LOW),
            jax.ShapeDtypeStruct(grads, LOW),
            jax.ShapeDtypeStruct(grads, LOW),
            jax.ShapeDtypeStruct((6, width), FULL),
        ],
        scratch_shapes=[
            pltpu.VMEM((PADDED, width), FULL),
            pltpu.VMEM((PADDED, width), FULL),
            pltpu.VMEM((6, 8, width), FULL),
            pltpu.VMEM((images, width, PADDED), LOW),
        ],
        compiler_params=params(),
        cost_estimate=cost(1e10, 2e7),
    )(mine, down, grad_normed, mid, att, ctx, cot, vectors)


def back_body(table, columns, images, me_ref, ga_ref, qkv_ref, prob_ref, *refs):
    pieces = refs[:-6]
    dqkv_ref, pair_ref, cols_ref, weight_s, gc_s, sems = refs[-6:]
    step = pl.program_id(0)

    @pl.when(step == 0)
    def _():
        for group in range(LANES):
            fetch(group, table, pieces, columns, weight_s.at[group], sems.at[group], me_ref[0])

    fetched(weight_s.at[step], sems.at[step])
    gc_s[...] = dot(ga_ref[...], weight_s[step]).astype(LOW)
    lane = halves()

    def tile(image, index):
        return qkv_ref[0, image * PADDED : (image + 1) * PADDED, 128 * index : 128 * (index + 1)]

    def upstream(image, head):
        at = 128 if head == 2 else 0
        value = gc_s[image * PADDED : (image + 1) * PADDED, at : at + 128]
        return half_of(value, lane, V_ODD[head])

    def first(image, head):
        return dot(tile(image, V_TILE[head]), upstream(image, head), 1, 1)

    def second(grad_prob, image, head):
        soft = prob_ref[image, head].astype(FULL)
        weighted = soft * grad_prob
        inner = jnp.sum(weighted, axis=0, keepdims=True)
        grad_score = weighted - soft * inner
        if image == 0:
            pair_ref[head] = grad_score
        else:
            pair_ref[head] += grad_score
        return grad_score.astype(LOW)

    def third(low_score, image, head):
        odd = QK_ODD[head]
        return (
            dot(low_score, half_of(tile(image, K_TILE[head]), lane, odd), 0, 0) * HD**-0.5,
            dot(low_score, half_of(tile(image, Q_TILE[head]), lane, odd)),
            dot(prob_ref[image, head], upstream(image, head)),
        )

    work = [(image, head) for image in range(images) for head in range(HEADS_LANE)]
    probs, scores, grads = {}, {}, {}
    sums = [jnp.zeros((8, 128), FULL)] * 3
    for turn_index in range(len(work) + 2):
        if turn_index < len(work):
            probs[turn_index] = first(*work[turn_index])
        if 0 <= turn_index - 1 < len(work):
            scores[turn_index - 1] = second(probs.pop(turn_index - 1), *work[turn_index - 1])
        done = turn_index - 2
        if done < 0:
            continue
        image, head = work[done]
        grads[head] = third(scores.pop(done), image, head)
        if head < HEADS_LANE - 1:
            continue
        packed = (
            grads[0][0] + grads[1][0],
            grads[2][0] + grads[2][2],
            grads[0][2] + grads[1][2],
            grads[0][1] + grads[1][1],
            grads[2][1],
        )
        rows = slice(image * PADDED, (image + 1) * PADDED)
        for index, value in enumerate(packed):
            low_value = value.astype(LOW)
            dqkv_ref[0, rows, 128 * index : 128 * (index + 1)] = low_value
            if index < 3:
                sums[index] = sums[index] + fold(low_value.astype(FULL))
    for index in range(3):
        cols_ref[0, :, 128 * index : 128 * (index + 1)] = sums[index]


def back(mine, grad_att, qkv, prob, gathered, columns, images):
    rows, width = grad_att.shape
    heads = prob.shape[1]
    pieces, table = gathered
    return pl.pallas_call(
        functools.partial(back_body, table, columns, images),
        grid=(LANES,),
        in_specs=[
            pl.BlockSpec(memory_space=pltpu.SMEM),
            whole(grad_att.shape),
            pl.BlockSpec((1, rows, PACK), lambda g: (g, 0, 0)),
            pl.BlockSpec((images, HEADS_LANE, PADDED, PADDED), lambda g: (0, g, 0, 0)),
        ]
        + [anywhere()] * len(pieces),
        out_specs=[
            pl.BlockSpec((1, rows, PACK), lambda g: (g, 0, 0)),
            pl.BlockSpec((HEADS_LANE, PADDED, PADDED), lambda g: (g, 0, 0)),
            pl.BlockSpec((1, 8, 384), lambda g: (g, 0, 0)),
        ],
        out_shape=[
            jax.ShapeDtypeStruct((LANES, rows, PACK), LOW),
            jax.ShapeDtypeStruct((heads, PADDED, PADDED), FULL),
            jax.ShapeDtypeStruct((LANES, 8, 384), FULL),
        ],
        scratch_shapes=[
            pltpu.VMEM((LANES, width, OUT_PACK), LOW),
            pltpu.VMEM((rows, OUT_PACK), LOW),
            pltpu.SemaphoreType.DMA((LANES,)),
        ],
        compiler_params=params(),
        cost_estimate=cost(3e10, 4e7),
    )(mine, grad_att, qkv, prob, *pieces)


def heads_body(pair_ref, cols_ref, thin_ref, heads_ref, spread_s, flat_s):
    heads = pair_ref.shape[0]
    spread_s[...] = jnp.zeros_like(spread_s)

    def head_sum(index, carry):
        for row in range(GRID):
            at = GRID * (GRID - 1 - row)
            spread_s[index, :, at : at + PATCHES] += pair_ref[
                index, row * GRID : (row + 1) * GRID, 0:PATCHES
            ]
        return carry

    lax.fori_loop(0, heads, head_sum, 0)
    for col in range(GRID):
        flat_s[16 * col : 16 * (col + 1), :] = spread_s[:, col, :]
    wide = exact_dot(flat_s[...], thin_ref[...], 1)
    table = jnp.zeros((16, TABLE), FULL)
    for col in range(GRID):
        table = table + turn(wide[16 * col : 16 * (col + 1)], GRID - 1 - col)
    for group in range(LANES):
        cols = jnp.sum(cols_ref[group], axis=0, keepdims=True)
        for head in range(HEADS_LANE):
            at = HD * (4 + head if head < 2 else 3)
            heads_ref[group, head : head + 1, 0:HD] = cols[:, HD * head : HD * (head + 1)]
            heads_ref[group, head : head + 1, HD : 2 * HD] = cols[:, at : at + HD]
        first = group * HEADS_LANE
        heads_ref[group, :, 2 * HD :] = table[first : first + HEADS_LANE, 0 : SPAN * SPAN]


def heads_back(pair, cols, thin):
    heads = pair.shape[0]
    return pl.pallas_call(
        heads_body,
        out_shape=jax.ShapeDtypeStruct((LANES, HEADS_LANE, 2 * HD + SPAN * SPAN), FULL),
        scratch_shapes=[
            pltpu.VMEM((16, GRID, SPREAD), FULL),
            pltpu.VMEM((16 * GRID, SPREAD), FULL),
        ],
        compiler_params=params(),
        cost_estimate=cost(3e9, 4e6),
    )(pair, cols, thin)


def project_body(me_ref, n_ref, dqkv_ref, keep_ref, send_ref, t_s):
    t_s[...] = n_ref[...].T
    for group in range(LANES):
        give(me_ref[0], keep_ref, send_ref, group, dot(t_s[...], dqkv_ref[group]).astype(LOW))


def project(mine, normed, dqkv):
    rows, width = normed.shape
    grads = jax.ShapeDtypeStruct((2, CHUNKS, width // CHUNKS, PACK), LOW)
    return pl.pallas_call(
        project_body,
        in_specs=[pl.BlockSpec(memory_space=pltpu.SMEM)] + [pl.BlockSpec(memory_space=pltpu.VMEM)] * 2,
        out_shape=[grads, grads],
        scratch_shapes=[pltpu.VMEM((width, rows), LOW)],
        compiler_params=params(),
        cost_estimate=cost(8e9, 1e7),
    )(mine, normed, dqkv)


def input_body(table, me_ref, dqkv_ref, gm_ref, x_ref, vec_ref, *refs):
    pieces = refs[:-7]
    out_ref, rows_ref, weight_s, pad_s, out_s, sums_s, sems = refs[-7:]
    step = pl.program_id(0)

    @pl.when(step == 0)
    def _():
        for group in range(LANES):
            fetch(group, table, pieces, (0, PACK), weight_s.at[group], sems.at[group], me_ref[0])
        pad_s[...] = jnp.zeros_like(pad_s)
        sums_s[...] = jnp.zeros_like(sums_s)
        for group in range(LANES):
            fetched(weight_s.at[group], sems.at[group])

    scaled, inverse = normalise(load_images(pad_s, x_ref, step))
    grad = dot(dqkv_ref[0], weight_s[0], 1, 1)
    for group in range(1, LANES):
        grad = grad + dot(dqkv_ref[group], weight_s[group], 1, 1)
    sums_s[0] += fold(grad * scaled)
    sums_s[1] += fold(grad)
    for index in range(2):
        rows_ref[index : index + 1, :] = jnp.sum(sums_s[index], axis=0, keepdims=True)
    result = gm_ref[...] + norm_back(grad, vec_ref[0:1, :], scaled, inverse)
    store_images(out_ref, out_s, result, step)


def input_back(mine, dqkv, grad_mid, x, vectors, gathered, images):
    width = x.shape[1]
    pieces, table = gathered
    return pl.pallas_call(
        functools.partial(input_body, table),
        grid=(images // TWO,),
        in_specs=[
            pl.BlockSpec(memory_space=pltpu.SMEM),
            pl.BlockSpec((LANES, TWO * PADDED, PACK), lambda i: (0, i, 0)),
            pl.BlockSpec((TWO * PADDED, width), lambda i: (i, 0)),
            whole(x.shape),
            whole(vectors.shape),
        ]
        + [anywhere()] * len(pieces),
        out_specs=[whole(x.shape), whole((2, width))],
        out_shape=[jax.ShapeDtypeStruct(x.shape, FULL), jax.ShapeDtypeStruct((2, width), FULL)],
        scratch_shapes=[
            pltpu.VMEM((LANES, width, PACK), LOW),
            pltpu.VMEM((TWO * PADDED, width), FULL),
            pltpu.VMEM((TWO * PADDED, width), FULL),
            pltpu.VMEM((2, 8, width), FULL),
            pltpu.SemaphoreType.DMA((LANES,)),
        ],
        compiler_params=params(),
        cost_estimate=cost(1.5e10, 1.5e7),
    )(mine, dqkv, grad_mid, x, vectors, *pieces)


def swap(values, axis, bit):
    count = lax.axis_size(axis)
    return lax.ppermute(values, axis, [(index, index ^ bit) for index in range(count)])


def after(values, *others):
    return lax.optimization_barrier((values,) + others)[0]


def sync(*values):
    return lax.optimization_barrier(values)


def join(former, latter, axis=0):
    return jnp.concatenate([former, latter], axis=axis)


def split_rows(held):
    half = held.shape[1] // 2
    return held[:, :half], held[:, half:]


def pieces_of(upper, upper_x, lower, lower_y, near_core, far_core):
    arrays = [upper, upper_x, lower, lower_y, near_core[0], far_core[0], near_core[1], far_core[1]]
    half = upper.shape[1]

    def part(first, far):
        top = [(first + far, slot) for slot in range(8)]
        low = [(first + 2 + slot // 4, 4 * far + slot % 4) for slot in range(8)]
        return ((0, top), (half, low))

    return arrays, (part(0, 0), part(4, 0), part(0, 1), part(4, 1))


def total_of(terms):
    total = terms[0].astype(FULL)
    for one in terms[1:]:
        total = total + one.astype(FULL)
    return total


def sum_call(body, grid, views, outs, moved):
    return pl.pallas_call(
        body,
        grid=(grid,),
        in_specs=[pl.BlockSpec(block, index) for _, block, index in views],
        out_specs=[pl.BlockSpec(block, index) for _, _, block, index in outs],
        out_shape=[jax.ShapeDtypeStruct(shape, dtype) for shape, dtype, _, _ in outs],
        compiler_params=params(),
        cost_estimate=cost(1e6, moved),
    )(*[array for array, _, _ in views])


def sum_away(keeps, gots):
    half = keeps[0].shape[2] // 2
    wide = sum(keep.shape[3] for keep in keeps)
    views = []
    for keep, got in zip(keeps, gots):
        block = (1, 2, half, keep.shape[3])
        for array in (keep, got):
            views.append((array, block, lambda j: (1, j, 0, 0)))
            views.append((array, block, lambda j: (j // 2, 2 + j % 2, 1, 0)))

    def body(*refs):
        ins, (upper, lower) = refs[:-2], refs[-2:]
        first = 0
        for index in range(0, len(ins), 4):
            keep_u, keep_l, got_u, got_l = ins[index : index + 4]
            at = slice(first, first + keep_u.shape[3])
            first = at.stop
            upper[:, :, at] = total_of((keep_u[0], got_u[0])).astype(LOW)
            lower[0, :, :, at] = total_of((keep_l[0], got_l[0])).astype(LOW)

    outs = [
        ((8, half, wide), LOW, (2, half, wide), lambda j: (j, 0, 0)),
        ((2, 4, half, wide), LOW, (1, 2, half, wide), lambda j: (j // 2, j % 2, 0, 0)),
    ]
    return sum_call(body, 4, views, outs, 8e6)


def sum_here(keeps, gots, upper_got, lower_got):
    half = keeps[0].shape[2] // 2
    wide = sum(keep.shape[3] for keep in keeps)
    places = (
        lambda j: (0, j, 0, 0),
        lambda j: (0, 4 + j, 0, 0),
        lambda j: (0, j, 1, 0),
        lambda j: (1, j, 1, 0),
    )
    views = [
        (upper_got, (1, half, wide), lambda j: (j, 0, 0)),
        (upper_got, (1, half, wide), lambda j: (4 + j, 0, 0)),
        (lower_got, (1, 1, half, wide), lambda j: (0, j, 0, 0)),
        (lower_got, (1, 1, half, wide), lambda j: (1, j, 0, 0)),
    ]
    for keep, got in zip(keeps, gots):
        for array in (keep, got):
            views.extend((array, (1, 1, half, keep.shape[3]), place) for place in places)

    def body(*refs):
        far, ins, outs = refs[:4], refs[4:-4], refs[-4:]
        first = 0
        for index in range(0, len(ins), 8):
            at = slice(first, first + ins[index].shape[3])
            first = at.stop
            for view in range(4):
                came = far[view][0, :, at] if view < 2 else far[view][0, 0, :, at]
                terms = (ins[index + view][0, 0], ins[index + 4 + view][0, 0], came)
                outs[view][0, :, at] = total_of(terms).astype(outs[view].dtype)

    outs = [
        ((4, half, wide), dtype, (1, half, wide), lambda j: (j, 0, 0))
        for dtype in (FULL, LOW, FULL, LOW)
    ]
    return sum_call(body, 4, views, outs, 1.2e7)


def sum_line(upper, upper_got, lower, lower_got):
    half, wide = upper.shape[1:]
    views = []
    for array in (upper, upper_got, lower, lower_got):
        views.append((array, (1, half, wide), lambda j: (j, 0, 0)))
        views.append((array, (1, half, wide), lambda j: (2 + j, 0, 0)))

    def body(*refs):
        for side in range(2):
            out = refs[8 + side]
            out[0, :half] = total_of((refs[side][0], refs[2 + side][0])).astype(out.dtype)
            out[0, half:] = total_of((refs[4 + side][0], refs[6 + side][0])).astype(out.dtype)

    outs = [
        ((2, 2 * half, wide), dtype, (1, 2 * half, wide), lambda j: (j, 0, 0))
        for dtype in (FULL, LOW)
    ]
    return sum_call(body, 2, views, outs, 6e6)


def adam(weight, moment_one, moment_two, incoming, step_rate, decay_rate):
    first_new = BETA_ONE * moment_one + (1.0 - BETA_ONE) * incoming
    second_new = BETA_TWO * moment_two + (1.0 - BETA_TWO) * incoming * incoming
    update = (
        first_new
        / (1.0 - BETA_ONE**STEP)
        / (jnp.sqrt(second_new / (1.0 - BETA_TWO**STEP)) + ADAM_EPSILON)
    )
    return (second_new, weight * (1.0 - step_rate * decay_rate) - step_rate * update)


def pack_attention(weights):
    query, key, value, out = (weights[index] for index in range(4))
    rows = query.shape[0]
    blank = jnp.zeros((rows, HD), weights.dtype)
    first = jnp.concatenate([query, value[:, 128:], value[:, :128], key, blank], axis=1)
    last = jnp.concatenate([out[:, :128], blank, out[:, 128:]], axis=1)
    return first, last


def unpack_attention(first, last):
    query = first[:, :192]
    value = jnp.concatenate([first[:, 256:384], first[:, 192:256]], axis=1)
    key = first[:, 384:576]
    out = jnp.concatenate([last[:, :128], last[:, 192:]], axis=1)
    return jnp.stack([query, key, value, out])


def shards(
    block_input,
    cotangent,
    image_size,
    attention_weights,
    attention_first,
    attention_second,
    mlp_weights,
    mlp_first,
    mlp_second,
    head_params,
    head_first,
    head_second,
    norm_params,
    norm_first,
    norm_second,
):
    near = lax.axis_size("dp") == CHUNKS
    lane_index = lax.axis_index("mp")
    local_rows, width = block_input.shape
    images = local_rows // PATCHES
    local_heads = head_params.shape[0]
    chunk_rows = width // CHUNKS
    thin = jnp.asarray(thin_matrix(), LOW)

    first, last = pack_attention(attention_weights.astype(LOW))
    mlp_low = mlp_weights.astype(LOW)
    units = mlp_low.shape[2]
    part = units // 2
    unit_bias = norm_params[8:].reshape(LANES, 1, units)
    second = jnp.concatenate([last, mlp_low[0, :, :part], mlp_low[1, :, :part]], axis=1)
    third = jnp.concatenate([mlp_low[0, :, part:], mlp_low[1, :, part:]], axis=1)
    if near:
        mine = jnp.stack([lax.axis_index("dp"), lane_index, lane_index]).astype(jnp.int32)
        core = lambda values: swap(values, "mp", 1)
        x_axis = lambda values: swap(values, "mp", 2)
        y_axis = lambda values: swap(values, "dp", 1)
        z_near = lambda values: swap(values, "dp", 2)
        z_far = lambda values: swap(values, "dp", 4)
        one, two, three = first[None], second[None], third[None]
        got = z_far(one)
        normed_one, grad_down = first_norm(block_input, cotangent, norm_params, images)
        got, normed_one = sync(got, normed_one)
        one = join(one, got)
        got = z_near(one)
        two_got = z_far(after(two, one))
        other = x_axis(after(head_params, one))
        near_table, far_table = core(head_params), core(other)
        upper, lower = split_rows(join(one, got))
        upper, lower = sync(upper, lower)
        upper_got, lower_got = y_axis(upper), x_axis(lower)
        two = join(two, after(two_got, upper, lower))
        two_got = z_near(two)
        bias, add = spread_bias(
            (head_params, after(near_table, two), other, after(far_table, two)), thin
        )
        upper_got, lower_got, bias = sync(upper_got, lower_got, bias)
        upper, lower = sync(join(upper, upper_got), join(lower, lower_got))
        upper_far, lower_far = x_axis(upper), y_axis(lower)
        near_core = sync(core(upper), core(lower))
        two_upper, two_lower = split_rows(join(two, after(two_got, upper, lower)))
        two_upper, two_lower, three = sync(two_upper, two_lower, after(three, *near_core))
        two_upper_got, two_lower_got = y_axis(two_upper), x_axis(two_lower)
        three_got = z_far(three)
        upper_far, lower_far, two_upper_got, two_lower_got, three_got = sync(
            upper_far, lower_far, two_upper_got, two_lower_got, three_got
        )
        far_core = sync(core(upper_far), core(lower_far))
        three = join(three, three_got)
        first_all = pieces_of(upper, upper_far, lower, lower_far, near_core, far_core)
        two_upper, two_lower = join(two_upper, two_upper_got), join(two_lower, two_lower_got)
        two_upper, two_lower, three, normed_one = sync(two_upper, two_lower, three, normed_one)
        two_upper_far, two_lower_far = x_axis(two_upper), y_axis(two_lower)
        three_got = z_near(three)
    else:
        mine = jnp.stack([0 * lane_index, 0 * lane_index, lane_index]).astype(jnp.int32)

        def gather_far(piece):
            full = lax.all_gather(piece, "dp", axis=0, tiled=True)
            full = lax.all_gather(full, "mp", axis=0, tiled=False)
            full = full.reshape(LANES, CHUNKS, chunk_rows, piece.shape[1])
            order = [reversed_bits(index) for index in range(CHUNKS)]
            full = jnp.stack([full[:, index] for index in order], axis=1)
            slots = range(CHUNKS)
            table = tuple(((0, [(group, slot) for slot in slots]),) for group in range(LANES))
            return [full[index] for index in range(LANES)], table

        tables = lax.all_gather(head_params, "mp", axis=0, tiled=False)
        tables = tuple(tables[index] for index in range(LANES))
        normed_one, grad_down = first_norm(block_input, cotangent, norm_params, images)
        bias, add = spread_bias(tables, thin)
        first_all = gather_far(first)
        second_all = gather_far(second)
        third_all = gather_far(third)

    qkv, prob, ctx = attend(mine, image_size, normed_one, bias, add, first_all, images)
    if near:
        ctx, three_got, two_upper_far, two_lower_far = sync(
            ctx, three_got, two_upper_far, two_lower_far
        )
        three_upper, three_lower, two_upper, two_lower = sync(
            *split_rows(join(three, three_got)), two_upper, two_lower
        )
        three_upper_got, three_lower_got = y_axis(three_upper), x_axis(three_lower)
        two_near = sync(core(two_upper), core(two_lower))
        two_far = (core(after(two_upper_far, *two_near)), core(after(two_lower_far, *two_near)))
        two_near, two_far, three_upper_got, three_lower_got = sync(
            two_near, two_far, three_upper_got, three_lower_got
        )
        second_all = pieces_of(two_upper, two_upper_far, two_lower, two_lower_far, two_near, two_far)
        three_upper, three_lower, ctx = sync(
            join(three_upper, three_upper_got), join(three_lower, three_lower_got), ctx
        )
        three_upper_far, three_lower_far = x_axis(three_upper), y_axis(three_lower)
        three_near = (core(three_upper), core(three_lower))
    att, mid, normed_two = middle(
        mine, ctx, block_input, norm_params, second_all, (0, OUT_PACK), images
    )
    if near:
        normed_two, three_upper_far, three_lower_far, three_near = sync(
            normed_two, three_upper_far, three_lower_far, three_near
        )
        three_far = (core(three_upper_far), core(three_lower_far))
        third_all = pieces_of(
            three_upper, three_upper_far, three_lower, three_lower_far, three_near, three_far
        )
    groups = ((second_all, OUT_PACK, OUT_PACK + part), (third_all, 0, part))
    down, grad_normed, keep_mlp, send_mlp, unit_sums = feed(
        mine, normed_two, grad_down, unit_bias, groups, units, images
    )
    if near:
        mlp_core = core(send_mlp)
    output, grad_mid, grad_att, keep_out, send_out, second_rows = second_back(
        mine, down, grad_normed, mid, att, ctx, cotangent, norm_params, images
    )
    if near:
        mlp_core, grad_att, send_out = sync(mlp_core, grad_att, send_out)
        keeps, gots = (keep_mlp, keep_out), (mlp_core, core(send_out))
        upper, lower, grad_att = sync(*sum_away(keeps, gots), grad_att)
        upper_got, lower_got = x_axis(upper), y_axis(lower)
    dqkv, pair, cols = back(
        mine, grad_att, qkv, prob, second_all, (0, OUT_PACK), images
    )
    keep_att, send_att = project(mine, normed_one, dqkv)
    if near:
        keep_att, send_att, upper_got, lower_got = sync(keep_att, send_att, upper_got, lower_got)
        att_core = core(send_att)
        upper, upper_away, lower, lower_away = sum_here(keeps, gots, upper_got, lower_got)
        upper_away, lower_away, att_core, pair = sync(upper_away, lower_away, att_core, pair)
        upper_got, lower_got = y_axis(upper_away), x_axis(lower_away)
        keeps, gots = (keep_att,), (att_core,)
        att_upper, att_lower, pair = sync(*sum_away(keeps, gots), pair)
        att_upper_got, att_lower_got = x_axis(att_upper), y_axis(att_lower)
    grad_heads = heads_back(pair, cols, thin)
    if near:
        upper_got, lower_got, grad_heads = sync(upper_got, lower_got, grad_heads)
        line, line_away = sum_line(upper, upper_got, lower, lower_got)
        line_away, dqkv = sync(line_away, dqkv)
        line_got = z_near(line_away)
        upper_got, lower_got = att_upper_got, att_lower_got
    grad_input, first_rows = input_back(
        mine, dqkv, grad_mid, block_input, norm_params, first_all, images
    )

    norms = jnp.concatenate([first_rows, second_rows, unit_sums.reshape(-1, width)], axis=0)
    if near:
        norms, upper_got, lower_got = sync(norms, upper_got, lower_got)
        upper, upper_away, lower, lower_away = sum_here(keeps, gots, upper_got, lower_got)
        upper_away, lower_away, norms, line_got = sync(upper_away, lower_away, norms, line_got)
        upper_got, lower_got = y_axis(upper_away), x_axis(lower_away)
        heads_width = grad_heads.shape[2]
        count = norms.shape[0]
        norms = jnp.pad(norms, ((0, 0), (0, heads_width - width)))
        packs = [join(norms, grad_heads[index]) for index in range(LANES)]
        small = (packs[0] + core(packs[1])) + (x_axis(packs[2]) + swap(packs[3], "mp", 3))
        small, upper_got, lower_got = sync(small, upper_got, lower_got)
        here, away = sum_line(upper, upper_got, lower, lower_got)
        small, here, away = sync(small, here, away)
        got = z_near(away)
        small_got = y_axis(small)
        line = line + line_got.astype(FULL)
        line_got = z_far(line[1].astype(LOW))
        got, small_got = sync(got, small_got)
        here = here + got.astype(FULL)
        small = small + small_got
        away, small = sync(here[1].astype(LOW), small)
        got = z_far(away)
        small = (small + z_near(small)) + (z_far(small) + swap(small, "dp", 6))
        sum_mlp = line[0] + line_got.astype(FULL)
        sum_att = here[0] + got.astype(FULL)
        sum_mlp, sum_out = sum_mlp[:, : 2 * units], sum_mlp[:, 2 * units :]
        reduced_norms = small[:count, :width]
        reduced_heads = small[count:]
    else:
        reduced_norms = lax.psum(norms, ("dp", "mp"))
        reduced_heads = lax.psum_scatter(
            lax.psum(grad_heads, "dp"), "mp", scatter_dimension=0, tiled=False
        )

        def scatter_far(keep, send):
            terms = jnp.stack([keep[0], send[0], keep[1], send[1]])
            order = [reversed_bits(index) for index in range(CHUNKS)]
            terms = jnp.stack([terms[:, index] for index in order], axis=1)
            terms = terms.reshape(LANES, width, terms.shape[-1])
            mine_only = lax.psum_scatter(terms, "mp", scatter_dimension=0, tiled=False)
            return lax.psum_scatter(
                mine_only.astype(FULL), "dp", scatter_dimension=0, tiled=True
            )

        sum_mlp = scatter_far(keep_mlp, send_mlp)
        sum_out = scatter_far(keep_out, send_out)
        sum_att = scatter_far(keep_att, send_att)

    reduced_attention = unpack_attention(sum_att, sum_out)
    reduced_mlp = jnp.stack([sum_mlp[:, :units], sum_mlp[:, units:]])
    attention_second_new, attention_new = adam(
        attention_weights,
        attention_first,
        attention_second,
        reduced_attention,
        RATE_MATRIX,
        DECAY_MATRIX,
    )
    mlp_second_new, mlp_new = adam(
        mlp_weights, mlp_first, mlp_second, reduced_mlp, RATE_MATRIX, DECAY_MATRIX
    )
    head_second_new, head_new = adam(
        head_params, head_first, head_second, reduced_heads, RATE_VECTOR, 0.0
    )
    norm_second_new, norm_new = adam(
        norm_params, norm_first, norm_second, reduced_norms, RATE_VECTOR, 0.0
    )
    return (
        output,
        grad_input,
        reduced_attention,
        attention_second_new,
        attention_new,
        reduced_mlp,
        mlp_second_new,
        mlp_new,
        reduced_heads,
        head_second_new,
        head_new,
        reduced_norms,
        norm_second_new,
        norm_new,
    )


def solution(mesh):
    rows = P(("dp", "mp"), None)
    matrix = P(None, "dp", "mp")
    head = P("mp", None)
    placed = (rows, rows, P("dp", None)) + (matrix,) * 6 + (head,) * 3 + (P(),) * 3
    given = (rows, rows) + (matrix,) * 6 + (head,) * 3 + (P(),) * 3
    return jax.shard_map(shards, mesh=mesh, in_specs=placed, out_specs=given, check_vma=False)
```

```python
import functools

import jax
import jax.numpy as jnp
import numpy as np
from jax import lax
from jax.experimental import pallas as pl
from jax.experimental.pallas import tpu as pltpu
from jax.sharding import PartitionSpec as P

HD = 64
GRID = 14
SPAN = 2 * GRID - 1
STEP = 10
PATCHES = 196
PADDED = 208
PACK = 640
OUT_PACK = 256
CHUNKS = 8
LANES = 4
HEADS_LANE = 3
TWO = 2
TABLE = 768
SPREAD = 384

EPSILON = 1e-06
NEGATIVE = -1e30
BETA_ONE = 0.9
BETA_TWO = 0.999
ADAM_EPSILON = 1e-08
RATE_MATRIX = 0.05
RATE_VECTOR = 0.4
DECAY_MATRIX = 0.05

LOW = jnp.bfloat16
FULL = jnp.float32
INV_SQRT2 = 0.7071067811865476
INV_SQRT2PI = 0.3989422804014327
VMEM_LIMIT = 60 << 20


def dot(former, latter, former_dim=1, latter_dim=0):
    return lax.dot_general(
        former,
        latter,
        (((former_dim,), (latter_dim,)), ((), ())),
        preferred_element_type=FULL,
    )


def normalise(values):
    row_mean = jnp.mean(values, axis=-1, keepdims=True)
    centre = values - row_mean
    variance = jnp.mean(centre * centre, axis=-1, keepdims=True)
    inverse = lax.rsqrt(variance + EPSILON)
    return centre * inverse, inverse


def norm_back(incoming, norm_gain, scaled, inverse):
    weighted = incoming * norm_gain
    centred = weighted - jnp.mean(weighted, axis=-1, keepdims=True)
    return inverse * (centred - scaled * jnp.mean(weighted * scaled, axis=-1, keepdims=True))


def fold(values):
    rows, cols = values.shape
    return jnp.sum(values.reshape(rows // 8, 8, cols), axis=0)


def reversed_bits(index):
    return (index & 1) * 4 + (index & 2) + (index & 4) // 4


def whole(shape):
    zeros = (0,) * len(shape)
    return pl.BlockSpec(tuple(shape), lambda *_: zeros)


def params():
    return pltpu.CompilerParams(vmem_limit_bytes=VMEM_LIMIT)


def cost(flops, moved):
    return pl.CostEstimate(flops=int(flops), bytes_accessed=int(moved), transcendentals=0)


def fetch(group, table, refs, columns, target, sem, place):
    for rows, part in table[group]:
        for slot, (source, lead) in enumerate(part):
            height = refs[source].shape[1]
            chunk = target.shape[0] // CHUNKS
            start = (reversed_bits(slot) ^ place) * chunk + rows
            pltpu.make_async_copy(
                refs[source].at[lead, :, columns[0] : columns[1]],
                target.at[pl.ds(pl.multiple_of(start, 16), height), :],
                sem,
            ).start()


def fetched(target, sem):
    pltpu.make_async_copy(target, target, sem).wait()


def anywhere():
    return pl.BlockSpec(memory_space=pl.ANY)


def load_images(pad, source, step):
    count = pad.shape[0] // PADDED
    for first in range(0, source.shape[0] // PATCHES, count):

        @pl.when(step == first // count)
        def _(first=first):
            for index in range(count):
                at = (first + index) * PATCHES
                pad[index * PADDED : index * PADDED + PATCHES, :] = source[at : at + PATCHES, :]

    return pad[...]


def store_images(target, pad, value, step):
    count = pad.shape[0] // PADDED
    pad[...] = value
    for first in range(0, target.shape[0] // PATCHES, count):

        @pl.when(step == first // count)
        def _(first=first):
            for index in range(count):
                at = (first + index) * PATCHES
                target[at : at + PATCHES, :] = pad[index * PADDED : index * PADDED + PATCHES, :]


def first_norm_body(images, x_ref, cot_ref, vec_ref, normed_ref, gd_ref, pad_s):
    pad_s[...] = jnp.zeros_like(pad_s)
    for image in range(images):
        rows = slice(image * PATCHES, (image + 1) * PATCHES)
        target = slice(image * PADDED, (image + 1) * PADDED)
        scaled, _ = normalise(x_ref[rows, :])
        pad_s[0:PATCHES, :] = scaled * vec_ref[0:1, :] + vec_ref[1:2, :]
        normed_ref[target, :] = pad_s[...].astype(LOW)
        pad_s[0:PATCHES, :] = cot_ref[rows, :] * vec_ref[7:8, :]
        gd_ref[target, :] = pad_s[...].astype(LOW)


def first_norm(x, cot, vectors, images):
    width = x.shape[1]
    return pl.pallas_call(
        functools.partial(first_norm_body, images),
        out_shape=[jax.ShapeDtypeStruct((images * PADDED, width), LOW)] * 2,
        scratch_shapes=[pltpu.VMEM((PADDED, width), FULL)],
        compiler_params=params(),
        cost_estimate=cost(3e9, 4e6),
    )(x, cot, vectors)


def thin_matrix():
    matrix = np.zeros((TABLE, SPREAD), np.float32)
    for row in range(SPAN):
        for col in range(GRID):
            matrix[row * SPAN + col, row * GRID + col] = 1.0
    return matrix


def exact_dot(values, onehot, latter_dim=0):
    high = values.astype(LOW)
    rest = values - high.astype(FULL)
    mid = rest.astype(LOW)
    low = (rest - mid.astype(FULL)).astype(LOW)
    return (
        dot(high, onehot, 1, latter_dim)
        + dot(mid, onehot, 1, latter_dim)
        + dot(low, onehot, 1, latter_dim)
    )


def turn(values, shift):
    return pltpu.roll(values, shift % values.shape[1], 1)


def bias_body(t0, t1, t2, t3, thin_ref, bias_ref, add_ref, table_s, turned_s, spread_s):
    table_s[...] = jnp.zeros_like(table_s)
    for group, table in enumerate((t0, t1, t2, t3)):
        heads = slice(group * HEADS_LANE, (group + 1) * HEADS_LANE)
        table_s[heads, 0 : SPAN * SPAN] = table[:, 2 * HD :]
        rows = [table[head : head + 1, :HD] for head in range(HEADS_LANE)]
        more = [table[head : head + 1, HD : 2 * HD] for head in range(HEADS_LANE)]
        add_ref[group] = jnp.concatenate(
            rows + [more[2], more[0], more[1], jnp.zeros((1, PACK - 384), FULL)], axis=1
        )
    table = table_s[...]
    for col in range(GRID):
        turned_s[16 * col : 16 * (col + 1), :] = turn(table, col - (GRID - 1))
    spread = exact_dot(turned_s[...], thin_ref[...])
    for col in range(GRID):
        spread_s[:, col, :] = spread[16 * col : 16 * (col + 1)]

    def head(index, carry):
        bias_ref[index] = jnp.zeros(bias_ref.shape[1:], FULL)
        for row in range(GRID):
            start = GRID * (GRID - 1 - row)
            bias_ref[index, row * GRID : (row + 1) * GRID, 0:PATCHES] = spread_s[
                index, :, start : start + PATCHES
            ]
        return carry

    lax.fori_loop(0, bias_ref.shape[0], head, 0)


def spread_bias(tables, thin):
    heads = LANES * HEADS_LANE
    return pl.pallas_call(
        bias_body,
        out_shape=[
            jax.ShapeDtypeStruct((heads, PADDED, PADDED), FULL),
            jax.ShapeDtypeStruct((LANES, 1, PACK), FULL),
        ],
        scratch_shapes=[
            pltpu.VMEM((16, TABLE), FULL),
            pltpu.VMEM((16 * GRID, TABLE), FULL),
            pltpu.VMEM((16, GRID, SPREAD), FULL),
        ],
        compiler_params=params(),
        cost_estimate=cost(3e9, 4e6),
    )(*tables, thin)


Q_TILE = (0, 0, 1)
K_TILE = (3, 3, 4)
V_TILE = (2, 2, 1)
QK_ODD = (False, True, False)
V_ODD = (False, True, True)


def grid_places():
    position = np.arange(PADDED)
    row = np.where(position < PATCHES, position // GRID, 4 * GRID)
    places = np.stack([row, position % GRID]).astype(np.int32)
    return np.broadcast_to(places[:, :, None], (2, PADDED, 128)).copy()


def halves():
    lane = lax.broadcasted_iota(jnp.int32, (PADDED, 128), 1)
    return lane


def half_of(value, lane, odd):
    keep = lane >= HD if odd else lane < HD
    return jnp.where(keep, value, jnp.zeros_like(value))


def attend_body(table, images, me_ref, size_ref, grid_ref, n_ref, bias_ref, add_ref, *refs):
    pieces = refs[:-5]
    qkv_ref, prob_ref, ctx_ref, weight_s, sems = refs[-5:]
    step = pl.program_id(0)

    @pl.when(step == 0)
    def _():
        for group in range(LANES):
            fetch(group, table, pieces, (0, PACK), weight_s.at[group], sems.at[group], me_ref[0])

    fetched(weight_s.at[step], sems.at[step])
    scale = jnp.where(
        lax.broadcasted_iota(jnp.int32, (1, PACK), 1) < HEADS_LANE * HD, HD**-0.5, 1.0
    )
    acc = dot(n_ref[...], weight_s[step])
    qkv_ref[0] = ((acc + add_ref[0]) * scale).astype(LOW)

    lane = halves()
    masks = []
    for image in range(images):
        index = me_ref[2] * images + image
        inside = (grid_ref[0] < size_ref[index, 0]) & (grid_ref[1] < size_ref[index, 1])
        masks.append(jnp.where(inside, 0.0, NEGATIVE).astype(LOW))
    zero = jnp.zeros_like(masks[0])
    one = jnp.ones_like(masks[0])

    def tile(image, index):
        return qkv_ref[0, image * PADDED : (image + 1) * PADDED, 128 * index : 128 * (index + 1)]

    def score(image, head):
        odd = QK_ODD[head]
        mark = 0 if odd else HD
        keep = lane >= HD if odd else lane < HD
        key = jnp.where(
            keep, tile(image, K_TILE[head]), jnp.where(lane == mark, masks[image], zero)
        )
        query = jnp.where(lane == mark, one, tile(image, Q_TILE[head]))
        return dot(key, query, 1, 1) + bias_ref[head]

    def soften(scores, image, head):
        top = jnp.max(scores, axis=0, keepdims=True)
        exponent = jnp.exp(scores - top)
        total = jnp.sum(exponent, axis=0, keepdims=True)
        prob = (exponent * (1.0 / total)).astype(LOW)
        prob_ref[image, head] = prob
        return prob

    def gather(prob, image, head):
        return dot(prob, half_of(tile(image, V_TILE[head]), lane, V_ODD[head]), 0, 0)

    work = [(image, head) for image in range(images) for head in range(HEADS_LANE)]
    scores, probs, outs = {}, {}, {}
    for turn_index in range(len(work) + 2):
        if turn_index < len(work):
            scores[turn_index] = score(*work[turn_index])
        if 0 <= turn_index - 1 < len(work):
            probs[turn_index - 1] = soften(scores.pop(turn_index - 1), *work[turn_index - 1])
        done = turn_index - 2
        if done >= 0:
            image, head = work[done]
            outs[head] = gather(probs.pop(done), image, head)
            if head == HEADS_LANE - 1:
                rows = slice(image * PADDED, (image + 1) * PADDED)
                ctx_ref[rows, :128] = (outs[0] + outs[1]).astype(LOW)
                ctx_ref[rows, 128:] = outs[2].astype(LOW)


def attend(mine, sizes, normed, bias, add, gathered, images):
    rows, width = normed.shape
    heads = bias.shape[0]
    pieces, table = gathered
    return pl.pallas_call(
        functools.partial(attend_body, table, images),
        grid=(LANES,),
        in_specs=[
            pl.BlockSpec(memory_space=pltpu.SMEM),
            pl.BlockSpec(memory_space=pltpu.SMEM),
            whole((2, PADDED, 128)),
            whole(normed.shape),
            pl.BlockSpec((HEADS_LANE, PADDED, PADDED), lambda g: (g, 0, 0)),
            pl.BlockSpec((1, 1, PACK), lambda g: (g, 0, 0)),
        ]
        + [anywhere()] * len(pieces),
        out_specs=[
            pl.BlockSpec((1, rows, PACK), lambda g: (g, 0, 0)),
            pl.BlockSpec((images, HEADS_LANE, PADDED, PADDED), lambda g: (0, g, 0, 0)),
            pl.BlockSpec((rows, OUT_PACK), lambda g: (0, g)),
        ],
        out_shape=[
            jax.ShapeDtypeStruct((LANES, rows, PACK), LOW),
            jax.ShapeDtypeStruct((images, heads, PADDED, PADDED), LOW),
            jax.ShapeDtypeStruct((rows, LANES * OUT_PACK), LOW),
        ],
        scratch_shapes=[
            pltpu.VMEM((LANES, width, PACK), LOW),
            pltpu.SemaphoreType.DMA((LANES,)),
        ],
        compiler_params=params(),
        cost_estimate=cost(1.5e10, 2e7),
    )(mine, sizes, jnp.asarray(grid_places()), normed, bias, add, *pieces)


def middle_body(table, columns, me_ref, ctx_ref, x_ref, vec_ref, *refs):
    pieces = refs[:-6]
    att_ref, mid_ref, n_ref, weight_s, pad_s, sems = refs[-6:]
    step = pl.program_id(0)

    @pl.when(step == 0)
    def _():
        for group in range(LANES):
            fetch(group, table, pieces, columns, weight_s.at[group], sems.at[group], me_ref[0])
        for group in range(LANES):
            fetched(weight_s.at[group], sems.at[group])
        pad_s[...] = jnp.zeros_like(pad_s)

    total = vec_ref[4:5, :]
    for group in range(LANES):
        total = total + dot(
            ctx_ref[:, group * OUT_PACK : (group + 1) * OUT_PACK], weight_s[group], 1, 1
        )
    att_ref[...] = total.astype(LOW)
    mid = load_images(pad_s, x_ref, step) + vec_ref[5:6, :] * total
    mid_ref[...] = mid
    scaled, _ = normalise(mid)
    n_ref[...] = (scaled * vec_ref[2:3, :] + vec_ref[3:4, :]).astype(LOW)


def middle(mine, ctx, x, vectors, gathered, columns, images):
    rows = images * PADDED
    width = x.shape[1]
    pieces, table = gathered
    block = lambda: pl.BlockSpec((TWO * PADDED, width), lambda i: (i, 0))
    return pl.pallas_call(
        functools.partial(middle_body, table, columns),
        grid=(images // TWO,),
        in_specs=[
            pl.BlockSpec(memory_space=pltpu.SMEM),
            pl.BlockSpec((TWO * PADDED, LANES * OUT_PACK), lambda i: (i, 0)),
            whole(x.shape),
            whole(vectors.shape),
        ]
        + [anywhere()] * len(pieces),
        out_specs=[block(), block(), block()],
        out_shape=[
            jax.ShapeDtypeStruct((rows, width), LOW),
            jax.ShapeDtypeStruct((rows, width), FULL),
            jax.ShapeDtypeStruct((rows, width), LOW),
        ],
        scratch_shapes=[
            pltpu.VMEM((LANES, width, OUT_PACK), LOW),
            pltpu.VMEM((TWO * PADDED, width), FULL),
            pltpu.SemaphoreType.DMA((LANES,)),
        ],
        compiler_params=params(),
        cost_estimate=cost(8e9, 1.5e7),
    )(mine, ctx, x, vectors, *pieces)


def gelu_pair(values):
    density = jnp.exp(values * values * -0.5) * INV_SQRT2PI
    below = 0.5 * lax.erf(values * INV_SQRT2) + 0.5
    return values * below, below + values * density


def feed_body(blocks, layout, me_ref, n_ref, gd_ref, ub_ref, *refs):
    count = sum(part[3] for part in layout)
    pieces = refs[:count]
    out_ref, gn_ref, keep_ref, send_ref, gub_ref, nt_s, gdt_s, up_s, down_s, act_s, gh_s, sems = refs[count:]
    step = pl.program_id(0)
    place = me_ref[0]
    rows = n_ref.shape[0]
    units = up_s.shape[3]
    per = rows // blocks

    def begin(group):
        slot = group % 2
        for index, (_, table, first, number, up_at, down_at) in enumerate(layout):
            held = pieces[first : first + number]
            for target, at, kind in ((up_s, up_at, 0), (down_s, down_at, 1)):
                fetch(
                    group,
                    table,
                    held,
                    (at, at + units),
                    target.at[slot, index],
                    sems.at[slot, kind, index],
                    place,
                )

    @pl.when(step == 0)
    def _():
        begin(0)
        nt_s[...] = n_ref[...].T
        gdt_s[...] = gd_ref[...].T
        out_ref[...] = jnp.zeros_like(out_ref)
        gn_ref[...] = jnp.zeros_like(gn_ref)

    for group in range(LANES):

        @pl.when(step == group)
        def _(group=group):
            if group + 1 < LANES:
                begin(group + 1)

    now = step % 2
    parts = len(layout)
    for index in range(parts):
        for kind, target in enumerate((up_s, down_s)):
            fetched(target.at[now, index], sems.at[now, kind, index])
    up_weight = [up_s[now, index] for index in range(parts)]
    down_weight = [down_s[now, index] for index in range(parts)]
    if parts > 1:
        up_weight = [jnp.concatenate(up_weight, axis=1)]
        down_weight = [jnp.concatenate(down_weight, axis=1)]
    up_weight, down_weight = up_weight[0], down_weight[0]
    true_lane = step ^ me_ref[1]
    unit_bias = ub_ref[true_lane]
    unit_sums = jnp.zeros((8, up_weight.shape[1]), FULL)
    for block in range(blocks):
        part = slice(block * per, (block + 1) * per)
        hidden = dot(n_ref[part, :], up_weight) + unit_bias
        active, slope = gelu_pair(hidden)
        active = active.astype(LOW)
        act_s[part, :] = active
        grad = (dot(gd_ref[part, :], down_weight) * slope).astype(LOW)
        gh_s[part, :] = grad
        unit_sums = unit_sums + fold(grad.astype(FULL))
        out_ref[part, :] += dot(active, down_weight, 1, 1)
        gn_ref[part, :] += dot(grad, up_weight, 1, 1)
    gub_ref[true_lane] = jnp.sum(unit_sums, axis=0, keepdims=True)
    grad_up = dot(nt_s[...], gh_s[...]).astype(LOW)
    grad_down = dot(gdt_s[...], act_s[...]).astype(LOW)
    chunk_rows = keep_ref.shape[2]
    wide = grad_up.shape[1]
    for odd, target in enumerate((keep_ref, send_ref)):

        @pl.when(step % 2 == odd)
        def _(target=target):
            for chunk in range(CHUNKS):
                slot = reversed_bits(chunk) ^ reversed_bits(place)
                at = slice(chunk * chunk_rows, (chunk + 1) * chunk_rows)
                target[0, slot, :, :wide] = grad_up[at]
                target[0, slot, :, wide:] = grad_down[at]


def feed(mine, normed, grad_down, unit_bias, groups, units, images):
    rows, width = normed.shape
    blocks = max(1, images // 4)
    parts = len(groups)
    sub = units // parts
    pieces, layout = [], []
    for (arrays, table), up_at, down_at in groups:
        layout.append((None, table, len(pieces), len(arrays), up_at, down_at))
        pieces.extend(arrays)
    chunk_rows = width // CHUNKS
    grad_block = (1, CHUNKS, chunk_rows, 2 * units)
    grads = jax.ShapeDtypeStruct((2,) + grad_block[1:], LOW)
    return pl.pallas_call(
        functools.partial(feed_body, blocks, layout),
        grid=(LANES,),
        in_specs=[
            pl.BlockSpec(memory_space=pltpu.SMEM),
            whole((rows, width)),
            whole((rows, width)),
            whole((LANES, 1, units)),
        ]
        + [anywhere()] * len(pieces),
        out_specs=[
            whole((rows, width)),
            whole((rows, width)),
            pl.BlockSpec(grad_block, lambda j: (j // 2, 0, 0, 0)),
            pl.BlockSpec(grad_block, lambda j: (jnp.maximum(j - 1, 0) // 2, 0, 0, 0)),
            whole((LANES, 1, units)),
        ],
        out_shape=[jax.ShapeDtypeStruct((rows, width), FULL)] * 2
        + [grads] * 2
        + [jax.ShapeDtypeStruct((LANES, 1, units), FULL)],
        scratch_shapes=[
            pltpu.VMEM((width, rows), LOW),
            pltpu.VMEM((width, rows), LOW),
            pltpu.VMEM((2, parts, width, sub), LOW),
            pltpu.VMEM((2, parts, width, sub), LOW),
            pltpu.VMEM((rows, units), LOW),
            pltpu.VMEM((rows, units), LOW),
            pltpu.SemaphoreType.DMA((2, 2, parts)),
        ],
        compiler_params=params(),
        cost_estimate=cost(3.5e10, 4e7),
    )(mine, normed, grad_down, unit_bias, *pieces)


def second_body(
    me_ref, down_ref, gn_ref, mid_ref, att_ref, ctx_ref, cot_ref, vec_ref, out_ref, gm_ref, ga_ref, keep_ref, send_ref, rows_ref, pad_s, out_s, sums_s, gat_s
):
    step = pl.program_id(0)

    @pl.when(step == 0)
    def _():
        pad_s[...] = jnp.zeros_like(pad_s)
        sums_s[...] = jnp.zeros_like(sums_s)

    cot = load_images(pad_s, cot_ref, step)
    down = down_ref[...] + vec_ref[6:7, :]
    mid = mid_ref[...]
    store_images(out_ref, out_s, mid + vec_ref[7:8, :] * down, step)
    scaled, inverse = normalise(mid)
    grad_normed = gn_ref[...]
    grad_mid = cot + norm_back(grad_normed, vec_ref[2:3, :], scaled, inverse)
    gm_ref[...] = grad_mid
    grad_att = (grad_mid * vec_ref[5:6, :]).astype(LOW)
    ga_ref[...] = grad_att
    gat_s[step] = grad_att.T
    sums_s[0] += fold(grad_normed * scaled)
    sums_s[1] += fold(grad_normed)
    sums_s[2] += fold(grad_mid)
    sums_s[3] += fold(grad_mid * att_ref[...].astype(FULL))
    sums_s[4] += fold(cot)
    sums_s[5] += fold(cot * down)

    @pl.when(step == pl.num_programs(0) - 1)
    def _():
        sums = [jnp.sum(sums_s[index], axis=0, keepdims=True) for index in range(6)]
        sums[2] = sums[2] * vec_ref[5:6, :]
        sums[4] = sums[4] * vec_ref[7:8, :]
        for index in range(6):
            rows_ref[index : index + 1, :] = sums[index]
        images = gat_s.shape[0]
        for group in range(LANES):
            at = slice(group * OUT_PACK, (group + 1) * OUT_PACK)
            grad = dot(gat_s[0], ctx_ref[0:PADDED, at])
            for image in range(1, images):
                grad = grad + dot(
                    gat_s[image], ctx_ref[image * PADDED : (image + 1) * PADDED, at]
                )
            give(me_ref[0], keep_ref, send_ref, group, grad.astype(LOW))


def give(place, keep_ref, send_ref, group, grad):
    rows = keep_ref.shape[2]
    mine = reversed_bits(place)
    target = (keep_ref, send_ref)[group % 2]
    for chunk in range(CHUNKS):
        target[group // 2, reversed_bits(chunk) ^ mine] = grad[chunk * rows : (chunk + 1) * rows]


def second_back(mine, down, grad_normed, mid, att, ctx, cot, vectors, images):
    rows, width = mid.shape
    block = lambda: pl.BlockSpec((PADDED, width), lambda i: (i, 0))
    grads = (2, CHUNKS, width // CHUNKS, OUT_PACK)
    return pl.pallas_call(
        second_body,
        grid=(images,),
        in_specs=[
            pl.BlockSpec(memory_space=pltpu.SMEM),
            block(),
            block(),
            block(),
            block(),
            whole(ctx.shape),
            whole(cot.shape),
            whole(vectors.shape),
        ],
        out_specs=[whole(cot.shape), block(), block(), whole(grads), whole(grads), whole((6, width))],
        out_shape=[
            jax.ShapeDtypeStruct(cot.shape, FULL),
            jax.ShapeDtypeStruct((rows, width), FULL),
            jax.ShapeDtypeStruct((rows, width), LOW),
            jax.ShapeDtypeStruct(grads, LOW),
            jax.ShapeDtypeStruct(grads, LOW),
            jax.ShapeDtypeStruct((6, width), FULL),
        ],
        scratch_shapes=[
            pltpu.VMEM((PADDED, width), FULL),
            pltpu.VMEM((PADDED, width), FULL),
            pltpu.VMEM((6, 8, width), FULL),
            pltpu.VMEM((images, width, PADDED), LOW),
        ],
        compiler_params=params(),
        cost_estimate=cost(1e10, 2e7),
    )(mine, down, grad_normed, mid, att, ctx, cot, vectors)


def back_body(table, columns, images, me_ref, ga_ref, qkv_ref, prob_ref, *refs):
    pieces = refs[:-6]
    dqkv_ref, pair_ref, cols_ref, weight_s, gc_s, sems = refs[-6:]
    step = pl.program_id(0)

    @pl.when(step == 0)
    def _():
        for group in range(LANES):
            fetch(group, table, pieces, columns, weight_s.at[group], sems.at[group], me_ref[0])

    fetched(weight_s.at[step], sems.at[step])
    gc_s[...] = dot(ga_ref[...], weight_s[step]).astype(LOW)
    lane = halves()

    def tile(image, index):
        return qkv_ref[0, image * PADDED : (image + 1) * PADDED, 128 * index : 128 * (index + 1)]

    def upstream(image, head):
        at = 128 if head == 2 else 0
        value = gc_s[image * PADDED : (image + 1) * PADDED, at : at + 128]
        return half_of(value, lane, V_ODD[head])

    def first(image, head):
        return dot(tile(image, V_TILE[head]), upstream(image, head), 1, 1)

    def second(grad_prob, image, head):
        soft = prob_ref[image, head].astype(FULL)
        weighted = soft * grad_prob
        inner = jnp.sum(weighted, axis=0, keepdims=True)
        grad_score = weighted - soft * inner
        if image == 0:
            pair_ref[head] = grad_score
        else:
            pair_ref[head] += grad_score
        return grad_score.astype(LOW)

    def third(low_score, image, head):
        odd = QK_ODD[head]
        return (
            dot(low_score, half_of(tile(image, K_TILE[head]), lane, odd), 0, 0) * HD**-0.5,
            dot(low_score, half_of(tile(image, Q_TILE[head]), lane, odd)),
            dot(prob_ref[image, head], upstream(image, head)),
        )

    work = [(image, head) for image in range(images) for head in range(HEADS_LANE)]
    probs, scores, grads = {}, {}, {}
    sums = [jnp.zeros((8, 128), FULL)] * 3
    for turn_index in range(len(work) + 2):
        if turn_index < len(work):
            probs[turn_index] = first(*work[turn_index])
        if 0 <= turn_index - 1 < len(work):
            scores[turn_index - 1] = second(probs.pop(turn_index - 1), *work[turn_index - 1])
        done = turn_index - 2
        if done < 0:
            continue
        image, head = work[done]
        grads[head] = third(scores.pop(done), image, head)
        if head < HEADS_LANE - 1:
            continue
        packed = (
            grads[0][0] + grads[1][0],
            grads[2][0] + grads[2][2],
            grads[0][2] + grads[1][2],
            grads[0][1] + grads[1][1],
            grads[2][1],
        )
        rows = slice(image * PADDED, (image + 1) * PADDED)
        for index, value in enumerate(packed):
            low_value = value.astype(LOW)
            dqkv_ref[0, rows, 128 * index : 128 * (index + 1)] = low_value
            if index < 3:
                sums[index] = sums[index] + fold(low_value.astype(FULL))
    for index in range(3):
        cols_ref[0, :, 128 * index : 128 * (index + 1)] = sums[index]


def back(mine, grad_att, qkv, prob, gathered, columns, images):
    rows, width = grad_att.shape
    heads = prob.shape[1]
    pieces, table = gathered
    return pl.pallas_call(
        functools.partial(back_body, table, columns, images),
        grid=(LANES,),
        in_specs=[
            pl.BlockSpec(memory_space=pltpu.SMEM),
            whole(grad_att.shape),
            pl.BlockSpec((1, rows, PACK), lambda g: (g, 0, 0)),
            pl.BlockSpec((images, HEADS_LANE, PADDED, PADDED), lambda g: (0, g, 0, 0)),
        ]
        + [anywhere()] * len(pieces),
        out_specs=[
            pl.BlockSpec((1, rows, PACK), lambda g: (g, 0, 0)),
            pl.BlockSpec((HEADS_LANE, PADDED, PADDED), lambda g: (g, 0, 0)),
            pl.BlockSpec((1, 8, 384), lambda g: (g, 0, 0)),
        ],
        out_shape=[
            jax.ShapeDtypeStruct((LANES, rows, PACK), LOW),
            jax.ShapeDtypeStruct((heads, PADDED, PADDED), FULL),
            jax.ShapeDtypeStruct((LANES, 8, 384), FULL),
        ],
        scratch_shapes=[
            pltpu.VMEM((LANES, width, OUT_PACK), LOW),
            pltpu.VMEM((rows, OUT_PACK), LOW),
            pltpu.SemaphoreType.DMA((LANES,)),
        ],
        compiler_params=params(),
        cost_estimate=cost(3e10, 4e7),
    )(mine, grad_att, qkv, prob, *pieces)


def heads_body(pair_ref, cols_ref, thin_ref, heads_ref, spread_s, flat_s):
    heads = pair_ref.shape[0]
    spread_s[...] = jnp.zeros_like(spread_s)

    def head_sum(index, carry):
        for row in range(GRID):
            at = GRID * (GRID - 1 - row)
            spread_s[index, :, at : at + PATCHES] += pair_ref[
                index, row * GRID : (row + 1) * GRID, 0:PATCHES
            ]
        return carry

    lax.fori_loop(0, heads, head_sum, 0)
    for col in range(GRID):
        flat_s[16 * col : 16 * (col + 1), :] = spread_s[:, col, :]
    wide = exact_dot(flat_s[...], thin_ref[...], 1)
    table = jnp.zeros((16, TABLE), FULL)
    for col in range(GRID):
        table = table + turn(wide[16 * col : 16 * (col + 1)], GRID - 1 - col)
    for group in range(LANES):
        cols = jnp.sum(cols_ref[group], axis=0, keepdims=True)
        for head in range(HEADS_LANE):
            at = HD * (4 + head if head < 2 else 3)
            heads_ref[group, head : head + 1, 0:HD] = cols[:, HD * head : HD * (head + 1)]
            heads_ref[group, head : head + 1, HD : 2 * HD] = cols[:, at : at + HD]
        first = group * HEADS_LANE
        heads_ref[group, :, 2 * HD :] = table[first : first + HEADS_LANE, 0 : SPAN * SPAN]


def heads_back(pair, cols, thin):
    heads = pair.shape[0]
    return pl.pallas_call(
        heads_body,
        out_shape=jax.ShapeDtypeStruct((LANES, HEADS_LANE, 2 * HD + SPAN * SPAN), FULL),
        scratch_shapes=[
            pltpu.VMEM((16, GRID, SPREAD), FULL),
            pltpu.VMEM((16 * GRID, SPREAD), FULL),
        ],
        compiler_params=params(),
        cost_estimate=cost(3e9, 4e6),
    )(pair, cols, thin)


def project_body(me_ref, n_ref, dqkv_ref, keep_ref, send_ref, t_s):
    t_s[...] = n_ref[...].T
    for group in range(LANES):
        give(me_ref[0], keep_ref, send_ref, group, dot(t_s[...], dqkv_ref[group]).astype(LOW))


def project(mine, normed, dqkv):
    rows, width = normed.shape
    grads = jax.ShapeDtypeStruct((2, CHUNKS, width // CHUNKS, PACK), LOW)
    return pl.pallas_call(
        project_body,
        in_specs=[pl.BlockSpec(memory_space=pltpu.SMEM)] + [pl.BlockSpec(memory_space=pltpu.VMEM)] * 2,
        out_shape=[grads, grads],
        scratch_shapes=[pltpu.VMEM((width, rows), LOW)],
        compiler_params=params(),
        cost_estimate=cost(8e9, 1e7),
    )(mine, normed, dqkv)


def input_body(table, me_ref, dqkv_ref, gm_ref, x_ref, vec_ref, *refs):
    pieces = refs[:-7]
    out_ref, rows_ref, weight_s, pad_s, out_s, sums_s, sems = refs[-7:]
    step = pl.program_id(0)

    @pl.when(step == 0)
    def _():
        for group in range(LANES):
            fetch(group, table, pieces, (0, PACK), weight_s.at[group], sems.at[group], me_ref[0])
        pad_s[...] = jnp.zeros_like(pad_s)
        sums_s[...] = jnp.zeros_like(sums_s)
        for group in range(LANES):
            fetched(weight_s.at[group], sems.at[group])

    scaled, inverse = normalise(load_images(pad_s, x_ref, step))
    grad = dot(dqkv_ref[0], weight_s[0], 1, 1)
    for group in range(1, LANES):
        grad = grad + dot(dqkv_ref[group], weight_s[group], 1, 1)
    sums_s[0] += fold(grad * scaled)
    sums_s[1] += fold(grad)
    for index in range(2):
        rows_ref[index : index + 1, :] = jnp.sum(sums_s[index], axis=0, keepdims=True)
    result = gm_ref[...] + norm_back(grad, vec_ref[0:1, :], scaled, inverse)
    store_images(out_ref, out_s, result, step)


def input_back(mine, dqkv, grad_mid, x, vectors, gathered, images):
    width = x.shape[1]
    pieces, table = gathered
    return pl.pallas_call(
        functools.partial(input_body, table),
        grid=(images // TWO,),
        in_specs=[
            pl.BlockSpec(memory_space=pltpu.SMEM),
            pl.BlockSpec((LANES, TWO * PADDED, PACK), lambda i: (0, i, 0)),
            pl.BlockSpec((TWO * PADDED, width), lambda i: (i, 0)),
            whole(x.shape),
            whole(vectors.shape),
        ]
        + [anywhere()] * len(pieces),
        out_specs=[whole(x.shape), whole((2, width))],
        out_shape=[jax.ShapeDtypeStruct(x.shape, FULL), jax.ShapeDtypeStruct((2, width), FULL)],
        scratch_shapes=[
            pltpu.VMEM((LANES, width, PACK), LOW),
            pltpu.VMEM((TWO * PADDED, width), FULL),
            pltpu.VMEM((TWO * PADDED, width), FULL),
            pltpu.VMEM((2, 8, width), FULL),
            pltpu.SemaphoreType.DMA((LANES,)),
        ],
        compiler_params=params(),
        cost_estimate=cost(1.5e10, 1.5e7),
    )(mine, dqkv, grad_mid, x, vectors, *pieces)


def swap(values, axis, bit):
    count = lax.axis_size(axis)
    return lax.ppermute(values, axis, [(index, index ^ bit) for index in range(count)])


def after(values, *others):
    return lax.optimization_barrier((values,) + others)[0]


def sync(*values):
    return lax.optimization_barrier(values)


def join(former, latter, axis=0):
    return jnp.concatenate([former, latter], axis=axis)


def split_rows(held):
    half = held.shape[1] // 2
    return held[:, :half], held[:, half:]


def pieces_of(upper, upper_x, lower, lower_y, near_core, far_core):
    arrays = [upper, upper_x, lower, lower_y, near_core[0], far_core[0], near_core[1], far_core[1]]
    half = upper.shape[1]

    def part(first, far):
        top = [(first + far, slot) for slot in range(8)]
        low = [(first + 2 + slot // 4, 4 * far + slot % 4) for slot in range(8)]
        return ((0, top), (half, low))

    return arrays, (part(0, 0), part(4, 0), part(0, 1), part(4, 1))


def total_of(terms):
    total = terms[0].astype(FULL)
    for one in terms[1:]:
        total = total + one.astype(FULL)
    return total


def sum_call(body, grid, views, outs, moved):
    return pl.pallas_call(
        body,
        grid=(grid,),
        in_specs=[pl.BlockSpec(block, index) for _, block, index in views],
        out_specs=[pl.BlockSpec(block, index) for _, _, block, index in outs],
        out_shape=[jax.ShapeDtypeStruct(shape, dtype) for shape, dtype, _, _ in outs],
        compiler_params=params(),
        cost_estimate=cost(1e6, moved),
    )(*[array for array, _, _ in views])


def sum_away(keeps, gots):
    half = keeps[0].shape[2] // 2
    wide = sum(keep.shape[3] for keep in keeps)
    views = []
    for keep, got in zip(keeps, gots):
        block = (1, 2, half, keep.shape[3])
        for array in (keep, got):
            views.append((array, block, lambda j: (1, j, 0, 0)))
            views.append((array, block, lambda j: (j // 2, 2 + j % 2, 1, 0)))

    def body(*refs):
        ins, (upper, lower) = refs[:-2], refs[-2:]
        first = 0
        for index in range(0, len(ins), 4):
            keep_u, keep_l, got_u, got_l = ins[index : index + 4]
            at = slice(first, first + keep_u.shape[3])
            first = at.stop
            upper[:, :, at] = total_of((keep_u[0], got_u[0])).astype(LOW)
            lower[0, :, :, at] = total_of((keep_l[0], got_l[0])).astype(LOW)

    outs = [
        ((8, half, wide), LOW, (2, half, wide), lambda j: (j, 0, 0)),
        ((2, 4, half, wide), LOW, (1, 2, half, wide), lambda j: (j // 2, j % 2, 0, 0)),
    ]
    return sum_call(body, 4, views, outs, 8e6)


def sum_here(keeps, gots, upper_got, lower_got):
    half = keeps[0].shape[2] // 2
    wide = sum(keep.shape[3] for keep in keeps)
    places = (
        lambda j: (0, j, 0, 0),
        lambda j: (0, 4 + j, 0, 0),
        lambda j: (0, j, 1, 0),
        lambda j: (1, j, 1, 0),
    )
    views = [
        (upper_got, (1, half, wide), lambda j: (j, 0, 0)),
        (upper_got, (1, half, wide), lambda j: (4 + j, 0, 0)),
        (lower_got, (1, 1, half, wide), lambda j: (0, j, 0, 0)),
        (lower_got, (1, 1, half, wide), lambda j: (1, j, 0, 0)),
    ]
    for keep, got in zip(keeps, gots):
        for array in (keep, got):
            views.extend((array, (1, 1, half, keep.shape[3]), place) for place in places)

    def body(*refs):
        far, ins, outs = refs[:4], refs[4:-4], refs[-4:]
        first = 0
        for index in range(0, len(ins), 8):
            at = slice(first, first + ins[index].shape[3])
            first = at.stop
            for view in range(4):
                came = far[view][0, :, at] if view < 2 else far[view][0, 0, :, at]
                terms = (ins[index + view][0, 0], ins[index + 4 + view][0, 0], came)
                outs[view][0, :, at] = total_of(terms).astype(outs[view].dtype)

    outs = [
        ((4, half, wide), dtype, (1, half, wide), lambda j: (j, 0, 0))
        for dtype in (FULL, LOW, FULL, LOW)
    ]
    return sum_call(body, 4, views, outs, 1.2e7)


def sum_line(upper, upper_got, lower, lower_got):
    half, wide = upper.shape[1:]
    views = []
    for array in (upper, upper_got, lower, lower_got):
        views.append((array, (1, half, wide), lambda j: (j, 0, 0)))
        views.append((array, (1, half, wide), lambda j: (2 + j, 0, 0)))

    def body(*refs):
        for side in range(2):
            out = refs[8 + side]
            out[0, :half] = total_of((refs[side][0], refs[2 + side][0])).astype(out.dtype)
            out[0, half:] = total_of((refs[4 + side][0], refs[6 + side][0])).astype(out.dtype)

    outs = [
        ((2, 2 * half, wide), dtype, (1, 2 * half, wide), lambda j: (j, 0, 0))
        for dtype in (FULL, LOW)
    ]
    return sum_call(body, 2, views, outs, 6e6)


def adam(weight, moment_one, moment_two, incoming, step_rate, decay_rate):
    first_new = BETA_ONE * moment_one + (1.0 - BETA_ONE) * incoming
    second_new = BETA_TWO * moment_two + (1.0 - BETA_TWO) * incoming * incoming
    update = (
        first_new
        / (1.0 - BETA_ONE**STEP)
        / (jnp.sqrt(second_new / (1.0 - BETA_TWO**STEP)) + ADAM_EPSILON)
    )
    return (second_new, weight * (1.0 - step_rate * decay_rate) - step_rate * update)


def pack_attention(weights):
    query, key, value, out = (weights[index] for index in range(4))
    rows = query.shape[0]
    blank = jnp.zeros((rows, HD), weights.dtype)
    first = jnp.concatenate([query, value[:, 128:], value[:, :128], key, blank], axis=1)
    last = jnp.concatenate([out[:, :128], blank, out[:, 128:]], axis=1)
    return first, last


def unpack_attention(first, last):
    query = first[:, :192]
    value = jnp.concatenate([first[:, 256:384], first[:, 192:256]], axis=1)
    key = first[:, 384:576]
    out = jnp.concatenate([last[:, :128], last[:, 192:]], axis=1)
    return jnp.stack([query, key, value, out])


def shards(
    block_input,
    cotangent,
    image_size,
    attention_weights,
    attention_first,
    attention_second,
    mlp_weights,
    mlp_first,
    mlp_second,
    head_params,
    head_first,
    head_second,
    norm_params,
    norm_first,
    norm_second,
):
    near = lax.axis_size("dp") == CHUNKS
    lane_index = lax.axis_index("mp")
    local_rows, width = block_input.shape
    images = local_rows // PATCHES
    local_heads = head_params.shape[0]
    chunk_rows = width // CHUNKS
    thin = jnp.asarray(thin_matrix(), LOW)

    first, last = pack_attention(attention_weights.astype(LOW))
    mlp_low = mlp_weights.astype(LOW)
    units = mlp_low.shape[2]
    unit_bias = norm_params[8:].reshape(LANES, 1, units)
    first = jnp.concatenate([first, last], axis=1)
    second = jnp.concatenate([mlp_low[0], mlp_low[1]], axis=1)
    out_at = (PACK, PACK + OUT_PACK)
    if near:
        mine = jnp.stack([lax.axis_index("dp"), lane_index, lane_index]).astype(jnp.int32)
        core = lambda values: swap(values, "mp", 1)
        x_axis = lambda values: swap(values, "mp", 2)
        y_axis = lambda values: swap(values, "dp", 1)
        z_near = lambda values: swap(values, "dp", 2)
        z_far = lambda values: swap(values, "dp", 4)
        one, two = first[None], second[None]
        got = z_far(one)
        normed_one, grad_down = first_norm(block_input, cotangent, norm_params, images)
        got, normed_one, other = sync(got, normed_one, x_axis(after(head_params, first)))
        one = join(one, got)
        got = z_near(one)
        two_got = z_far(after(two, one))
        got, near_table, far_table = sync(got, core(head_params), core(other))
        upper, lower = split_rows(join(one, got))
        upper, lower = sync(upper, lower)
        upper_got, lower_got = y_axis(upper), x_axis(lower)
        upper_got, lower_got = sync(upper_got, lower_got)
        upper, lower = sync(join(upper, upper_got), join(lower, lower_got))
        upper_far, lower_far = x_axis(upper), y_axis(lower)
        two = join(two, after(two_got, upper, lower))
        two_got = z_near(two)
        bias, add = spread_bias(
            (head_params, after(near_table, two), other, after(far_table, two)), thin
        )
        near_core = sync(core(upper), core(lower))
        upper_far, lower_far, two_got, bias = sync(
            upper_far, lower_far, after(two_got, *near_core), bias
        )
        far_core = sync(core(upper_far), core(lower_far))
        first_all = pieces_of(upper, upper_far, lower, lower_far, near_core, far_core)
        two_upper, two_lower = split_rows(join(two, two_got))
        two_upper, two_lower, normed_one = sync(two_upper, two_lower, normed_one)
        two_upper_got, two_lower_got = y_axis(two_upper), x_axis(two_lower)
    else:
        mine = jnp.stack([0 * lane_index, 0 * lane_index, lane_index]).astype(jnp.int32)

        def gather_far(piece):
            full = lax.all_gather(piece, "dp", axis=0, tiled=True)
            full = lax.all_gather(full, "mp", axis=0, tiled=False)
            full = full.reshape(LANES, CHUNKS, chunk_rows, piece.shape[1])
            order = [reversed_bits(index) for index in range(CHUNKS)]
            full = jnp.stack([full[:, index] for index in order], axis=1)
            slots = range(CHUNKS)
            table = tuple(((0, [(group, slot) for slot in slots]),) for group in range(LANES))
            return [full[index] for index in range(LANES)], table

        tables = lax.all_gather(head_params, "mp", axis=0, tiled=False)
        tables = tuple(tables[index] for index in range(LANES))
        normed_one, grad_down = first_norm(block_input, cotangent, norm_params, images)
        bias, add = spread_bias(tables, thin)
        first_all = gather_far(first)
        second_all = gather_far(second)

    qkv, prob, ctx = attend(mine, image_size, normed_one, bias, add, first_all, images)
    if near:
        ctx, two_upper_got, two_lower_got = sync(ctx, two_upper_got, two_lower_got)
        two_upper, two_lower, ctx = sync(
            join(two_upper, two_upper_got), join(two_lower, two_lower_got), ctx
        )
        near_two = (core(two_upper), core(two_lower))
        far_two = (x_axis(two_upper), y_axis(two_lower))
    att, mid, normed_two = middle(
        mine, ctx, block_input, norm_params, first_all, out_at, images
    )
    if near:
        normed_two, *far_two = sync(normed_two, *far_two, *near_two)
        far_two, near_two = far_two[:2], far_two[2:]
        second_all = pieces_of(
            two_upper,
            far_two[0],
            two_lower,
            far_two[1],
            near_two,
            sync(core(far_two[0]), core(far_two[1])),
        )
    groups = ((second_all, 0, units),)
    down, grad_normed, keep_mlp, send_mlp, unit_sums = feed(
        mine, normed_two, grad_down, unit_bias, groups, units, images
    )
    if near:
        mlp_core = core(send_mlp)
    output, grad_mid, grad_att, keep_out, send_out, second_rows = second_back(
        mine, down, grad_normed, mid, att, ctx, cotangent, norm_params, images
    )
    if near:
        mlp_core, grad_att, send_out = sync(mlp_core, grad_att, send_out)
        keeps, gots = (keep_mlp, keep_out), (mlp_core, core(send_out))
        upper, lower, grad_att = sync(*sum_away(keeps, gots), grad_att)
        upper_got, lower_got = x_axis(upper), y_axis(lower)
    dqkv, pair, cols = back(
        mine, grad_att, qkv, prob, first_all, out_at, images
    )
    keep_att, send_att = project(mine, normed_one, dqkv)
    grad_heads = heads_back(after(pair, keep_att), cols, thin)
    if near:
        keep_att, send_att, upper_got, lower_got, grad_heads = sync(
            keep_att, send_att, upper_got, lower_got, grad_heads
        )
        att_core = core(send_att)
        upper, upper_away, lower, lower_away = sum_here(keeps, gots, upper_got, lower_got)
        upper_away, lower_away, att_core = sync(upper_away, lower_away, att_core)
        upper_got, lower_got = y_axis(upper_away), x_axis(lower_away)
        keeps, gots = (keep_att,), (att_core,)
        att_upper, att_lower, dqkv = sync(*sum_away(keeps, gots), dqkv)
        att_upper_got, att_lower_got = x_axis(att_upper), y_axis(att_lower)
    grad_input, first_rows = input_back(
        mine, dqkv, grad_mid, block_input, norm_params, first_all, images
    )
    norms = jnp.concatenate([first_rows, second_rows, unit_sums.reshape(-1, width)], axis=0)
    if near:
        count = norms.shape[0]
        rest = count + local_heads
        norms, *heads = sync(norms, *[grad_heads[index] for index in range(LANES)])
        norms = jnp.pad(norms, ((0, 0), (0, grad_heads.shape[2] - width)))
        keep = jnp.concatenate([norms, heads[0], heads[2]], axis=0)
        small_got = core(jnp.concatenate([norms, heads[1], heads[3]], axis=0))
        upper_got, lower_got, small_got = sync(upper_got, lower_got, small_got)
        line, line_away = sum_line(upper, upper_got, lower, lower_got)
        line_got = z_near(line_away)
        small = keep + small_got
        small_got = x_axis(join(small[:count], small[rest:]))
        upper_got, lower_got, line_away, small_got = sync(
            att_upper_got, att_lower_got, line_away, small_got
        )
        small = small[:rest] + small_got
        upper, upper_away, lower, lower_away = sum_here(keeps, gots, upper_got, lower_got)
        upper_away, lower_away, small = sync(upper_away, lower_away, small)
        upper_got, lower_got = y_axis(upper_away), x_axis(lower_away)
        small_got = y_axis(small)
        here, away = sum_line(upper, upper_got, lower, lower_got)
        small_got, line_got, away = sync(small_got, line_got, away)
        line = line + line_got.astype(FULL)
        small, line_away = sync(small + small_got, line[1].astype(LOW))
        got, line_got = z_near(away), z_far(line_away)
        came = (z_near(small), z_far(small), swap(small, "dp", 6))
        here = here + got.astype(FULL)
        got = z_far(here[1].astype(LOW))
        small = (small + came[0]) + (came[1] + came[2])
        sum_mlp = line[0] + line_got.astype(FULL)
        sum_att = here[0] + got.astype(FULL)
        sum_mlp, sum_out = sum_mlp[:, : 2 * units], sum_mlp[:, 2 * units :]
        reduced_norms = small[:count, :width]
        reduced_heads = small[count:]
    else:
        reduced_norms = lax.psum(norms, ("dp", "mp"))
        reduced_heads = lax.psum_scatter(
            lax.psum(grad_heads, "dp"), "mp", scatter_dimension=0, tiled=False
        )

        def scatter_far(keep, send):
            terms = jnp.stack([keep[0], send[0], keep[1], send[1]])
            order = [reversed_bits(index) for index in range(CHUNKS)]
            terms = jnp.stack([terms[:, index] for index in order], axis=1)
            terms = terms.reshape(LANES, width, terms.shape[-1])
            mine_only = lax.psum_scatter(terms, "mp", scatter_dimension=0, tiled=False)
            return lax.psum_scatter(
                mine_only.astype(FULL), "dp", scatter_dimension=0, tiled=True
            )

        sum_mlp = scatter_far(keep_mlp, send_mlp)
        sum_out = scatter_far(keep_out, send_out)
        sum_att = scatter_far(keep_att, send_att)

    reduced_attention = unpack_attention(sum_att, sum_out)
    reduced_mlp = jnp.stack([sum_mlp[:, :units], sum_mlp[:, units:]])
    attention_second_new, attention_new = adam(
        attention_weights,
        attention_first,
        attention_second,
        reduced_attention,
        RATE_MATRIX,
        DECAY_MATRIX,
    )
    mlp_second_new, mlp_new = adam(
        mlp_weights, mlp_first, mlp_second, reduced_mlp, RATE_MATRIX, DECAY_MATRIX
    )
    head_second_new, head_new = adam(
        head_params, head_first, head_second, reduced_heads, RATE_VECTOR, 0.0
    )
    norm_second_new, norm_new = adam(
        norm_params, norm_first, norm_second, reduced_norms, RATE_VECTOR, 0.0
    )
    return (
        output,
        grad_input,
        reduced_attention,
        attention_second_new,
        attention_new,
        reduced_mlp,
        mlp_second_new,
        mlp_new,
        reduced_heads,
        head_second_new,
        head_new,
        reduced_norms,
        norm_second_new,
        norm_new,
    )


def solution(mesh):
    rows = P(("dp", "mp"), None)
    matrix = P(None, "dp", "mp")
    head = P("mp", None)
    placed = (rows, rows, P("dp", None)) + (matrix,) * 6 + (head,) * 3 + (P(),) * 3
    given = (rows, rows) + (matrix,) * 6 + (head,) * 3 + (P(),) * 3
    return jax.shard_map(shards, mesh=mesh, in_specs=placed, out_specs=given, check_vma=False)
```

```python
import functools

import jax
import jax.numpy as jnp
import numpy as np
from jax import lax
from jax.experimental import pallas as pl
from jax.experimental.pallas import tpu as pltpu
from jax.sharding import PartitionSpec as P

HD = 64
GRID = 14
SPAN = 2 * GRID - 1
STEP = 10
PATCHES = 196
PADDED = 208
PACK = 640
OUT_PACK = 256
CHUNKS = 8
LANES = 4
HEADS_LANE = 3
TWO = 2
TABLE = 768
SPREAD = 384

EPSILON = 1e-06
NEGATIVE = -1e30
BETA_ONE = 0.9
BETA_TWO = 0.999
ADAM_EPSILON = 1e-08
RATE_MATRIX = 0.05
RATE_VECTOR = 0.4
DECAY_MATRIX = 0.05

LOW = jnp.bfloat16
FULL = jnp.float32
INV_SQRT2 = 0.7071067811865476
INV_SQRT2PI = 0.3989422804014327
VMEM_LIMIT = 60 << 20


def dot(former, latter, former_dim=1, latter_dim=0):
    return lax.dot_general(
        former,
        latter,
        (((former_dim,), (latter_dim,)), ((), ())),
        preferred_element_type=FULL,
    )


def normalise(values):
    row_mean = jnp.mean(values, axis=-1, keepdims=True)
    centre = values - row_mean
    variance = jnp.mean(centre * centre, axis=-1, keepdims=True)
    inverse = lax.rsqrt(variance + EPSILON)
    return centre * inverse, inverse


def norm_back(incoming, norm_gain, scaled, inverse):
    weighted = incoming * norm_gain
    centred = weighted - jnp.mean(weighted, axis=-1, keepdims=True)
    return inverse * (centred - scaled * jnp.mean(weighted * scaled, axis=-1, keepdims=True))


def fold(values):
    rows, cols = values.shape
    return jnp.sum(values.reshape(rows // 8, 8, cols), axis=0)


def reversed_bits(index):
    return (index & 1) * 4 + (index & 2) + (index & 4) // 4


def whole(shape):
    zeros = (0,) * len(shape)
    return pl.BlockSpec(tuple(shape), lambda *_: zeros)


def params():
    return pltpu.CompilerParams(vmem_limit_bytes=VMEM_LIMIT)


def cost(flops, moved):
    return pl.CostEstimate(flops=int(flops), bytes_accessed=int(moved), transcendentals=0)


def fetch(group, table, refs, columns, target, sem, place):
    for rows, part in table[group]:
        for slot, (source, lead) in enumerate(part):
            height = refs[source].shape[1]
            chunk = target.shape[0] // CHUNKS
            start = (reversed_bits(slot) ^ place) * chunk + rows
            pltpu.make_async_copy(
                refs[source].at[lead, :, columns[0] : columns[1]],
                target.at[pl.ds(pl.multiple_of(start, 16), height), :],
                sem,
            ).start()


def fetched(target, sem):
    pltpu.make_async_copy(target, target, sem).wait()


def anywhere():
    return pl.BlockSpec(memory_space=pl.ANY)


def load_images(pad, source, step):
    count = pad.shape[0] // PADDED
    for first in range(0, source.shape[0] // PATCHES, count):

        @pl.when(step == first // count)
        def _(first=first):
            for index in range(count):
                at = (first + index) * PATCHES
                pad[index * PADDED : index * PADDED + PATCHES, :] = source[at : at + PATCHES, :]

    return pad[...]


def store_images(target, pad, value, step):
    count = pad.shape[0] // PADDED
    pad[...] = value
    for first in range(0, target.shape[0] // PATCHES, count):

        @pl.when(step == first // count)
        def _(first=first):
            for index in range(count):
                at = (first + index) * PATCHES
                target[at : at + PATCHES, :] = pad[index * PADDED : index * PADDED + PATCHES, :]


def first_norm_body(images, x_ref, cot_ref, vec_ref, normed_ref, gd_ref, pad_s):
    pad_s[...] = jnp.zeros_like(pad_s)
    for image in range(images):
        rows = slice(image * PATCHES, (image + 1) * PATCHES)
        target = slice(image * PADDED, (image + 1) * PADDED)
        scaled, _ = normalise(x_ref[rows, :])
        pad_s[0:PATCHES, :] = scaled * vec_ref[0:1, :] + vec_ref[1:2, :]
        normed_ref[target, :] = pad_s[...].astype(LOW)
        pad_s[0:PATCHES, :] = cot_ref[rows, :] * vec_ref[7:8, :]
        gd_ref[target, :] = pad_s[...].astype(LOW)


def first_norm(x, cot, vectors, images):
    width = x.shape[1]
    return pl.pallas_call(
        functools.partial(first_norm_body, images),
        out_shape=[jax.ShapeDtypeStruct((images * PADDED, width), LOW)] * 2,
        scratch_shapes=[pltpu.VMEM((PADDED, width), FULL)],
        compiler_params=params(),
        cost_estimate=cost(3e9, 4e6),
    )(x, cot, vectors)


def thin_matrix():
    matrix = np.zeros((TABLE, SPREAD), np.float32)
    for row in range(SPAN):
        for col in range(GRID):
            matrix[row * SPAN + col, row * GRID + col] = 1.0
    return matrix


def exact_dot(values, onehot, latter_dim=0):
    high = values.astype(LOW)
    rest = values - high.astype(FULL)
    mid = rest.astype(LOW)
    low = (rest - mid.astype(FULL)).astype(LOW)
    return (
        dot(high, onehot, 1, latter_dim)
        + dot(mid, onehot, 1, latter_dim)
        + dot(low, onehot, 1, latter_dim)
    )


def turn(values, shift):
    return pltpu.roll(values, shift % values.shape[1], 1)


def bias_body(t0, t1, t2, t3, thin_ref, bias_ref, add_ref, table_s, turned_s, spread_s):
    table_s[...] = jnp.zeros_like(table_s)
    for group, table in enumerate((t0, t1, t2, t3)):
        heads = slice(group * HEADS_LANE, (group + 1) * HEADS_LANE)
        table_s[heads, 0 : SPAN * SPAN] = table[:, 2 * HD :]
        rows = [table[head : head + 1, :HD] for head in range(HEADS_LANE)]
        more = [table[head : head + 1, HD : 2 * HD] for head in range(HEADS_LANE)]
        add_ref[group] = jnp.concatenate(
            rows + [more[2], more[0], more[1], jnp.zeros((1, PACK - 384), FULL)], axis=1
        )
    table = table_s[...]
    for col in range(GRID):
        turned_s[16 * col : 16 * (col + 1), :] = turn(table, col - (GRID - 1))
    spread = exact_dot(turned_s[...], thin_ref[...])
    for col in range(GRID):
        spread_s[:, col, :] = spread[16 * col : 16 * (col + 1)]

    def head(index, carry):
        bias_ref[index] = jnp.zeros(bias_ref.shape[1:], FULL)
        for row in range(GRID):
            start = GRID * (GRID - 1 - row)
            bias_ref[index, row * GRID : (row + 1) * GRID, 0:PATCHES] = spread_s[
                index, :, start : start + PATCHES
            ]
        return carry

    lax.fori_loop(0, bias_ref.shape[0], head, 0)


def spread_bias(tables, thin):
    heads = LANES * HEADS_LANE
    return pl.pallas_call(
        bias_body,
        out_shape=[
            jax.ShapeDtypeStruct((heads, PADDED, PADDED), FULL),
            jax.ShapeDtypeStruct((LANES, 1, PACK), FULL),
        ],
        scratch_shapes=[
            pltpu.VMEM((16, TABLE), FULL),
            pltpu.VMEM((16 * GRID, TABLE), FULL),
            pltpu.VMEM((16, GRID, SPREAD), FULL),
        ],
        compiler_params=params(),
        cost_estimate=cost(3e9, 4e6),
    )(*tables, thin)


Q_TILE = (0, 0, 1)
K_TILE = (3, 3, 4)
V_TILE = (2, 2, 1)
QK_ODD = (False, True, False)
V_ODD = (False, True, True)


def grid_places():
    position = np.arange(PADDED)
    row = np.where(position < PATCHES, position // GRID, 4 * GRID)
    places = np.stack([row, position % GRID]).astype(np.int32)
    return np.broadcast_to(places[:, :, None], (2, PADDED, 128)).copy()


def halves():
    lane = lax.broadcasted_iota(jnp.int32, (PADDED, 128), 1)
    return lane


def half_of(value, lane, odd):
    keep = lane >= HD if odd else lane < HD
    return jnp.where(keep, value, jnp.zeros_like(value))


def attend_body(table, images, me_ref, size_ref, grid_ref, n_ref, bias_ref, add_ref, *refs):
    pieces = refs[:-5]
    qkv_ref, prob_ref, ctx_ref, weight_s, sems = refs[-5:]
    step = pl.program_id(0)

    @pl.when(step == 0)
    def _():
        for group in range(LANES):
            fetch(group, table, pieces, (0, PACK), weight_s.at[group], sems.at[group], me_ref[0])

    fetched(weight_s.at[step], sems.at[step])
    scale = jnp.where(
        lax.broadcasted_iota(jnp.int32, (1, PACK), 1) < HEADS_LANE * HD, HD**-0.5, 1.0
    )
    acc = dot(n_ref[...], weight_s[step])
    qkv_ref[0] = ((acc + add_ref[0]) * scale).astype(LOW)

    lane = halves()
    masks = []
    for image in range(images):
        index = me_ref[2] * images + image
        inside = (grid_ref[0] < size_ref[index, 0]) & (grid_ref[1] < size_ref[index, 1])
        masks.append(jnp.where(inside, 0.0, NEGATIVE).astype(LOW))
    zero = jnp.zeros_like(masks[0])
    one = jnp.ones_like(masks[0])

    def tile(image, index):
        return qkv_ref[0, image * PADDED : (image + 1) * PADDED, 128 * index : 128 * (index + 1)]

    def score(image, head):
        odd = QK_ODD[head]
        mark = 0 if odd else HD
        keep = lane >= HD if odd else lane < HD
        key = jnp.where(
            keep, tile(image, K_TILE[head]), jnp.where(lane == mark, masks[image], zero)
        )
        query = jnp.where(lane == mark, one, tile(image, Q_TILE[head]))
        return dot(key, query, 1, 1) + bias_ref[head]

    def soften(scores, image, head):
        top = jnp.max(scores, axis=0, keepdims=True)
        exponent = jnp.exp(scores - top)
        total = jnp.sum(exponent, axis=0, keepdims=True)
        prob = (exponent * (1.0 / total)).astype(LOW)
        prob_ref[image, head] = prob
        return prob

    def gather(prob, image, head):
        return dot(prob, half_of(tile(image, V_TILE[head]), lane, V_ODD[head]), 0, 0)

    work = [(image, head) for image in range(images) for head in range(HEADS_LANE)]
    scores, probs, outs = {}, {}, {}
    for turn_index in range(len(work) + 2):
        if turn_index < len(work):
            scores[turn_index] = score(*work[turn_index])
        if 0 <= turn_index - 1 < len(work):
            probs[turn_index - 1] = soften(scores.pop(turn_index - 1), *work[turn_index - 1])
        done = turn_index - 2
        if done >= 0:
            image, head = work[done]
            outs[head] = gather(probs.pop(done), image, head)
            if head == HEADS_LANE - 1:
                rows = slice(image * PADDED, (image + 1) * PADDED)
                ctx_ref[rows, :128] = (outs[0] + outs[1]).astype(LOW)
                ctx_ref[rows, 128:] = outs[2].astype(LOW)


def attend(mine, sizes, normed, bias, add, gathered, images):
    rows, width = normed.shape
    heads = bias.shape[0]
    pieces, table = gathered
    return pl.pallas_call(
        functools.partial(attend_body, table, images),
        grid=(LANES,),
        in_specs=[
            pl.BlockSpec(memory_space=pltpu.SMEM),
            pl.BlockSpec(memory_space=pltpu.SMEM),
            whole((2, PADDED, 128)),
            whole(normed.shape),
            pl.BlockSpec((HEADS_LANE, PADDED, PADDED), lambda g: (g, 0, 0)),
            pl.BlockSpec((1, 1, PACK), lambda g: (g, 0, 0)),
        ]
        + [anywhere()] * len(pieces),
        out_specs=[
            pl.BlockSpec((1, rows, PACK), lambda g: (g, 0, 0)),
            pl.BlockSpec((images, HEADS_LANE, PADDED, PADDED), lambda g: (0, g, 0, 0)),
            pl.BlockSpec((rows, OUT_PACK), lambda g: (0, g)),
        ],
        out_shape=[
            jax.ShapeDtypeStruct((LANES, rows, PACK), LOW),
            jax.ShapeDtypeStruct((images, heads, PADDED, PADDED), LOW),
            jax.ShapeDtypeStruct((rows, LANES * OUT_PACK), LOW),
        ],
        scratch_shapes=[
            pltpu.VMEM((LANES, width, PACK), LOW),
            pltpu.SemaphoreType.DMA((LANES,)),
        ],
        compiler_params=params(),
        cost_estimate=cost(1.5e10, 2e7),
    )(mine, sizes, jnp.asarray(grid_places()), normed, bias, add, *pieces)


def middle_body(table, columns, me_ref, ctx_ref, x_ref, vec_ref, *refs):
    pieces = refs[:-6]
    att_ref, mid_ref, n_ref, weight_s, pad_s, sems = refs[-6:]
    step = pl.program_id(0)

    @pl.when(step == 0)
    def _():
        for group in range(LANES):
            fetch(group, table, pieces, columns, weight_s.at[group], sems.at[group], me_ref[0])
        for group in range(LANES):
            fetched(weight_s.at[group], sems.at[group])
        pad_s[...] = jnp.zeros_like(pad_s)

    total = vec_ref[4:5, :]
    for group in range(LANES):
        total = total + dot(
            ctx_ref[:, group * OUT_PACK : (group + 1) * OUT_PACK], weight_s[group], 1, 1
        )
    att_ref[...] = total.astype(LOW)
    mid = load_images(pad_s, x_ref, step) + vec_ref[5:6, :] * total
    mid_ref[...] = mid
    scaled, _ = normalise(mid)
    n_ref[...] = (scaled * vec_ref[2:3, :] + vec_ref[3:4, :]).astype(LOW)


def middle(mine, ctx, x, vectors, gathered, columns, images):
    rows = images * PADDED
    width = x.shape[1]
    pieces, table = gathered
    block = lambda: pl.BlockSpec((TWO * PADDED, width), lambda i: (i, 0))
    return pl.pallas_call(
        functools.partial(middle_body, table, columns),
        grid=(images // TWO,),
        in_specs=[
            pl.BlockSpec(memory_space=pltpu.SMEM),
            pl.BlockSpec((TWO * PADDED, LANES * OUT_PACK), lambda i: (i, 0)),
            whole(x.shape),
            whole(vectors.shape),
        ]
        + [anywhere()] * len(pieces),
        out_specs=[block(), block(), block()],
        out_shape=[
            jax.ShapeDtypeStruct((rows, width), LOW),
            jax.ShapeDtypeStruct((rows, width), FULL),
            jax.ShapeDtypeStruct((rows, width), LOW),
        ],
        scratch_shapes=[
            pltpu.VMEM((LANES, width, OUT_PACK), LOW),
            pltpu.VMEM((TWO * PADDED, width), FULL),
            pltpu.SemaphoreType.DMA((LANES,)),
        ],
        compiler_params=params(),
        cost_estimate=cost(8e9, 1.5e7),
    )(mine, ctx, x, vectors, *pieces)


def gelu_pair(values):
    density = jnp.exp(values * values * -0.5) * INV_SQRT2PI
    below = 0.5 * lax.erf(values * INV_SQRT2) + 0.5
    return values * below, below + values * density


def feed_body(blocks, layout, me_ref, n_ref, gd_ref, ub_ref, *refs):
    count = sum(part[3] for part in layout)
    pieces = refs[:count]
    out_ref, gn_ref, keep_ref, send_ref, gub_ref, nt_s, gdt_s, up_s, down_s, act_s, gh_s, sems = refs[count:]
    step = pl.program_id(0)
    place = me_ref[0]
    rows = n_ref.shape[0]
    units = up_s.shape[3]
    per = rows // blocks

    def begin(group):
        slot = group % 2
        for index, (_, table, first, number, up_at, down_at) in enumerate(layout):
            held = pieces[first : first + number]
            for target, at, kind in ((up_s, up_at, 0), (down_s, down_at, 1)):
                fetch(
                    group,
                    table,
                    held,
                    (at, at + units),
                    target.at[slot, index],
                    sems.at[slot, kind, index],
                    place,
                )

    @pl.when(step == 0)
    def _():
        begin(0)
        nt_s[...] = n_ref[...].T
        gdt_s[...] = gd_ref[...].T
        out_ref[...] = jnp.zeros_like(out_ref)
        gn_ref[...] = jnp.zeros_like(gn_ref)

    for group in range(LANES):

        @pl.when(step == group)
        def _(group=group):
            if group + 1 < LANES:
                begin(group + 1)

    now = step % 2
    parts = len(layout)
    for index in range(parts):
        for kind, target in enumerate((up_s, down_s)):
            fetched(target.at[now, index], sems.at[now, kind, index])
    up_weight = [up_s[now, index] for index in range(parts)]
    down_weight = [down_s[now, index] for index in range(parts)]
    if parts > 1:
        up_weight = [jnp.concatenate(up_weight, axis=1)]
        down_weight = [jnp.concatenate(down_weight, axis=1)]
    up_weight, down_weight = up_weight[0], down_weight[0]
    true_lane = step ^ me_ref[1]
    unit_bias = ub_ref[true_lane]
    unit_sums = jnp.zeros((8, up_weight.shape[1]), FULL)
    for block in range(blocks):
        part = slice(block * per, (block + 1) * per)
        hidden = dot(n_ref[part, :], up_weight) + unit_bias
        active, slope = gelu_pair(hidden)
        active = active.astype(LOW)
        act_s[part, :] = active
        grad = (dot(gd_ref[part, :], down_weight) * slope).astype(LOW)
        gh_s[part, :] = grad
        unit_sums = unit_sums + fold(grad.astype(FULL))
        out_ref[part, :] += dot(active, down_weight, 1, 1)
        gn_ref[part, :] += dot(grad, up_weight, 1, 1)
    gub_ref[true_lane] = jnp.sum(unit_sums, axis=0, keepdims=True)
    grad_up = dot(nt_s[...], gh_s[...]).astype(LOW)
    grad_down = dot(gdt_s[...], act_s[...]).astype(LOW)
    chunk_rows = keep_ref.shape[2]
    wide = grad_up.shape[1]
    for odd, target in enumerate((keep_ref, send_ref)):

        @pl.when(step % 2 == odd)
        def _(target=target):
            for chunk in range(CHUNKS):
                slot = reversed_bits(chunk) ^ reversed_bits(place)
                at = slice(chunk * chunk_rows, (chunk + 1) * chunk_rows)
                target[0, slot, :, :wide] = grad_up[at]
                target[0, slot, :, wide:] = grad_down[at]


def feed(mine, normed, grad_down, unit_bias, groups, units, images):
    rows, width = normed.shape
    blocks = max(1, images // 4)
    parts = len(groups)
    sub = units // parts
    pieces, layout = [], []
    for (arrays, table), up_at, down_at in groups:
        layout.append((None, table, len(pieces), len(arrays), up_at, down_at))
        pieces.extend(arrays)
    chunk_rows = width // CHUNKS
    grad_block = (1, CHUNKS, chunk_rows, 2 * units)
    grads = jax.ShapeDtypeStruct((2,) + grad_block[1:], LOW)
    return pl.pallas_call(
        functools.partial(feed_body, blocks, layout),
        grid=(LANES,),
        in_specs=[
            pl.BlockSpec(memory_space=pltpu.SMEM),
            whole((rows, width)),
            whole((rows, width)),
            whole((LANES, 1, units)),
        ]
        + [anywhere()] * len(pieces),
        out_specs=[
            whole((rows, width)),
            whole((rows, width)),
            pl.BlockSpec(grad_block, lambda j: (j // 2, 0, 0, 0)),
            pl.BlockSpec(grad_block, lambda j: (jnp.maximum(j - 1, 0) // 2, 0, 0, 0)),
            whole((LANES, 1, units)),
        ],
        out_shape=[jax.ShapeDtypeStruct((rows, width), FULL)] * 2
        + [grads] * 2
        + [jax.ShapeDtypeStruct((LANES, 1, units), FULL)],
        scratch_shapes=[
            pltpu.VMEM((width, rows), LOW),
            pltpu.VMEM((width, rows), LOW),
            pltpu.VMEM((2, parts, width, sub), LOW),
            pltpu.VMEM((2, parts, width, sub), LOW),
            pltpu.VMEM((rows, units), LOW),
            pltpu.VMEM((rows, units), LOW),
            pltpu.SemaphoreType.DMA((2, 2, parts)),
        ],
        compiler_params=params(),
        cost_estimate=cost(3.5e10, 4e7),
    )(mine, normed, grad_down, unit_bias, *pieces)


def second_body(
    me_ref, down_ref, gn_ref, mid_ref, att_ref, ctx_ref, cot_ref, vec_ref, out_ref, gm_ref, ga_ref, keep_ref, send_ref, rows_ref, pad_s, out_s, sums_s, gat_s
):
    step = pl.program_id(0)

    @pl.when(step == 0)
    def _():
        pad_s[...] = jnp.zeros_like(pad_s)
        sums_s[...] = jnp.zeros_like(sums_s)

    cot = load_images(pad_s, cot_ref, step)
    down = down_ref[...] + vec_ref[6:7, :]
    mid = mid_ref[...]
    store_images(out_ref, out_s, mid + vec_ref[7:8, :] * down, step)
    scaled, inverse = normalise(mid)
    grad_normed = gn_ref[...]
    grad_mid = cot + norm_back(grad_normed, vec_ref[2:3, :], scaled, inverse)
    gm_ref[...] = grad_mid
    grad_att = (grad_mid * vec_ref[5:6, :]).astype(LOW)
    ga_ref[...] = grad_att
    gat_s[step] = grad_att.T
    sums_s[0] += fold(grad_normed * scaled)
    sums_s[1] += fold(grad_normed)
    sums_s[2] += fold(grad_mid)
    sums_s[3] += fold(grad_mid * att_ref[...].astype(FULL))
    sums_s[4] += fold(cot)
    sums_s[5] += fold(cot * down)

    @pl.when(step == pl.num_programs(0) - 1)
    def _():
        sums = [jnp.sum(sums_s[index], axis=0, keepdims=True) for index in range(6)]
        sums[2] = sums[2] * vec_ref[5:6, :]
        sums[4] = sums[4] * vec_ref[7:8, :]
        for index in range(6):
            rows_ref[index : index + 1, :] = sums[index]
        images = gat_s.shape[0]
        for group in range(LANES):
            at = slice(group * OUT_PACK, (group + 1) * OUT_PACK)
            grad = dot(gat_s[0], ctx_ref[0:PADDED, at])
            for image in range(1, images):
                grad = grad + dot(
                    gat_s[image], ctx_ref[image * PADDED : (image + 1) * PADDED, at]
                )
            give(me_ref[0], keep_ref, send_ref, group, grad.astype(LOW))


def give(place, keep_ref, send_ref, group, grad):
    rows = keep_ref.shape[2]
    mine = reversed_bits(place)
    target = (keep_ref, send_ref)[group % 2]
    for chunk in range(CHUNKS):
        target[group // 2, reversed_bits(chunk) ^ mine] = grad[chunk * rows : (chunk + 1) * rows]


def second_back(mine, down, grad_normed, mid, att, ctx, cot, vectors, images):
    rows, width = mid.shape
    block = lambda: pl.BlockSpec((PADDED, width), lambda i: (i, 0))
    grads = (2, CHUNKS, width // CHUNKS, OUT_PACK)
    return pl.pallas_call(
        second_body,
        grid=(images,),
        in_specs=[
            pl.BlockSpec(memory_space=pltpu.SMEM),
            block(),
            block(),
            block(),
            block(),
            whole(ctx.shape),
            whole(cot.shape),
            whole(vectors.shape),
        ],
        out_specs=[whole(cot.shape), block(), block(), whole(grads), whole(grads), whole((6, width))],
        out_shape=[
            jax.ShapeDtypeStruct(cot.shape, FULL),
            jax.ShapeDtypeStruct((rows, width), FULL),
            jax.ShapeDtypeStruct((rows, width), LOW),
            jax.ShapeDtypeStruct(grads, LOW),
            jax.ShapeDtypeStruct(grads, LOW),
            jax.ShapeDtypeStruct((6, width), FULL),
        ],
        scratch_shapes=[
            pltpu.VMEM((PADDED, width), FULL),
            pltpu.VMEM((PADDED, width), FULL),
            pltpu.VMEM((6, 8, width), FULL),
            pltpu.VMEM((images, width, PADDED), LOW),
        ],
        compiler_params=params(),
        cost_estimate=cost(1e10, 2e7),
    )(mine, down, grad_normed, mid, att, ctx, cot, vectors)


def back_body(table, columns, images, me_ref, ga_ref, qkv_ref, prob_ref, *refs):
    pieces = refs[:-6]
    dqkv_ref, pair_ref, cols_ref, weight_s, gc_s, sems = refs[-6:]
    step = pl.program_id(0)

    @pl.when(step == 0)
    def _():
        for group in range(LANES):
            fetch(group, table, pieces, columns, weight_s.at[group], sems.at[group], me_ref[0])

    fetched(weight_s.at[step], sems.at[step])
    gc_s[...] = dot(ga_ref[...], weight_s[step]).astype(LOW)
    lane = halves()

    def tile(image, index):
        return qkv_ref[0, image * PADDED : (image + 1) * PADDED, 128 * index : 128 * (index + 1)]

    def upstream(image, head):
        at = 128 if head == 2 else 0
        value = gc_s[image * PADDED : (image + 1) * PADDED, at : at + 128]
        return half_of(value, lane, V_ODD[head])

    def first(image, head):
        return dot(tile(image, V_TILE[head]), upstream(image, head), 1, 1)

    def second(grad_prob, image, head):
        soft = prob_ref[image, head].astype(FULL)
        weighted = soft * grad_prob
        inner = jnp.sum(weighted, axis=0, keepdims=True)
        grad_score = weighted - soft * inner
        if image == 0:
            pair_ref[head] = grad_score
        else:
            pair_ref[head] += grad_score
        return grad_score.astype(LOW)

    def third(low_score, image, head):
        odd = QK_ODD[head]
        return (
            dot(low_score, half_of(tile(image, K_TILE[head]), lane, odd), 0, 0) * HD**-0.5,
            dot(low_score, half_of(tile(image, Q_TILE[head]), lane, odd)),
            dot(prob_ref[image, head], upstream(image, head)),
        )

    work = [(image, head) for image in range(images) for head in range(HEADS_LANE)]
    probs, scores, grads = {}, {}, {}
    sums = [jnp.zeros((8, 128), FULL)] * 3
    for turn_index in range(len(work) + 2):
        if turn_index < len(work):
            probs[turn_index] = first(*work[turn_index])
        if 0 <= turn_index - 1 < len(work):
            scores[turn_index - 1] = second(probs.pop(turn_index - 1), *work[turn_index - 1])
        done = turn_index - 2
        if done < 0:
            continue
        image, head = work[done]
        grads[head] = third(scores.pop(done), image, head)
        if head < HEADS_LANE - 1:
            continue
        packed = (
            grads[0][0] + grads[1][0],
            grads[2][0] + grads[2][2],
            grads[0][2] + grads[1][2],
            grads[0][1] + grads[1][1],
            grads[2][1],
        )
        rows = slice(image * PADDED, (image + 1) * PADDED)
        for index, value in enumerate(packed):
            low_value = value.astype(LOW)
            dqkv_ref[0, rows, 128 * index : 128 * (index + 1)] = low_value
            if index < 3:
                sums[index] = sums[index] + fold(low_value.astype(FULL))
    for index in range(3):
        cols_ref[0, :, 128 * index : 128 * (index + 1)] = sums[index]


def back(mine, grad_att, qkv, prob, gathered, columns, images):
    rows, width = grad_att.shape
    heads = prob.shape[1]
    pieces, table = gathered
    return pl.pallas_call(
        functools.partial(back_body, table, columns, images),
        grid=(LANES,),
        in_specs=[
            pl.BlockSpec(memory_space=pltpu.SMEM),
            whole(grad_att.shape),
            pl.BlockSpec((1, rows, PACK), lambda g: (g, 0, 0)),
            pl.BlockSpec((images, HEADS_LANE, PADDED, PADDED), lambda g: (0, g, 0, 0)),
        ]
        + [anywhere()] * len(pieces),
        out_specs=[
            pl.BlockSpec((1, rows, PACK), lambda g: (g, 0, 0)),
            pl.BlockSpec((HEADS_LANE, PADDED, PADDED), lambda g: (g, 0, 0)),
            pl.BlockSpec((1, 8, 384), lambda g: (g, 0, 0)),
        ],
        out_shape=[
            jax.ShapeDtypeStruct((LANES, rows, PACK), LOW),
            jax.ShapeDtypeStruct((heads, PADDED, PADDED), FULL),
            jax.ShapeDtypeStruct((LANES, 8, 384), FULL),
        ],
        scratch_shapes=[
            pltpu.VMEM((LANES, width, OUT_PACK), LOW),
            pltpu.VMEM((rows, OUT_PACK), LOW),
            pltpu.SemaphoreType.DMA((LANES,)),
        ],
        compiler_params=params(),
        cost_estimate=cost(3e10, 4e7),
    )(mine, grad_att, qkv, prob, *pieces)


def heads_body(pair_ref, cols_ref, thin_ref, heads_ref, spread_s, flat_s):
    heads = pair_ref.shape[0]
    spread_s[...] = jnp.zeros_like(spread_s)

    def head_sum(index, carry):
        for row in range(GRID):
            at = GRID * (GRID - 1 - row)
            spread_s[index, :, at : at + PATCHES] += pair_ref[
                index, row * GRID : (row + 1) * GRID, 0:PATCHES
            ]
        return carry

    lax.fori_loop(0, heads, head_sum, 0)
    for col in range(GRID):
        flat_s[16 * col : 16 * (col + 1), :] = spread_s[:, col, :]
    wide = exact_dot(flat_s[...], thin_ref[...], 1)
    table = jnp.zeros((16, TABLE), FULL)
    for col in range(GRID):
        table = table + turn(wide[16 * col : 16 * (col + 1)], GRID - 1 - col)
    for group in range(LANES):
        cols = jnp.sum(cols_ref[group], axis=0, keepdims=True)
        for head in range(HEADS_LANE):
            at = HD * (4 + head if head < 2 else 3)
            heads_ref[group, head : head + 1, 0:HD] = cols[:, HD * head : HD * (head + 1)]
            heads_ref[group, head : head + 1, HD : 2 * HD] = cols[:, at : at + HD]
        first = group * HEADS_LANE
        heads_ref[group, :, 2 * HD :] = table[first : first + HEADS_LANE, 0 : SPAN * SPAN]


def heads_back(pair, cols, thin):
    heads = pair.shape[0]
    return pl.pallas_call(
        heads_body,
        out_shape=jax.ShapeDtypeStruct((LANES, HEADS_LANE, 2 * HD + SPAN * SPAN), FULL),
        scratch_shapes=[
            pltpu.VMEM((16, GRID, SPREAD), FULL),
            pltpu.VMEM((16 * GRID, SPREAD), FULL),
        ],
        compiler_params=params(),
        cost_estimate=cost(3e9, 4e6),
    )(pair, cols, thin)


def project_body(me_ref, n_ref, dqkv_ref, keep_ref, send_ref, t_s):
    t_s[...] = n_ref[...].T
    for group in range(LANES):
        give(me_ref[0], keep_ref, send_ref, group, dot(t_s[...], dqkv_ref[group]).astype(LOW))


def project(mine, normed, dqkv):
    rows, width = normed.shape
    grads = jax.ShapeDtypeStruct((2, CHUNKS, width // CHUNKS, PACK), LOW)
    return pl.pallas_call(
        project_body,
        in_specs=[pl.BlockSpec(memory_space=pltpu.SMEM)] + [pl.BlockSpec(memory_space=pltpu.VMEM)] * 2,
        out_shape=[grads, grads],
        scratch_shapes=[pltpu.VMEM((width, rows), LOW)],
        compiler_params=params(),
        cost_estimate=cost(8e9, 1e7),
    )(mine, normed, dqkv)


def input_body(table, me_ref, dqkv_ref, gm_ref, x_ref, vec_ref, *refs):
    pieces = refs[:-7]
    out_ref, rows_ref, weight_s, pad_s, out_s, sums_s, sems = refs[-7:]
    step = pl.program_id(0)

    @pl.when(step == 0)
    def _():
        for group in range(LANES):
            fetch(group, table, pieces, (0, PACK), weight_s.at[group], sems.at[group], me_ref[0])
        pad_s[...] = jnp.zeros_like(pad_s)
        sums_s[...] = jnp.zeros_like(sums_s)
        for group in range(LANES):
            fetched(weight_s.at[group], sems.at[group])

    scaled, inverse = normalise(load_images(pad_s, x_ref, step))
    grad = dot(dqkv_ref[0], weight_s[0], 1, 1)
    for group in range(1, LANES):
        grad = grad + dot(dqkv_ref[group], weight_s[group], 1, 1)
    sums_s[0] += fold(grad * scaled)
    sums_s[1] += fold(grad)
    for index in range(2):
        rows_ref[index : index + 1, :] = jnp.sum(sums_s[index], axis=0, keepdims=True)
    result = gm_ref[...] + norm_back(grad, vec_ref[0:1, :], scaled, inverse)
    store_images(out_ref, out_s, result, step)


def input_back(mine, dqkv, grad_mid, x, vectors, gathered, images):
    width = x.shape[1]
    pieces, table = gathered
    return pl.pallas_call(
        functools.partial(input_body, table),
        grid=(images // TWO,),
        in_specs=[
            pl.BlockSpec(memory_space=pltpu.SMEM),
            pl.BlockSpec((LANES, TWO * PADDED, PACK), lambda i: (0, i, 0)),
            pl.BlockSpec((TWO * PADDED, width), lambda i: (i, 0)),
            whole(x.shape),
            whole(vectors.shape),
        ]
        + [anywhere()] * len(pieces),
        out_specs=[whole(x.shape), whole((2, width))],
        out_shape=[jax.ShapeDtypeStruct(x.shape, FULL), jax.ShapeDtypeStruct((2, width), FULL)],
        scratch_shapes=[
            pltpu.VMEM((LANES, width, PACK), LOW),
            pltpu.VMEM((TWO * PADDED, width), FULL),
            pltpu.VMEM((TWO * PADDED, width), FULL),
            pltpu.VMEM((2, 8, width), FULL),
            pltpu.SemaphoreType.DMA((LANES,)),
        ],
        compiler_params=params(),
        cost_estimate=cost(1.5e10, 1.5e7),
    )(mine, dqkv, grad_mid, x, vectors, *pieces)


def swap(values, axis, bit):
    count = lax.axis_size(axis)
    return lax.ppermute(values, axis, [(index, index ^ bit) for index in range(count)])


def after(values, *others):
    return lax.optimization_barrier((values,) + others)[0]


def sync(*values):
    return lax.optimization_barrier(values)


def join(former, latter, axis=0):
    return jnp.concatenate([former, latter], axis=axis)


def split_rows(held):
    half = held.shape[1] // 2
    return held[:, :half], held[:, half:]


def pieces_of(upper, upper_x, lower, lower_y, near_core, far_core):
    arrays = [upper, upper_x, lower, lower_y, near_core[0], far_core[0], near_core[1], far_core[1]]
    half = upper.shape[1]

    def part(first, far):
        top = [(first + far, slot) for slot in range(8)]
        low = [(first + 2 + slot // 4, 4 * far + slot % 4) for slot in range(8)]
        return ((0, top), (half, low))

    return arrays, (part(0, 0), part(4, 0), part(0, 1), part(4, 1))


def total_of(terms):
    total = terms[0].astype(FULL)
    for one in terms[1:]:
        total = total + one.astype(FULL)
    return total


def sum_call(body, grid, views, outs, moved):
    return pl.pallas_call(
        body,
        grid=(grid,),
        in_specs=[pl.BlockSpec(block, index) for _, block, index in views],
        out_specs=[pl.BlockSpec(block, index) for _, _, block, index in outs],
        out_shape=[jax.ShapeDtypeStruct(shape, dtype) for shape, dtype, _, _ in outs],
        compiler_params=params(),
        cost_estimate=cost(1e6, moved),
    )(*[array for array, _, _ in views])


def sum_away(keeps, gots):
    half = keeps[0].shape[2] // 2
    wide = sum(keep.shape[3] for keep in keeps)
    views = []
    for keep, got in zip(keeps, gots):
        block = (1, 2, half, keep.shape[3])
        for array in (keep, got):
            views.append((array, block, lambda j: (1, j, 0, 0)))
            views.append((array, block, lambda j: (j // 2, 2 + j % 2, 1, 0)))

    def body(*refs):
        ins, (upper, lower) = refs[:-2], refs[-2:]
        first = 0
        for index in range(0, len(ins), 4):
            keep_u, keep_l, got_u, got_l = ins[index : index + 4]
            at = slice(first, first + keep_u.shape[3])
            first = at.stop
            upper[:, :, at] = total_of((keep_u[0], got_u[0])).astype(LOW)
            lower[0, :, :, at] = total_of((keep_l[0], got_l[0])).astype(LOW)

    outs = [
        ((8, half, wide), LOW, (2, half, wide), lambda j: (j, 0, 0)),
        ((2, 4, half, wide), LOW, (1, 2, half, wide), lambda j: (j // 2, j % 2, 0, 0)),
    ]
    return sum_call(body, 4, views, outs, 8e6)


def sum_here(keeps, gots, upper_got, lower_got):
    half = keeps[0].shape[2] // 2
    wide = sum(keep.shape[3] for keep in keeps)
    places = (
        lambda j: (0, j, 0, 0),
        lambda j: (0, 2 + j, 0, 0),
        lambda j: (0, j, 1, 0),
        lambda j: (1, j, 1, 0),
    )
    views = [
        (upper_got, (2, half, wide), lambda j: (j, 0, 0)),
        (upper_got, (2, half, wide), lambda j: (2 + j, 0, 0)),
        (lower_got, (1, 2, half, wide), lambda j: (0, j, 0, 0)),
        (lower_got, (1, 2, half, wide), lambda j: (1, j, 0, 0)),
    ]
    for keep, got in zip(keeps, gots):
        for array in (keep, got):
            views.extend((array, (1, 2, half, keep.shape[3]), place) for place in places)

    def body(*refs):
        far, ins, outs = refs[:4], refs[4:-4], refs[-4:]
        first = 0
        for index in range(0, len(ins), 8):
            at = slice(first, first + ins[index].shape[3])
            first = at.stop
            for view in range(4):
                came = far[view][:, :, at] if view < 2 else far[view][0, :, :, at]
                terms = (ins[index + view][0], ins[index + 4 + view][0], came)
                outs[view][:, :, at] = total_of(terms).astype(outs[view].dtype)

    outs = [
        ((4, half, wide), dtype, (2, half, wide), lambda j: (j, 0, 0))
        for dtype in (FULL, LOW, FULL, LOW)
    ]
    return sum_call(body, 2, views, outs, 1.2e7)


def sum_line(upper, upper_got, lower, lower_got):
    half, wide = upper.shape[1:]
    views = []
    for array in (upper, upper_got, lower, lower_got):
        views.append((array, (1, half, wide), lambda j: (j, 0, 0)))
        views.append((array, (1, half, wide), lambda j: (2 + j, 0, 0)))

    def body(*refs):
        for side in range(2):
            out = refs[8 + side]
            out[0, :half] = total_of((refs[side][0], refs[2 + side][0])).astype(out.dtype)
            out[0, half:] = total_of((refs[4 + side][0], refs[6 + side][0])).astype(out.dtype)

    outs = [
        ((2, 2 * half, wide), dtype, (1, 2 * half, wide), lambda j: (j, 0, 0))
        for dtype in (FULL, LOW)
    ]
    return sum_call(body, 2, views, outs, 6e6)


def adam(weight, moment_one, moment_two, incoming, step_rate, decay_rate):
    first_new = BETA_ONE * moment_one + (1.0 - BETA_ONE) * incoming
    second_new = BETA_TWO * moment_two + (1.0 - BETA_TWO) * incoming * incoming
    update = (
        first_new
        / (1.0 - BETA_ONE**STEP)
        / (jnp.sqrt(second_new / (1.0 - BETA_TWO**STEP)) + ADAM_EPSILON)
    )
    return (second_new, weight * (1.0 - step_rate * decay_rate) - step_rate * update)


def pack_attention(weights):
    query, key, value, out = (weights[index] for index in range(4))
    rows = query.shape[0]
    blank = jnp.zeros((rows, HD), weights.dtype)
    first = jnp.concatenate([query, value[:, 128:], value[:, :128], key, blank], axis=1)
    last = jnp.concatenate([out[:, :128], blank, out[:, 128:]], axis=1)
    return first, last


def unpack_attention(first, last):
    query = first[:, :192]
    value = jnp.concatenate([first[:, 256:384], first[:, 192:256]], axis=1)
    key = first[:, 384:576]
    out = jnp.concatenate([last[:, :128], last[:, 192:]], axis=1)
    return jnp.stack([query, key, value, out])


def shards(
    block_input,
    cotangent,
    image_size,
    attention_weights,
    attention_first,
    attention_second,
    mlp_weights,
    mlp_first,
    mlp_second,
    head_params,
    head_first,
    head_second,
    norm_params,
    norm_first,
    norm_second,
):
    near = lax.axis_size("dp") == CHUNKS
    lane_index = lax.axis_index("mp")
    local_rows, width = block_input.shape
    images = local_rows // PATCHES
    local_heads = head_params.shape[0]
    chunk_rows = width // CHUNKS
    thin = jnp.asarray(thin_matrix(), LOW)

    first, last = pack_attention(attention_weights.astype(LOW))
    mlp_low = mlp_weights.astype(LOW)
    units = mlp_low.shape[2]
    unit_bias = norm_params[8:].reshape(LANES, 1, units)
    first = jnp.concatenate([first, last], axis=1)
    second = jnp.concatenate([mlp_low[0], mlp_low[1]], axis=1)
    out_at = (PACK, PACK + OUT_PACK)
    if near:
        mine = jnp.stack([lax.axis_index("dp"), lane_index, lane_index]).astype(jnp.int32)
        core = lambda values: swap(values, "mp", 1)
        x_axis = lambda values: swap(values, "mp", 2)
        y_axis = lambda values: swap(values, "dp", 1)
        z_near = lambda values: swap(values, "dp", 2)
        z_far = lambda values: swap(values, "dp", 4)
        one, two = first[None], second[None]
        got = z_far(one)
        normed_one, grad_down = first_norm(block_input, cotangent, norm_params, images)
        got, normed_one, other = sync(got, normed_one, x_axis(after(head_params, first)))
        one = join(one, got)
        got = z_near(one)
        two_got = z_far(after(two, one))
        got, near_table, far_table = sync(got, core(head_params), core(other))
        upper, lower = split_rows(join(one, got))
        upper, lower = sync(upper, lower)
        upper_got, lower_got = y_axis(upper), x_axis(lower)
        upper_got, lower_got = sync(upper_got, lower_got)
        upper, lower = sync(join(upper, upper_got), join(lower, lower_got))
        upper_far, lower_far = x_axis(upper), y_axis(lower)
        two = join(two, after(two_got, upper, lower))
        two_got = z_near(two)
        bias, add = spread_bias(
            (head_params, after(near_table, two), other, after(far_table, two)), thin
        )
        near_core = sync(core(upper), core(lower))
        upper_far, lower_far, two_got, bias = sync(
            upper_far, lower_far, after(two_got, *near_core), bias
        )
        far_core = sync(core(upper_far), core(lower_far))
        first_all = pieces_of(upper, upper_far, lower, lower_far, near_core, far_core)
        two_upper, two_lower = split_rows(join(two, two_got))
        two_upper, two_lower, normed_one = sync(two_upper, two_lower, normed_one)
        two_upper_got, two_lower_got = y_axis(two_upper), x_axis(two_lower)
    else:
        mine = jnp.stack([0 * lane_index, 0 * lane_index, lane_index]).astype(jnp.int32)

        def gather_far(piece):
            full = lax.all_gather(piece, "dp", axis=0, tiled=True)
            full = lax.all_gather(full, "mp", axis=0, tiled=False)
            full = full.reshape(LANES, CHUNKS, chunk_rows, piece.shape[1])
            order = [reversed_bits(index) for index in range(CHUNKS)]
            full = jnp.stack([full[:, index] for index in order], axis=1)
            slots = range(CHUNKS)
            table = tuple(((0, [(group, slot) for slot in slots]),) for group in range(LANES))
            return [full[index] for index in range(LANES)], table

        tables = lax.all_gather(head_params, "mp", axis=0, tiled=False)
        tables = tuple(tables[index] for index in range(LANES))
        normed_one, grad_down = first_norm(block_input, cotangent, norm_params, images)
        bias, add = spread_bias(tables, thin)
        first_all = gather_far(first)
        second_all = gather_far(second)

    qkv, prob, ctx = attend(mine, image_size, normed_one, bias, add, first_all, images)
    if near:
        ctx, two_upper_got, two_lower_got = sync(ctx, two_upper_got, two_lower_got)
        two_upper, two_lower, ctx = sync(
            join(two_upper, two_upper_got), join(two_lower, two_lower_got), ctx
        )
        near_two = (core(two_upper), core(two_lower))
        far_two = (x_axis(two_upper), y_axis(two_lower))
    att, mid, normed_two = middle(
        mine, ctx, block_input, norm_params, first_all, out_at, images
    )
    if near:
        normed_two, *far_two = sync(normed_two, *far_two, *near_two)
        far_two, near_two = far_two[:2], far_two[2:]
        second_all = pieces_of(
            two_upper,
            far_two[0],
            two_lower,
            far_two[1],
            near_two,
            sync(core(far_two[0]), core(far_two[1])),
        )
    groups = ((second_all, 0, units),)
    down, grad_normed, keep_mlp, send_mlp, unit_sums = feed(
        mine, normed_two, grad_down, unit_bias, groups, units, images
    )
    if near:
        mlp_core = core(send_mlp)
    output, grad_mid, grad_att, keep_out, send_out, second_rows = second_back(
        mine, down, grad_normed, mid, att, ctx, cotangent, norm_params, images
    )
    if near:
        mlp_core, grad_att, send_out = sync(mlp_core, grad_att, send_out)
        keeps, gots = (keep_mlp, keep_out), (mlp_core, core(send_out))
        upper, lower, grad_att = sync(*sum_away(keeps, gots), grad_att)
        upper_got, lower_got = x_axis(upper), y_axis(lower)
    dqkv, pair, cols = back(
        mine, grad_att, qkv, prob, first_all, out_at, images
    )
    keep_att, send_att = project(mine, normed_one, dqkv)
    grad_heads = heads_back(after(pair, keep_att), cols, thin)
    if near:
        keep_att, send_att, upper_got, lower_got, grad_heads = sync(
            keep_att, send_att, upper_got, lower_got, grad_heads
        )
        att_core = core(send_att)
        upper, upper_away, lower, lower_away = sum_here(keeps, gots, upper_got, lower_got)
        upper_away, lower_away, att_core = sync(upper_away, lower_away, att_core)
        upper_got, lower_got = y_axis(upper_away), x_axis(lower_away)
        keeps, gots = (keep_att,), (att_core,)
        att_upper, att_lower, dqkv = sync(*sum_away(keeps, gots), dqkv)
        att_upper_got, att_lower_got = x_axis(att_upper), y_axis(att_lower)
    grad_input, first_rows = input_back(
        mine, dqkv, grad_mid, block_input, norm_params, first_all, images
    )
    norms = jnp.concatenate([first_rows, second_rows, unit_sums.reshape(-1, width)], axis=0)
    if near:
        count = norms.shape[0]
        rest = count + local_heads
        norms, *heads = sync(norms, *[grad_heads[index] for index in range(LANES)])
        norms = jnp.pad(norms, ((0, 0), (0, grad_heads.shape[2] - width)))
        keep = jnp.concatenate([norms, heads[0], heads[2]], axis=0)
        small_got = core(jnp.concatenate([norms, heads[1], heads[3]], axis=0))
        upper_got, lower_got, small_got = sync(upper_got, lower_got, small_got)
        line, line_away = sum_line(upper, upper_got, lower, lower_got)
        line_got = z_near(line_away)
        small = keep + small_got
        small_got = x_axis(join(small[:count], small[rest:]))
        upper_got, lower_got, line_away, small_got = sync(
            att_upper_got, att_lower_got, line_away, small_got
        )
        small = small[:rest] + small_got
        upper, upper_away, lower, lower_away = sum_here(keeps, gots, upper_got, lower_got)
        upper_away, lower_away, small = sync(upper_away, lower_away, small)
        upper_got, lower_got = y_axis(upper_away), x_axis(lower_away)
        small_got = y_axis(small)
        here, away = sum_line(upper, upper_got, lower, lower_got)
        small_got, line_got, away = sync(small_got, line_got, away)
        line = line + line_got.astype(FULL)
        small, line_away = sync(small + small_got, line[1].astype(LOW))
        got, line_got = z_near(away), z_far(line_away)
        got, line_got, small = sync(got, line_got, small)
        came = (z_near(small), z_far(small), swap(small, "dp", 6))
        here = here + got.astype(FULL)
        got = z_far(here[1].astype(LOW))
        small = (small + came[0]) + (came[1] + came[2])
        sum_mlp = line[0] + line_got.astype(FULL)
        sum_att = here[0] + got.astype(FULL)
        sum_mlp, sum_out = sum_mlp[:, : 2 * units], sum_mlp[:, 2 * units :]
        reduced_norms = small[:count, :width]
        reduced_heads = small[count:]
    else:
        reduced_norms = lax.psum(norms, ("dp", "mp"))
        reduced_heads = lax.psum_scatter(
            lax.psum(grad_heads, "dp"), "mp", scatter_dimension=0, tiled=False
        )

        def scatter_far(keep, send):
            terms = jnp.stack([keep[0], send[0], keep[1], send[1]])
            order = [reversed_bits(index) for index in range(CHUNKS)]
            terms = jnp.stack([terms[:, index] for index in order], axis=1)
            terms = terms.reshape(LANES, width, terms.shape[-1])
            mine_only = lax.psum_scatter(terms, "mp", scatter_dimension=0, tiled=False)
            return lax.psum_scatter(
                mine_only.astype(FULL), "dp", scatter_dimension=0, tiled=True
            )

        sum_mlp = scatter_far(keep_mlp, send_mlp)
        sum_out = scatter_far(keep_out, send_out)
        sum_att = scatter_far(keep_att, send_att)

    reduced_attention = unpack_attention(sum_att, sum_out)
    reduced_mlp = jnp.stack([sum_mlp[:, :units], sum_mlp[:, units:]])
    attention_second_new, attention_new = adam(
        attention_weights,
        attention_first,
        attention_second,
        reduced_attention,
        RATE_MATRIX,
        DECAY_MATRIX,
    )
    mlp_second_new, mlp_new = adam(
        mlp_weights, mlp_first, mlp_second, reduced_mlp, RATE_MATRIX, DECAY_MATRIX
    )
    head_second_new, head_new = adam(
        head_params, head_first, head_second, reduced_heads, RATE_VECTOR, 0.0
    )
    norm_second_new, norm_new = adam(
        norm_params, norm_first, norm_second, reduced_norms, RATE_VECTOR, 0.0
    )
    return (
        output,
        grad_input,
        reduced_attention,
        attention_second_new,
        attention_new,
        reduced_mlp,
        mlp_second_new,
        mlp_new,
        reduced_heads,
        head_second_new,
        head_new,
        reduced_norms,
        norm_second_new,
        norm_new,
    )


def solution(mesh):
    rows = P(("dp", "mp"), None)
    matrix = P(None, "dp", "mp")
    head = P("mp", None)
    placed = (rows, rows, P("dp", None)) + (matrix,) * 6 + (head,) * 3 + (P(),) * 3
    given = (rows, rows) + (matrix,) * 6 + (head,) * 3 + (P(),) * 3
    return jax.shard_map(shards, mesh=mesh, in_specs=placed, out_specs=given, check_vma=False)
```

```python
import functools

import jax
import jax.numpy as jnp
import numpy as np
from jax import lax
from jax.experimental import pallas as pl
from jax.experimental.pallas import tpu as pltpu
from jax.sharding import PartitionSpec as P

HD = 64
GRID = 14
SPAN = 2 * GRID - 1
STEP = 10
PATCHES = 196
PADDED = 208
PACK = 640
OUT_PACK = 256
CHUNKS = 8
LANES = 4
HEADS_LANE = 3
TWO = 2
TABLE = 768
SPREAD = 384

EPSILON = 1e-06
NEGATIVE = -1e30
BETA_ONE = 0.9
BETA_TWO = 0.999
ADAM_EPSILON = 1e-08
RATE_MATRIX = 0.05
RATE_VECTOR = 0.4
DECAY_MATRIX = 0.05

LOW = jnp.bfloat16
FULL = jnp.float32
INV_SQRT2 = 0.7071067811865476
INV_SQRT2PI = 0.3989422804014327
VMEM_LIMIT = 60 << 20


def dot(former, latter, former_dim=1, latter_dim=0):
    return lax.dot_general(
        former,
        latter,
        (((former_dim,), (latter_dim,)), ((), ())),
        preferred_element_type=FULL,
    )


def normalise(values):
    row_mean = jnp.mean(values, axis=-1, keepdims=True)
    centre = values - row_mean
    variance = jnp.mean(centre * centre, axis=-1, keepdims=True)
    inverse = lax.rsqrt(variance + EPSILON)
    return centre * inverse, inverse


def norm_back(incoming, norm_gain, scaled, inverse):
    weighted = incoming * norm_gain
    centred = weighted - jnp.mean(weighted, axis=-1, keepdims=True)
    return inverse * (centred - scaled * jnp.mean(weighted * scaled, axis=-1, keepdims=True))


def fold(values):
    rows, cols = values.shape
    return jnp.sum(values.reshape(rows // 8, 8, cols), axis=0)


def reversed_bits(index):
    return (index & 1) * 4 + (index & 2) + (index & 4) // 4


def whole(shape):
    zeros = (0,) * len(shape)
    return pl.BlockSpec(tuple(shape), lambda *_: zeros)


def params():
    return pltpu.CompilerParams(vmem_limit_bytes=VMEM_LIMIT)


def cost(flops, moved):
    return pl.CostEstimate(flops=int(flops), bytes_accessed=int(moved), transcendentals=0)


def fetch(group, table, refs, columns, target, sem, place):
    for rows, part in table[group]:
        for slot, (source, lead) in enumerate(part):
            height = refs[source].shape[1]
            chunk = target.shape[0] // CHUNKS
            start = (reversed_bits(slot) ^ place) * chunk + rows
            pltpu.make_async_copy(
                refs[source].at[lead, :, columns[0] : columns[1]],
                target.at[pl.ds(pl.multiple_of(start, 16), height), :],
                sem,
            ).start()


def fetched(target, sem):
    pltpu.make_async_copy(target, target, sem).wait()


def anywhere():
    return pl.BlockSpec(memory_space=pl.ANY)


def load_images(pad, source, step):
    count = pad.shape[0] // PADDED
    for first in range(0, source.shape[0] // PATCHES, count):

        @pl.when(step == first // count)
        def _(first=first):
            for index in range(count):
                at = (first + index) * PATCHES
                pad[index * PADDED : index * PADDED + PATCHES, :] = source[at : at + PATCHES, :]

    return pad[...]


def store_images(target, pad, value, step):
    count = pad.shape[0] // PADDED
    pad[...] = value
    for first in range(0, target.shape[0] // PATCHES, count):

        @pl.when(step == first // count)
        def _(first=first):
            for index in range(count):
                at = (first + index) * PATCHES
                target[at : at + PATCHES, :] = pad[index * PADDED : index * PADDED + PATCHES, :]


def first_norm_body(images, x_ref, cot_ref, vec_ref, normed_ref, gd_ref, pad_s):
    pad_s[...] = jnp.zeros_like(pad_s)
    for image in range(images):
        rows = slice(image * PATCHES, (image + 1) * PATCHES)
        target = slice(image * PADDED, (image + 1) * PADDED)
        scaled, _ = normalise(x_ref[rows, :])
        pad_s[0:PATCHES, :] = scaled * vec_ref[0:1, :] + vec_ref[1:2, :]
        normed_ref[target, :] = pad_s[...].astype(LOW)
        pad_s[0:PATCHES, :] = cot_ref[rows, :] * vec_ref[7:8, :]
        gd_ref[target, :] = pad_s[...].astype(LOW)


def first_norm(x, cot, vectors, images):
    width = x.shape[1]
    return pl.pallas_call(
        functools.partial(first_norm_body, images),
        out_shape=[jax.ShapeDtypeStruct((images * PADDED, width), LOW)] * 2,
        scratch_shapes=[pltpu.VMEM((PADDED, width), FULL)],
        compiler_params=params(),
        cost_estimate=cost(3e9, 4e6),
    )(x, cot, vectors)


def thin_matrix():
    matrix = np.zeros((TABLE, SPREAD), np.float32)
    for row in range(SPAN):
        for col in range(GRID):
            matrix[row * SPAN + col, row * GRID + col] = 1.0
    return matrix


def exact_dot(values, onehot, latter_dim=0):
    high = values.astype(LOW)
    rest = values - high.astype(FULL)
    mid = rest.astype(LOW)
    low = (rest - mid.astype(FULL)).astype(LOW)
    return (
        dot(high, onehot, 1, latter_dim)
        + dot(mid, onehot, 1, latter_dim)
        + dot(low, onehot, 1, latter_dim)
    )


def turn(values, shift):
    return pltpu.roll(values, shift % values.shape[1], 1)


def bias_body(t0, t1, t2, t3, thin_ref, bias_ref, add_ref, table_s, turned_s, spread_s):
    table_s[...] = jnp.zeros_like(table_s)
    for group, table in enumerate((t0, t1, t2, t3)):
        heads = slice(group * HEADS_LANE, (group + 1) * HEADS_LANE)
        table_s[heads, 0 : SPAN * SPAN] = table[:, 2 * HD :]
        rows = [table[head : head + 1, :HD] for head in range(HEADS_LANE)]
        more = [table[head : head + 1, HD : 2 * HD] for head in range(HEADS_LANE)]
        add_ref[group] = jnp.concatenate(
            rows + [more[2], more[0], more[1], jnp.zeros((1, PACK - 384), FULL)], axis=1
        )
    table = table_s[...]
    for col in range(GRID):
        turned_s[16 * col : 16 * (col + 1), :] = turn(table, col - (GRID - 1))
    spread = exact_dot(turned_s[...], thin_ref[...])
    for col in range(GRID):
        spread_s[:, col, :] = spread[16 * col : 16 * (col + 1)]

    def head(index, carry):
        bias_ref[index] = jnp.zeros(bias_ref.shape[1:], FULL)
        for row in range(GRID):
            start = GRID * (GRID - 1 - row)
            bias_ref[index, row * GRID : (row + 1) * GRID, 0:PATCHES] = spread_s[
                index, :, start : start + PATCHES
            ]
        return carry

    lax.fori_loop(0, bias_ref.shape[0], head, 0)


def spread_bias(tables, thin):
    heads = LANES * HEADS_LANE
    return pl.pallas_call(
        bias_body,
        out_shape=[
            jax.ShapeDtypeStruct((heads, PADDED, PADDED), FULL),
            jax.ShapeDtypeStruct((LANES, 1, PACK), FULL),
        ],
        scratch_shapes=[
            pltpu.VMEM((16, TABLE), FULL),
            pltpu.VMEM((16 * GRID, TABLE), FULL),
            pltpu.VMEM((16, GRID, SPREAD), FULL),
        ],
        compiler_params=params(),
        cost_estimate=cost(3e9, 4e6),
    )(*tables, thin)


Q_TILE = (0, 0, 1)
K_TILE = (3, 3, 4)
V_TILE = (2, 2, 1)
QK_ODD = (False, True, False)
V_ODD = (False, True, True)


def grid_places():
    position = np.arange(PADDED)
    row = np.where(position < PATCHES, position // GRID, 4 * GRID)
    places = np.stack([row, position % GRID]).astype(np.int32)
    return np.broadcast_to(places[:, :, None], (2, PADDED, 128)).copy()


def halves():
    lane = lax.broadcasted_iota(jnp.int32, (PADDED, 128), 1)
    return lane


def half_of(value, lane, odd):
    keep = lane >= HD if odd else lane < HD
    return jnp.where(keep, value, jnp.zeros_like(value))


def attend_body(table, images, me_ref, size_ref, grid_ref, n_ref, bias_ref, add_ref, *refs):
    pieces = refs[:-5]
    qkv_ref, prob_ref, ctx_ref, weight_s, sems = refs[-5:]
    step = pl.program_id(0)

    @pl.when(step == 0)
    def _():
        for group in range(LANES):
            fetch(group, table, pieces, (0, PACK), weight_s.at[group], sems.at[group], me_ref[0])

    fetched(weight_s.at[step], sems.at[step])
    scale = jnp.where(
        lax.broadcasted_iota(jnp.int32, (1, PACK), 1) < HEADS_LANE * HD, HD**-0.5, 1.0
    )
    acc = dot(n_ref[...], weight_s[step])
    qkv_ref[0] = ((acc + add_ref[0]) * scale).astype(LOW)

    lane = halves()
    masks = []
    for image in range(images):
        index = me_ref[2] * images + image
        inside = (grid_ref[0] < size_ref[index, 0]) & (grid_ref[1] < size_ref[index, 1])
        masks.append(jnp.where(inside, 0.0, NEGATIVE).astype(LOW))
    zero = jnp.zeros_like(masks[0])
    one = jnp.ones_like(masks[0])

    def tile(image, index):
        return qkv_ref[0, image * PADDED : (image + 1) * PADDED, 128 * index : 128 * (index + 1)]

    def score(image, head):
        odd = QK_ODD[head]
        mark = 0 if odd else HD
        keep = lane >= HD if odd else lane < HD
        key = jnp.where(
            keep, tile(image, K_TILE[head]), jnp.where(lane == mark, masks[image], zero)
        )
        query = jnp.where(lane == mark, one, tile(image, Q_TILE[head]))
        return dot(key, query, 1, 1) + bias_ref[head]

    def soften(scores, image, head):
        top = jnp.max(scores, axis=0, keepdims=True)
        exponent = jnp.exp(scores - top)
        total = jnp.sum(exponent, axis=0, keepdims=True)
        prob = (exponent * (1.0 / total)).astype(LOW)
        prob_ref[image, head] = prob
        return prob

    def gather(prob, image, head):
        return dot(prob, half_of(tile(image, V_TILE[head]), lane, V_ODD[head]), 0, 0)

    work = [(image, head) for image in range(images) for head in range(HEADS_LANE)]
    scores, probs, outs = {}, {}, {}
    for turn_index in range(len(work) + 2):
        if turn_index < len(work):
            scores[turn_index] = score(*work[turn_index])
        if 0 <= turn_index - 1 < len(work):
            probs[turn_index - 1] = soften(scores.pop(turn_index - 1), *work[turn_index - 1])
        done = turn_index - 2
        if done >= 0:
            image, head = work[done]
            outs[head] = gather(probs.pop(done), image, head)
            if head == HEADS_LANE - 1:
                rows = slice(image * PADDED, (image + 1) * PADDED)
                ctx_ref[rows, :128] = (outs[0] + outs[1]).astype(LOW)
                ctx_ref[rows, 128:] = outs[2].astype(LOW)


def attend(mine, sizes, normed, bias, add, gathered, images):
    rows, width = normed.shape
    heads = bias.shape[0]
    pieces, table = gathered
    return pl.pallas_call(
        functools.partial(attend_body, table, images),
        grid=(LANES,),
        in_specs=[
            pl.BlockSpec(memory_space=pltpu.SMEM),
            pl.BlockSpec(memory_space=pltpu.SMEM),
            whole((2, PADDED, 128)),
            whole(normed.shape),
            pl.BlockSpec((HEADS_LANE, PADDED, PADDED), lambda g: (g, 0, 0)),
            pl.BlockSpec((1, 1, PACK), lambda g: (g, 0, 0)),
        ]
        + [anywhere()] * len(pieces),
        out_specs=[
            pl.BlockSpec((1, rows, PACK), lambda g: (g, 0, 0)),
            pl.BlockSpec((images, HEADS_LANE, PADDED, PADDED), lambda g: (0, g, 0, 0)),
            pl.BlockSpec((rows, OUT_PACK), lambda g: (0, g)),
        ],
        out_shape=[
            jax.ShapeDtypeStruct((LANES, rows, PACK), LOW),
            jax.ShapeDtypeStruct((images, heads, PADDED, PADDED), LOW),
            jax.ShapeDtypeStruct((rows, LANES * OUT_PACK), LOW),
        ],
        scratch_shapes=[
            pltpu.VMEM((LANES, width, PACK), LOW),
            pltpu.SemaphoreType.DMA((LANES,)),
        ],
        compiler_params=params(),
        cost_estimate=cost(1.5e10, 2e7),
    )(mine, sizes, jnp.asarray(grid_places()), normed, bias, add, *pieces)


def middle_body(table, columns, me_ref, ctx_ref, x_ref, vec_ref, *refs):
    pieces = refs[:-6]
    att_ref, mid_ref, n_ref, weight_s, pad_s, sems = refs[-6:]
    step = pl.program_id(0)

    @pl.when(step == 0)
    def _():
        for group in range(LANES):
            fetch(group, table, pieces, columns, weight_s.at[group], sems.at[group], me_ref[0])
        for group in range(LANES):
            fetched(weight_s.at[group], sems.at[group])
        pad_s[...] = jnp.zeros_like(pad_s)

    total = vec_ref[4:5, :]
    for group in range(LANES):
        total = total + dot(
            ctx_ref[:, group * OUT_PACK : (group + 1) * OUT_PACK], weight_s[group], 1, 1
        )
    att_ref[...] = total.astype(LOW)
    mid = load_images(pad_s, x_ref, step) + vec_ref[5:6, :] * total
    mid_ref[...] = mid
    scaled, _ = normalise(mid)
    n_ref[...] = (scaled * vec_ref[2:3, :] + vec_ref[3:4, :]).astype(LOW)


def middle(mine, ctx, x, vectors, gathered, columns, images):
    rows = images * PADDED
    width = x.shape[1]
    pieces, table = gathered
    block = lambda: pl.BlockSpec((TWO * PADDED, width), lambda i: (i, 0))
    return pl.pallas_call(
        functools.partial(middle_body, table, columns),
        grid=(images // TWO,),
        in_specs=[
            pl.BlockSpec(memory_space=pltpu.SMEM),
            pl.BlockSpec((TWO * PADDED, LANES * OUT_PACK), lambda i: (i, 0)),
            whole(x.shape),
            whole(vectors.shape),
        ]
        + [anywhere()] * len(pieces),
        out_specs=[block(), block(), block()],
        out_shape=[
            jax.ShapeDtypeStruct((rows, width), LOW),
            jax.ShapeDtypeStruct((rows, width), FULL),
            jax.ShapeDtypeStruct((rows, width), LOW),
        ],
        scratch_shapes=[
            pltpu.VMEM((LANES, width, OUT_PACK), LOW),
            pltpu.VMEM((TWO * PADDED, width), FULL),
            pltpu.SemaphoreType.DMA((LANES,)),
        ],
        compiler_params=params(),
        cost_estimate=cost(8e9, 1.5e7),
    )(mine, ctx, x, vectors, *pieces)


def gelu_pair(values):
    density = jnp.exp(values * values * -0.5) * INV_SQRT2PI
    below = 0.5 * lax.erf(values * INV_SQRT2) + 0.5
    return values * below, below + values * density


def feed_body(blocks, layout, me_ref, n_ref, gd_ref, ub_ref, *refs):
    count = sum(part[3] for part in layout)
    pieces = refs[:count]
    out_ref, gn_ref, keep_ref, send_ref, gub_ref, nt_s, gdt_s, up_s, down_s, act_s, gh_s, sems = refs[count:]
    step = pl.program_id(0)
    place = me_ref[0]
    rows = n_ref.shape[0]
    units = up_s.shape[3]
    per = rows // blocks

    def begin(group):
        slot = group % 2
        for index, (_, table, first, number, up_at, down_at) in enumerate(layout):
            held = pieces[first : first + number]
            for target, at, kind in ((up_s, up_at, 0), (down_s, down_at, 1)):
                fetch(
                    group,
                    table,
                    held,
                    (at, at + units),
                    target.at[slot, index],
                    sems.at[slot, kind, index],
                    place,
                )

    @pl.when(step == 0)
    def _():
        begin(0)
        nt_s[...] = n_ref[...].T
        gdt_s[...] = gd_ref[...].T
        out_ref[...] = jnp.zeros_like(out_ref)
        gn_ref[...] = jnp.zeros_like(gn_ref)

    for group in range(LANES):

        @pl.when(step == group)
        def _(group=group):
            if group + 1 < LANES:
                begin(group + 1)

    now = step % 2
    parts = len(layout)
    for index in range(parts):
        for kind, target in enumerate((up_s, down_s)):
            fetched(target.at[now, index], sems.at[now, kind, index])
    up_weight = [up_s[now, index] for index in range(parts)]
    down_weight = [down_s[now, index] for index in range(parts)]
    if parts > 1:
        up_weight = [jnp.concatenate(up_weight, axis=1)]
        down_weight = [jnp.concatenate(down_weight, axis=1)]
    up_weight, down_weight = up_weight[0], down_weight[0]
    true_lane = step ^ me_ref[1]
    unit_bias = ub_ref[true_lane]
    unit_sums = jnp.zeros((8, up_weight.shape[1]), FULL)
    for block in range(blocks):
        part = slice(block * per, (block + 1) * per)
        hidden = dot(n_ref[part, :], up_weight) + unit_bias
        active, slope = gelu_pair(hidden)
        active = active.astype(LOW)
        act_s[part, :] = active
        grad = (dot(gd_ref[part, :], down_weight) * slope).astype(LOW)
        gh_s[part, :] = grad
        unit_sums = unit_sums + fold(grad.astype(FULL))
        out_ref[part, :] += dot(active, down_weight, 1, 1)
        gn_ref[part, :] += dot(grad, up_weight, 1, 1)
    gub_ref[true_lane] = jnp.sum(unit_sums, axis=0, keepdims=True)
    grad_up = dot(nt_s[...], gh_s[...]).astype(LOW)
    grad_down = dot(gdt_s[...], act_s[...]).astype(LOW)
    chunk_rows = keep_ref.shape[2]
    wide = grad_up.shape[1]
    for odd, target in enumerate((keep_ref, send_ref)):

        @pl.when(step % 2 == odd)
        def _(target=target):
            for chunk in range(CHUNKS):
                slot = reversed_bits(chunk) ^ reversed_bits(place)
                at = slice(chunk * chunk_rows, (chunk + 1) * chunk_rows)
                target[0, slot, :, :wide] = grad_up[at]
                target[0, slot, :, wide:] = grad_down[at]


def feed(mine, normed, grad_down, unit_bias, groups, units, images):
    rows, width = normed.shape
    blocks = max(1, images // 4)
    parts = len(groups)
    sub = units // parts
    pieces, layout = [], []
    for (arrays, table), up_at, down_at in groups:
        layout.append((None, table, len(pieces), len(arrays), up_at, down_at))
        pieces.extend(arrays)
    chunk_rows = width // CHUNKS
    grad_block = (1, CHUNKS, chunk_rows, 2 * units)
    grads = jax.ShapeDtypeStruct((2,) + grad_block[1:], LOW)
    return pl.pallas_call(
        functools.partial(feed_body, blocks, layout),
        grid=(LANES,),
        in_specs=[
            pl.BlockSpec(memory_space=pltpu.SMEM),
            whole((rows, width)),
            whole((rows, width)),
            whole((LANES, 1, units)),
        ]
        + [anywhere()] * len(pieces),
        out_specs=[
            whole((rows, width)),
            whole((rows, width)),
            pl.BlockSpec(grad_block, lambda j: (j // 2, 0, 0, 0)),
            pl.BlockSpec(grad_block, lambda j: (jnp.maximum(j - 1, 0) // 2, 0, 0, 0)),
            whole((LANES, 1, units)),
        ],
        out_shape=[jax.ShapeDtypeStruct((rows, width), FULL)] * 2
        + [grads] * 2
        + [jax.ShapeDtypeStruct((LANES, 1, units), FULL)],
        scratch_shapes=[
            pltpu.VMEM((width, rows), LOW),
            pltpu.VMEM((width, rows), LOW),
            pltpu.VMEM((2, parts, width, sub), LOW),
            pltpu.VMEM((2, parts, width, sub), LOW),
            pltpu.VMEM((rows, units), LOW),
            pltpu.VMEM((rows, units), LOW),
            pltpu.SemaphoreType.DMA((2, 2, parts)),
        ],
        compiler_params=params(),
        cost_estimate=cost(3.5e10, 4e7),
    )(mine, normed, grad_down, unit_bias, *pieces)


def second_body(
    me_ref, down_ref, gn_ref, mid_ref, att_ref, ctx_ref, cot_ref, vec_ref, out_ref, gm_ref, ga_ref, keep_ref, send_ref, rows_ref, pad_s, out_s, sums_s, gat_s
):
    step = pl.program_id(0)

    @pl.when(step == 0)
    def _():
        pad_s[...] = jnp.zeros_like(pad_s)
        sums_s[...] = jnp.zeros_like(sums_s)

    cot = load_images(pad_s, cot_ref, step)
    down = down_ref[...] + vec_ref[6:7, :]
    mid = mid_ref[...]
    store_images(out_ref, out_s, mid + vec_ref[7:8, :] * down, step)
    scaled, inverse = normalise(mid)
    grad_normed = gn_ref[...]
    grad_mid = cot + norm_back(grad_normed, vec_ref[2:3, :], scaled, inverse)
    gm_ref[...] = grad_mid
    grad_att = (grad_mid * vec_ref[5:6, :]).astype(LOW)
    ga_ref[...] = grad_att
    gat_s[step] = grad_att.T
    sums_s[0] += fold(grad_normed * scaled)
    sums_s[1] += fold(grad_normed)
    sums_s[2] += fold(grad_mid)
    sums_s[3] += fold(grad_mid * att_ref[...].astype(FULL))
    sums_s[4] += fold(cot)
    sums_s[5] += fold(cot * down)

    @pl.when(step == pl.num_programs(0) - 1)
    def _():
        sums = [jnp.sum(sums_s[index], axis=0, keepdims=True) for index in range(6)]
        sums[2] = sums[2] * vec_ref[5:6, :]
        sums[4] = sums[4] * vec_ref[7:8, :]
        for index in range(6):
            rows_ref[index : index + 1, :] = sums[index]
        images = gat_s.shape[0]
        for group in range(LANES):
            at = slice(group * OUT_PACK, (group + 1) * OUT_PACK)
            grad = dot(gat_s[0], ctx_ref[0:PADDED, at])
            for image in range(1, images):
                grad = grad + dot(
                    gat_s[image], ctx_ref[image * PADDED : (image + 1) * PADDED, at]
                )
            give(me_ref[0], keep_ref, send_ref, group, grad.astype(LOW))


def give(place, keep_ref, send_ref, group, grad):
    rows = keep_ref.shape[2]
    mine = reversed_bits(place)
    target = (keep_ref, send_ref)[group % 2]
    for chunk in range(CHUNKS):
        target[group // 2, reversed_bits(chunk) ^ mine] = grad[chunk * rows : (chunk + 1) * rows]


def second_back(mine, down, grad_normed, mid, att, ctx, cot, vectors, images):
    rows, width = mid.shape
    block = lambda: pl.BlockSpec((PADDED, width), lambda i: (i, 0))
    grads = (2, CHUNKS, width // CHUNKS, OUT_PACK)
    return pl.pallas_call(
        second_body,
        grid=(images,),
        in_specs=[
            pl.BlockSpec(memory_space=pltpu.SMEM),
            block(),
            block(),
            block(),
            block(),
            whole(ctx.shape),
            whole(cot.shape),
            whole(vectors.shape),
        ],
        out_specs=[whole(cot.shape), block(), block(), whole(grads), whole(grads), whole((6, width))],
        out_shape=[
            jax.ShapeDtypeStruct(cot.shape, FULL),
            jax.ShapeDtypeStruct((rows, width), FULL),
            jax.ShapeDtypeStruct((rows, width), LOW),
            jax.ShapeDtypeStruct(grads, LOW),
            jax.ShapeDtypeStruct(grads, LOW),
            jax.ShapeDtypeStruct((6, width), FULL),
        ],
        scratch_shapes=[
            pltpu.VMEM((PADDED, width), FULL),
            pltpu.VMEM((PADDED, width), FULL),
            pltpu.VMEM((6, 8, width), FULL),
            pltpu.VMEM((images, width, PADDED), LOW),
        ],
        compiler_params=params(),
        cost_estimate=cost(1e10, 2e7),
    )(mine, down, grad_normed, mid, att, ctx, cot, vectors)


def back_body(table, columns, images, me_ref, ga_ref, qkv_ref, prob_ref, *refs):
    pieces = refs[:-6]
    dqkv_ref, pair_ref, cols_ref, weight_s, gc_s, sems = refs[-6:]
    step = pl.program_id(0)

    @pl.when(step == 0)
    def _():
        for group in range(LANES):
            fetch(group, table, pieces, columns, weight_s.at[group], sems.at[group], me_ref[0])

    fetched(weight_s.at[step], sems.at[step])
    gc_s[...] = dot(ga_ref[...], weight_s[step]).astype(LOW)
    lane = halves()

    def tile(image, index):
        return qkv_ref[0, image * PADDED : (image + 1) * PADDED, 128 * index : 128 * (index + 1)]

    def upstream(image, head):
        at = 128 if head == 2 else 0
        value = gc_s[image * PADDED : (image + 1) * PADDED, at : at + 128]
        return half_of(value, lane, V_ODD[head])

    def first(image, head):
        return dot(tile(image, V_TILE[head]), upstream(image, head), 1, 1)

    def second(grad_prob, image, head):
        soft = prob_ref[image, head].astype(FULL)
        weighted = soft * grad_prob
        inner = jnp.sum(weighted, axis=0, keepdims=True)
        grad_score = weighted - soft * inner
        if image == 0:
            pair_ref[head] = grad_score
        else:
            pair_ref[head] += grad_score
        return grad_score.astype(LOW)

    def third(low_score, image, head):
        odd = QK_ODD[head]
        return (
            dot(low_score, half_of(tile(image, K_TILE[head]), lane, odd), 0, 0) * HD**-0.5,
            dot(low_score, half_of(tile(image, Q_TILE[head]), lane, odd)),
            dot(prob_ref[image, head], upstream(image, head)),
        )

    work = [(image, head) for image in range(images) for head in range(HEADS_LANE)]
    probs, scores, grads = {}, {}, {}
    sums = [jnp.zeros((8, 128), FULL)] * 3
    for turn_index in range(len(work) + 2):
        if turn_index < len(work):
            probs[turn_index] = first(*work[turn_index])
        if 0 <= turn_index - 1 < len(work):
            scores[turn_index - 1] = second(probs.pop(turn_index - 1), *work[turn_index - 1])
        done = turn_index - 2
        if done < 0:
            continue
        image, head = work[done]
        grads[head] = third(scores.pop(done), image, head)
        if head < HEADS_LANE - 1:
            continue
        packed = (
            grads[0][0] + grads[1][0],
            grads[2][0] + grads[2][2],
            grads[0][2] + grads[1][2],
            grads[0][1] + grads[1][1],
            grads[2][1],
        )
        rows = slice(image * PADDED, (image + 1) * PADDED)
        for index, value in enumerate(packed):
            low_value = value.astype(LOW)
            dqkv_ref[0, rows, 128 * index : 128 * (index + 1)] = low_value
            if index < 3:
                sums[index] = sums[index] + fold(low_value.astype(FULL))
    for index in range(3):
        cols_ref[0, :, 128 * index : 128 * (index + 1)] = sums[index]


def back(mine, grad_att, qkv, prob, gathered, columns, images):
    rows, width = grad_att.shape
    heads = prob.shape[1]
    pieces, table = gathered
    return pl.pallas_call(
        functools.partial(back_body, table, columns, images),
        grid=(LANES,),
        in_specs=[
            pl.BlockSpec(memory_space=pltpu.SMEM),
            whole(grad_att.shape),
            pl.BlockSpec((1, rows, PACK), lambda g: (g, 0, 0)),
            pl.BlockSpec((images, HEADS_LANE, PADDED, PADDED), lambda g: (0, g, 0, 0)),
        ]
        + [anywhere()] * len(pieces),
        out_specs=[
            pl.BlockSpec((1, rows, PACK), lambda g: (g, 0, 0)),
            pl.BlockSpec((HEADS_LANE, PADDED, PADDED), lambda g: (g, 0, 0)),
            pl.BlockSpec((1, 8, 384), lambda g: (g, 0, 0)),
        ],
        out_shape=[
            jax.ShapeDtypeStruct((LANES, rows, PACK), LOW),
            jax.ShapeDtypeStruct((heads, PADDED, PADDED), FULL),
            jax.ShapeDtypeStruct((LANES, 8, 384), FULL),
        ],
        scratch_shapes=[
            pltpu.VMEM((LANES, width, OUT_PACK), LOW),
            pltpu.VMEM((rows, OUT_PACK), LOW),
            pltpu.SemaphoreType.DMA((LANES,)),
        ],
        compiler_params=params(),
        cost_estimate=cost(3e10, 4e7),
    )(mine, grad_att, qkv, prob, *pieces)


def heads_body(pair_ref, cols_ref, thin_ref, heads_ref, spread_s, flat_s):
    heads = pair_ref.shape[0]
    spread_s[...] = jnp.zeros_like(spread_s)

    def head_sum(index, carry):
        for row in range(GRID):
            at = GRID * (GRID - 1 - row)
            spread_s[index, :, at : at + PATCHES] += pair_ref[
                index, row * GRID : (row + 1) * GRID, 0:PATCHES
            ]
        return carry

    lax.fori_loop(0, heads, head_sum, 0)
    for col in range(GRID):
        flat_s[16 * col : 16 * (col + 1), :] = spread_s[:, col, :]
    wide = exact_dot(flat_s[...], thin_ref[...], 1)
    table = jnp.zeros((16, TABLE), FULL)
    for col in range(GRID):
        table = table + turn(wide[16 * col : 16 * (col + 1)], GRID - 1 - col)
    for group in range(LANES):
        cols = jnp.sum(cols_ref[group], axis=0, keepdims=True)
        for head in range(HEADS_LANE):
            at = HD * (4 + head if head < 2 else 3)
            heads_ref[group, head : head + 1, 0:HD] = cols[:, HD * head : HD * (head + 1)]
            heads_ref[group, head : head + 1, HD : 2 * HD] = cols[:, at : at + HD]
        first = group * HEADS_LANE
        heads_ref[group, :, 2 * HD :] = table[first : first + HEADS_LANE, 0 : SPAN * SPAN]


def heads_back(pair, cols, thin):
    heads = pair.shape[0]
    return pl.pallas_call(
        heads_body,
        out_shape=jax.ShapeDtypeStruct((LANES, HEADS_LANE, 2 * HD + SPAN * SPAN), FULL),
        scratch_shapes=[
            pltpu.VMEM((16, GRID, SPREAD), FULL),
            pltpu.VMEM((16 * GRID, SPREAD), FULL),
        ],
        compiler_params=params(),
        cost_estimate=cost(3e9, 4e6),
    )(pair, cols, thin)


def project_body(me_ref, n_ref, dqkv_ref, keep_ref, send_ref, t_s):
    t_s[...] = n_ref[...].T
    for group in range(LANES):
        give(me_ref[0], keep_ref, send_ref, group, dot(t_s[...], dqkv_ref[group]).astype(LOW))


def project(mine, normed, dqkv):
    rows, width = normed.shape
    grads = jax.ShapeDtypeStruct((2, CHUNKS, width // CHUNKS, PACK), LOW)
    return pl.pallas_call(
        project_body,
        in_specs=[pl.BlockSpec(memory_space=pltpu.SMEM)] + [pl.BlockSpec(memory_space=pltpu.VMEM)] * 2,
        out_shape=[grads, grads],
        scratch_shapes=[pltpu.VMEM((width, rows), LOW)],
        compiler_params=params(),
        cost_estimate=cost(8e9, 1e7),
    )(mine, normed, dqkv)


def input_body(table, me_ref, dqkv_ref, gm_ref, x_ref, vec_ref, *refs):
    pieces = refs[:-7]
    out_ref, rows_ref, weight_s, pad_s, out_s, sums_s, sems = refs[-7:]
    step = pl.program_id(0)

    @pl.when(step == 0)
    def _():
        for group in range(LANES):
            fetch(group, table, pieces, (0, PACK), weight_s.at[group], sems.at[group], me_ref[0])
        pad_s[...] = jnp.zeros_like(pad_s)
        sums_s[...] = jnp.zeros_like(sums_s)
        for group in range(LANES):
            fetched(weight_s.at[group], sems.at[group])

    scaled, inverse = normalise(load_images(pad_s, x_ref, step))
    grad = dot(dqkv_ref[0], weight_s[0], 1, 1)
    for group in range(1, LANES):
        grad = grad + dot(dqkv_ref[group], weight_s[group], 1, 1)
    sums_s[0] += fold(grad * scaled)
    sums_s[1] += fold(grad)
    for index in range(2):
        rows_ref[index : index + 1, :] = jnp.sum(sums_s[index], axis=0, keepdims=True)
    result = gm_ref[...] + norm_back(grad, vec_ref[0:1, :], scaled, inverse)
    store_images(out_ref, out_s, result, step)


def input_back(mine, dqkv, grad_mid, x, vectors, gathered, images):
    width = x.shape[1]
    pieces, table = gathered
    return pl.pallas_call(
        functools.partial(input_body, table),
        grid=(images // TWO,),
        in_specs=[
            pl.BlockSpec(memory_space=pltpu.SMEM),
            pl.BlockSpec((LANES, TWO * PADDED, PACK), lambda i: (0, i, 0)),
            pl.BlockSpec((TWO * PADDED, width), lambda i: (i, 0)),
            whole(x.shape),
            whole(vectors.shape),
        ]
        + [anywhere()] * len(pieces),
        out_specs=[whole(x.shape), whole((2, width))],
        out_shape=[jax.ShapeDtypeStruct(x.shape, FULL), jax.ShapeDtypeStruct((2, width), FULL)],
        scratch_shapes=[
            pltpu.VMEM((LANES, width, PACK), LOW),
            pltpu.VMEM((TWO * PADDED, width), FULL),
            pltpu.VMEM((TWO * PADDED, width), FULL),
            pltpu.VMEM((2, 8, width), FULL),
            pltpu.SemaphoreType.DMA((LANES,)),
        ],
        compiler_params=params(),
        cost_estimate=cost(1.5e10, 1.5e7),
    )(mine, dqkv, grad_mid, x, vectors, *pieces)


def swap(values, axis, bit):
    count = lax.axis_size(axis)
    return lax.ppermute(values, axis, [(index, index ^ bit) for index in range(count)])


def after(values, *others):
    return lax.optimization_barrier((values,) + others)[0]


def sync(*values):
    return lax.optimization_barrier(values)


def join(former, latter, axis=0):
    return jnp.concatenate([former, latter], axis=axis)


def split_rows(held):
    half = held.shape[1] // 2
    return held[:, :half], held[:, half:]


def pieces_of(upper, upper_x, lower, lower_y, near_core, far_core):
    arrays = [upper, upper_x, lower, lower_y, near_core[0], far_core[0], near_core[1], far_core[1]]
    half = upper.shape[1]

    def part(first, far):
        top = [(first + far, slot) for slot in range(8)]
        low = [(first + 2 + slot // 4, 4 * far + slot % 4) for slot in range(8)]
        return ((0, top), (half, low))

    return arrays, (part(0, 0), part(4, 0), part(0, 1), part(4, 1))


def total_of(terms):
    total = terms[0].astype(FULL)
    for one in terms[1:]:
        total = total + one.astype(FULL)
    return total


def sum_call(body, grid, views, outs, moved):
    return pl.pallas_call(
        body,
        grid=(grid,),
        in_specs=[pl.BlockSpec(block, index) for _, block, index in views],
        out_specs=[pl.BlockSpec(block, index) for _, _, block, index in outs],
        out_shape=[jax.ShapeDtypeStruct(shape, dtype) for shape, dtype, _, _ in outs],
        compiler_params=params(),
        cost_estimate=cost(1e6, moved),
    )(*[array for array, _, _ in views])


def sum_away(keeps, gots):
    half = keeps[0].shape[2] // 2
    wide = sum(keep.shape[3] for keep in keeps)
    views = []
    for keep, got in zip(keeps, gots):
        block = (1, 4, half, keep.shape[3])
        for array in (keep, got):
            views.append((array, block, lambda j: (1, j, 0, 0)))
            views.append((array, block, lambda j: (j, 1, 1, 0)))

    def body(*refs):
        ins, (upper, lower) = refs[:-2], refs[-2:]
        first = 0
        for index in range(0, len(ins), 4):
            keep_u, keep_l, got_u, got_l = ins[index : index + 4]
            at = slice(first, first + keep_u.shape[3])
            first = at.stop
            upper[:, :, at] = total_of((keep_u[0], got_u[0])).astype(LOW)
            lower[0, :, :, at] = total_of((keep_l[0], got_l[0])).astype(LOW)

    outs = [
        ((8, half, wide), LOW, (4, half, wide), lambda j: (j, 0, 0)),
        ((2, 4, half, wide), LOW, (1, 4, half, wide), lambda j: (j, 0, 0, 0)),
    ]
    return sum_call(body, 2, views, outs, 8e6)


def sum_here(keeps, gots, upper_got, lower_got):
    half = keeps[0].shape[2] // 2
    wide = sum(keep.shape[3] for keep in keeps)
    places = (
        lambda j: (0, j, 0, 0),
        lambda j: (0, 2 + j, 0, 0),
        lambda j: (0, j, 1, 0),
        lambda j: (1, j, 1, 0),
    )
    views = [
        (upper_got, (2, half, wide), lambda j: (j, 0, 0)),
        (upper_got, (2, half, wide), lambda j: (2 + j, 0, 0)),
        (lower_got, (1, 2, half, wide), lambda j: (0, j, 0, 0)),
        (lower_got, (1, 2, half, wide), lambda j: (1, j, 0, 0)),
    ]
    for keep, got in zip(keeps, gots):
        for array in (keep, got):
            views.extend((array, (1, 2, half, keep.shape[3]), place) for place in places)

    def body(*refs):
        far, ins, outs = refs[:4], refs[4:-4], refs[-4:]
        first = 0
        for index in range(0, len(ins), 8):
            at = slice(first, first + ins[index].shape[3])
            first = at.stop
            for view in range(4):
                came = far[view][:, :, at] if view < 2 else far[view][0, :, :, at]
                terms = (ins[index + view][0], ins[index + 4 + view][0], came)
                outs[view][:, :, at] = total_of(terms).astype(outs[view].dtype)

    outs = [
        ((4, half, wide), dtype, (2, half, wide), lambda j: (j, 0, 0))
        for dtype in (FULL, LOW, FULL, LOW)
    ]
    return sum_call(body, 2, views, outs, 1.2e7)


def sum_line(upper, upper_got, lower, lower_got):
    half, wide = upper.shape[1:]
    views = []
    for array in (upper, upper_got, lower, lower_got):
        views.append((array, (1, half, wide), lambda j: (j, 0, 0)))
        views.append((array, (1, half, wide), lambda j: (2 + j, 0, 0)))

    def body(*refs):
        for side in range(2):
            out = refs[8 + side]
            out[0, :half] = total_of((refs[side][0], refs[2 + side][0])).astype(out.dtype)
            out[0, half:] = total_of((refs[4 + side][0], refs[6 + side][0])).astype(out.dtype)

    outs = [
        ((2, 2 * half, wide), dtype, (1, 2 * half, wide), lambda j: (j, 0, 0))
        for dtype in (FULL, LOW)
    ]
    return sum_call(body, 2, views, outs, 6e6)


def adam(weight, moment_one, moment_two, incoming, step_rate, decay_rate):
    first_new = BETA_ONE * moment_one + (1.0 - BETA_ONE) * incoming
    second_new = BETA_TWO * moment_two + (1.0 - BETA_TWO) * incoming * incoming
    update = (
        first_new
        / (1.0 - BETA_ONE**STEP)
        / (jnp.sqrt(second_new / (1.0 - BETA_TWO**STEP)) + ADAM_EPSILON)
    )
    return (second_new, weight * (1.0 - step_rate * decay_rate) - step_rate * update)


def pack_attention(weights):
    query, key, value, out = (weights[index] for index in range(4))
    rows = query.shape[0]
    blank = jnp.zeros((rows, HD), weights.dtype)
    first = jnp.concatenate([query, value[:, 128:], value[:, :128], key, blank], axis=1)
    last = jnp.concatenate([out[:, :128], blank, out[:, 128:]], axis=1)
    return first, last


def unpack_attention(first, last):
    query = first[:, :192]
    value = jnp.concatenate([first[:, 256:384], first[:, 192:256]], axis=1)
    key = first[:, 384:576]
    out = jnp.concatenate([last[:, :128], last[:, 192:]], axis=1)
    return jnp.stack([query, key, value, out])


def shards(
    block_input,
    cotangent,
    image_size,
    attention_weights,
    attention_first,
    attention_second,
    mlp_weights,
    mlp_first,
    mlp_second,
    head_params,
    head_first,
    head_second,
    norm_params,
    norm_first,
    norm_second,
):
    near = lax.axis_size("dp") == CHUNKS
    lane_index = lax.axis_index("mp")
    local_rows, width = block_input.shape
    images = local_rows // PATCHES
    local_heads = head_params.shape[0]
    chunk_rows = width // CHUNKS
    thin = jnp.asarray(thin_matrix(), LOW)

    first, last = pack_attention(attention_weights.astype(LOW))
    mlp_low = mlp_weights.astype(LOW)
    units = mlp_low.shape[2]
    unit_bias = norm_params[8:].reshape(LANES, 1, units)
    first = jnp.concatenate([first, last], axis=1)
    second = jnp.concatenate([mlp_low[0], mlp_low[1]], axis=1)
    out_at = (PACK, PACK + OUT_PACK)
    if near:
        mine = jnp.stack([lax.axis_index("dp"), lane_index, lane_index]).astype(jnp.int32)
        core = lambda values: swap(values, "mp", 1)
        x_axis = lambda values: swap(values, "mp", 2)
        y_axis = lambda values: swap(values, "dp", 1)
        z_near = lambda values: swap(values, "dp", 2)
        z_far = lambda values: swap(values, "dp", 4)
        one, two = first[None], second[None]
        got = z_far(one)
        normed_one, grad_down = first_norm(block_input, cotangent, norm_params, images)
        got, normed_one, other = sync(got, normed_one, x_axis(after(head_params, first)))
        one = join(one, got)
        got = z_near(one)
        two_got = z_far(after(two, one))
        got, near_table, far_table = sync(got, core(head_params), core(other))
        upper, lower = split_rows(join(one, got))
        upper, lower = sync(upper, lower)
        upper_got, lower_got = y_axis(upper), x_axis(lower)
        upper_got, lower_got = sync(upper_got, lower_got)
        upper, lower = sync(join(upper, upper_got), join(lower, lower_got))
        upper_far, lower_far = x_axis(upper), y_axis(lower)
        two = join(two, after(two_got, upper, lower))
        two_got = z_near(two)
        bias, add = spread_bias(
            (head_params, after(near_table, two), other, after(far_table, two)), thin
        )
        near_core = sync(core(upper), core(lower))
        upper_far, lower_far, two_got, bias = sync(
            upper_far, lower_far, after(two_got, *near_core), bias
        )
        far_core = sync(core(upper_far), core(lower_far))
        first_all = pieces_of(upper, upper_far, lower, lower_far, near_core, far_core)
        two_upper, two_lower = split_rows(join(two, two_got))
        two_upper, two_lower, normed_one = sync(two_upper, two_lower, normed_one)
        two_upper_got, two_lower_got = y_axis(two_upper), x_axis(two_lower)
    else:
        mine = jnp.stack([0 * lane_index, 0 * lane_index, lane_index]).astype(jnp.int32)

        def gather_far(piece):
            full = lax.all_gather(piece, "dp", axis=0, tiled=True)
            full = lax.all_gather(full, "mp", axis=0, tiled=False)
            full = full.reshape(LANES, CHUNKS, chunk_rows, piece.shape[1])
            order = [reversed_bits(index) for index in range(CHUNKS)]
            full = jnp.stack([full[:, index] for index in order], axis=1)
            slots = range(CHUNKS)
            table = tuple(((0, [(group, slot) for slot in slots]),) for group in range(LANES))
            return [full[index] for index in range(LANES)], table

        tables = lax.all_gather(head_params, "mp", axis=0, tiled=False)
        tables = tuple(tables[index] for index in range(LANES))
        normed_one, grad_down = first_norm(block_input, cotangent, norm_params, images)
        bias, add = spread_bias(tables, thin)
        first_all = gather_far(first)
        second_all = gather_far(second)

    qkv, prob, ctx = attend(mine, image_size, normed_one, bias, add, first_all, images)
    if near:
        ctx, two_upper_got, two_lower_got = sync(ctx, two_upper_got, two_lower_got)
        two_upper, two_lower, ctx = sync(
            join(two_upper, two_upper_got), join(two_lower, two_lower_got), ctx
        )
        near_two = (core(two_upper), core(two_lower))
        far_two = (x_axis(two_upper), y_axis(two_lower))
    att, mid, normed_two = middle(
        mine, ctx, block_input, norm_params, first_all, out_at, images
    )
    if near:
        normed_two, *far_two = sync(normed_two, *far_two, *near_two)
        far_two, near_two = far_two[:2], far_two[2:]
        second_all = pieces_of(
            two_upper,
            far_two[0],
            two_lower,
            far_two[1],
            near_two,
            sync(core(far_two[0]), core(far_two[1])),
        )
    groups = ((second_all, 0, units),)
    down, grad_normed, keep_mlp, send_mlp, unit_sums = feed(
        mine, normed_two, grad_down, unit_bias, groups, units, images
    )
    if near:
        mlp_core = core(send_mlp)
    output, grad_mid, grad_att, keep_out, send_out, second_rows = second_back(
        mine, down, grad_normed, mid, att, ctx, cotangent, norm_params, images
    )
    if near:
        mlp_core, grad_att, send_out = sync(mlp_core, grad_att, send_out)
        keeps, gots = (keep_mlp, keep_out), (mlp_core, core(send_out))
        upper, lower, grad_att = sync(*sum_away(keeps, gots), grad_att)
        upper_got, lower_got = x_axis(upper), y_axis(lower)
    dqkv, pair, cols = back(
        mine, grad_att, qkv, prob, first_all, out_at, images
    )
    keep_att, send_att = project(mine, normed_one, dqkv)
    grad_heads = heads_back(after(pair, keep_att), cols, thin)
    if near:
        keep_att, send_att, upper_got, lower_got, grad_heads = sync(
            keep_att, send_att, upper_got, lower_got, grad_heads
        )
        att_core = core(send_att)
        upper, upper_away, lower, lower_away = sum_here(keeps, gots, upper_got, lower_got)
        upper_away, lower_away, att_core = sync(upper_away, lower_away, att_core)
        upper_got, lower_got = y_axis(upper_away), x_axis(lower_away)
        keeps, gots = (keep_att,), (att_core,)
        att_upper, att_lower, dqkv = sync(*sum_away(keeps, gots), dqkv)
        att_upper_got, att_lower_got = x_axis(att_upper), y_axis(att_lower)
    grad_input, first_rows = input_back(
        mine, dqkv, grad_mid, block_input, norm_params, first_all, images
    )
    norms = jnp.concatenate([first_rows, second_rows, unit_sums.reshape(-1, width)], axis=0)
    if near:
        count = norms.shape[0]
        rest = count + local_heads
        norms, *heads = sync(norms, *[grad_heads[index] for index in range(LANES)])
        norms = jnp.pad(norms, ((0, 0), (0, grad_heads.shape[2] - width)))
        keep = jnp.concatenate([norms, heads[0], heads[2]], axis=0)
        small_got = core(jnp.concatenate([norms, heads[1], heads[3]], axis=0))
        upper_got, lower_got, small_got = sync(upper_got, lower_got, small_got)
        line, line_away = sum_line(upper, upper_got, lower, lower_got)
        line_got = z_near(line_away)
        small = keep + small_got
        small_got = x_axis(join(small[:count], small[rest:]))
        upper_got, lower_got, line_away, small_got = sync(
            att_upper_got, att_lower_got, line_away, small_got
        )
        small = small[:rest] + small_got
        upper, upper_away, lower, lower_away = sum_here(keeps, gots, upper_got, lower_got)
        upper_away, lower_away, small = sync(upper_away, lower_away, small)
        upper_got, lower_got = y_axis(upper_away), x_axis(lower_away)
        small_got = y_axis(small)
        here, away = sum_line(upper, upper_got, lower, lower_got)
        small_got, line_got, away = sync(small_got, line_got, away)
        line = line + line_got.astype(FULL)
        small, line_away = sync(small + small_got, line[1].astype(LOW))
        got, line_got = z_near(away), z_far(line_away)
        got, line_got, small = sync(got, line_got, small)
        came = (z_near(small), z_far(small), swap(small, "dp", 6))
        here = here + got.astype(FULL)
        got = z_far(here[1].astype(LOW))
        sum_mlp = line[0] + line_got.astype(FULL)
        sum_att = here[0] + got.astype(FULL)
        sum_mlp, sum_out = sum_mlp[:, : 2 * units], sum_mlp[:, 2 * units :]
    else:
        reduced_norms = lax.psum(norms, ("dp", "mp"))
        reduced_heads = lax.psum_scatter(
            lax.psum(grad_heads, "dp"), "mp", scatter_dimension=0, tiled=False
        )

        def scatter_far(keep, send):
            terms = jnp.stack([keep[0], send[0], keep[1], send[1]])
            order = [reversed_bits(index) for index in range(CHUNKS)]
            terms = jnp.stack([terms[:, index] for index in order], axis=1)
            terms = terms.reshape(LANES, width, terms.shape[-1])
            mine_only = lax.psum_scatter(terms, "mp", scatter_dimension=0, tiled=False)
            return lax.psum_scatter(
                mine_only.astype(FULL), "dp", scatter_dimension=0, tiled=True
            )

        sum_mlp = scatter_far(keep_mlp, send_mlp)
        sum_out = scatter_far(keep_out, send_out)
        sum_att = scatter_far(keep_att, send_att)

    reduced_attention = unpack_attention(sum_att, sum_out)
    reduced_mlp = jnp.stack([sum_mlp[:, :units], sum_mlp[:, units:]])
    attention_second_new, attention_new = adam(
        attention_weights,
        attention_first,
        attention_second,
        reduced_attention,
        RATE_MATRIX,
        DECAY_MATRIX,
    )
    if near:
        came = [after(one, attention_new) for one in came]
        small = (small + came[0]) + (came[1] + came[2])
        reduced_norms = small[:count, :width]
        reduced_heads = small[count:]
    mlp_second_new, mlp_new = adam(
        mlp_weights, mlp_first, mlp_second, reduced_mlp, RATE_MATRIX, DECAY_MATRIX
    )
    head_second_new, head_new = adam(
        head_params, head_first, head_second, reduced_heads, RATE_VECTOR, 0.0
    )
    norm_second_new, norm_new = adam(
        norm_params, norm_first, norm_second, reduced_norms, RATE_VECTOR, 0.0
    )
    return (
        output,
        grad_input,
        reduced_attention,
        attention_second_new,
        attention_new,
        reduced_mlp,
        mlp_second_new,
        mlp_new,
        reduced_heads,
        head_second_new,
        head_new,
        reduced_norms,
        norm_second_new,
        norm_new,
    )


def solution(mesh):
    rows = P(("dp", "mp"), None)
    matrix = P(None, "dp", "mp")
    head = P("mp", None)
    placed = (rows, rows, P("dp", None)) + (matrix,) * 6 + (head,) * 3 + (P(),) * 3
    given = (rows, rows) + (matrix,) * 6 + (head,) * 3 + (P(),) * 3
    return jax.shard_map(shards, mesh=mesh, in_specs=placed, out_specs=given, check_vma=False)
```
